32 devices in a mesh: region: 8 (over z, core), group: 4 (over y, x).
Axes of the slice: x: 2, y: 2, z: 4, core: 2. Of those that a mesh axis runs over, the one named last changes fastest.
Arguments:
- features: bfloat16 [12288, 2048], P(('region', 'group')), may hold values from -1.5 to 1.5
- memory: bfloat16 [4096, 2048], P(('region', 'group')), may hold values from -1 to 1
- requests: int32 [32, 2], P(('region', 'group')), may hold values from 0 to 3, as said below
- owners: int32 [8, 4], P('region'), may hold values from 0 to 3, as said below
- labels: int32 [32, 384], P(('region', 'group')), may hold values from 0 to 1023, as said below
Outputs:
- feat_grad: bfloat16 [12288, 2048], P(('region', 'group'))
- new_memory: bfloat16 [4096, 2048], P(('region', 'group'))
The draws below stay inside these ranges and needn't reach their ends.
Inputs may be any that keep to these rules, and one draw needn't show every extreme that they name: `owners`: each row of a region is a permutation. `requests`: the 2 numbers of a device are distinct blocks of its region. At most 96 crops of one device carry labels of one region, and every device reaches that bound for some region.
All inputs are finite; a program needn't handle non-finite values.
Results may differ from the reference program's by a relative error of at most 0.006.
Values may be sent and summed in bfloat16 or wider, within the bound.
No kernel may reach another device: no remote copies, remote signals or barrier semaphores. Data moves between devices by JAX's collectives and lax.ppermute only.
A program may use at most 64 MiB of HBM per device.

```python
import jax
import jax.numpy as jnp
from jax import lax

D = 2048
BLOCK = 128
BATCH = 384
REGIONS = 8
GROUPW = 4
NB = 2
CAPR = 96
TOTAL = 12288
MEMROWS = 4096
DEVICES = 32


def memory_rows(key, row_list):
    base_key = jax.random.fold_in(key, 101)
    signs = jax.vmap(lambda row: jax.random.rademacher(jax.random.fold_in(base_key, row), (D,), dtype=jnp.float32))(row_list)
    return signs * D ** (-0.5)


def owner_table(key):
    base_key = jax.random.fold_in(key, 202)
    return jax.vmap(lambda region: jax.random.permutation(jax.random.fold_in(base_key, region), GROUPW))(jnp.arange(REGIONS)).astype(jnp.int32)


def request_table(key):
    heat_key = jax.random.fold_in(key, 303)
    pick_key = jax.random.fold_in(key, 304)

    def one_device(device):
        region = device // GROUPW
        heated = (jax.random.randint(jax.random.fold_in(heat_key, region), (GROUPW,), 0, 4) == 0).astype(jnp.int32)
        score = jax.random.randint(jax.random.fold_in(pick_key, device), (GROUPW,), 0, 64) + 64 * heated
        score = score * GROUPW + jnp.arange(GROUPW, dtype=jnp.int32)
        _, chosen = lax.top_k(score, NB)
        return chosen.astype(jnp.int32)
    return jax.vmap(one_device)(jnp.arange(DEVICES))


def draw_memory(key, part):
    return memory_rows(key, jnp.arange(MEMROWS)).astype(jnp.bfloat16)


def draw_owners(key, part):
    return owner_table(key)


def draw_requests(key, part):
    return request_table(key)


def draw_labels(key, part):
    perm_key = jax.random.fold_in(key, 505)
    heat_key = jax.random.fold_in(key, 506)
    shuffle_key = jax.random.fold_in(key, 507)
    row_key = jax.random.fold_in(key, 508)

    def one_device(device):
        order_rank = jax.random.permutation(jax.random.fold_in(perm_key, device), REGIONS * CAPR).astype(jnp.int32)
        heated = jax.random.randint(jax.random.fold_in(heat_key, device), (), 0, REGIONS)
        slot_region = jnp.arange(REGIONS * CAPR, dtype=jnp.int32) // CAPR
        priority = jnp.where(slot_region == heated, -1, order_rank)
        chosen = jnp.argsort(priority, stable=True)[:BATCH].astype(jnp.int32)
        mixing = jax.random.permutation(jax.random.fold_in(shuffle_key, device), BATCH)
        regions_of = chosen[mixing] // CAPR
        rows_of = jax.random.randint(jax.random.fold_in(row_key, device), (BATCH,), 0, BLOCK)
        return (regions_of * BLOCK + rows_of).astype(jnp.int32)
    return jax.vmap(one_device)(jnp.arange(DEVICES))


def draw_features(key, part):
    normal_part = jax.random.normal(jax.random.fold_in(key, 404), (TOTAL, D), jnp.float32)
    normal_part = jnp.clip(normal_part, -6.0, 6.0) * D ** (-0.5)
    return normal_part.astype(jnp.bfloat16)


def setup_inputs(seed: int = 0) -> dict:
    splits = jax.random.split(jax.random.key(seed), 6)
    return {
        "features": draw_features(jax.random.fold_in(splits[5], 71), 0),
        "memory": draw_memory(jax.random.fold_in(splits[5], 71), 0),
        "requests": draw_requests(jax.random.fold_in(splits[5], 71), 0),
        "owners": draw_owners(jax.random.fold_in(splits[5], 71), 0),
        "labels": draw_labels(jax.random.fold_in(splits[5], 71), 0),
    }


exponent_sharpness = 0.05
smoothing = 0.1
momentum_keep = 0.2

def device_grad(index, features, memory, requests, owners):
    region_index = index // GROUPW
    embedding_entries = lax.dynamic_slice_in_dim(features, (index * BATCH).astype(jnp.int32), BATCH, 0)
    wanted_owner = jnp.take(owners[region_index], requests[index], axis=0).astype(jnp.int32)
    row_ids = ((region_index * GROUPW + wanted_owner)[:, None] * BLOCK + jnp.arange(BLOCK, dtype=jnp.int32)[None, :]).reshape(-1)
    reciprocal_memory_slices = jnp.take(memory, row_ids.astype(jnp.int32), axis=0)
    cosine_affinities = jnp.dot(embedding_entries, reciprocal_memory_slices.T, preferred_element_type=jnp.float32) / exponent_sharpness
    shifted = cosine_affinities - lax.optimization_barrier(jnp.max(cosine_affinities, axis=1, keepdims=True))
    expo = jnp.exp(shifted)
    normalized_likelihoods = expo / lax.optimization_barrier(jnp.sum(expo, axis=1, keepdims=True))
    column = jnp.arange(NB * BLOCK, dtype=jnp.int32)
    smoothed_identity_weights = (jnp.where(column < BLOCK, (1.0 - smoothing) / BLOCK, 0.0) + smoothing / (NB * BLOCK)).astype(jnp.float32)
    pre_normalized_derivative = ((normalized_likelihoods - smoothed_identity_weights[None, :]) / exponent_sharpness).astype(jnp.bfloat16)
    return jnp.dot(pre_normalized_derivative, reciprocal_memory_slices, preferred_element_type=jnp.float32).astype(jnp.bfloat16)

def reference(features, memory, requests, owners, labels):
    grads = lax.map(lambda index: device_grad(index, features, memory, requests, owners), jnp.arange(DEVICES, dtype=jnp.int32))
    feat_grad = grads.reshape(TOTAL, D)
    device_of = jnp.arange(TOTAL, dtype=jnp.int32) // BATCH
    group_of = device_of % GROUPW
    flat_labels = labels.reshape(-1).astype(jnp.int32)
    target_row = (flat_labels // BLOCK * GROUPW + group_of) * BLOCK + flat_labels % BLOCK
    sums = jax.ops.segment_sum(features.astype(jnp.float32), target_row, num_segments=MEMROWS)
    counts = jax.ops.segment_sum(jnp.ones((TOTAL,), jnp.float32), target_row, num_segments=MEMROWS)
    old_rows = memory.astype(jnp.float32)
    averaged = sums / jnp.maximum(counts, 1.0)[:, None]
    mixed = jnp.where(counts[:, None] > 0, momentum_keep * old_rows + (1.0 - momentum_keep) * averaged, old_rows)
    scale = lax.rsqrt(lax.optimization_barrier(jnp.mean(mixed * mixed, axis=1, keepdims=True)) + 1e-06) * D ** (-0.5)
    new_memory = (mixed * scale).astype(jnp.bfloat16)
    return (feat_grad, new_memory)
```

```python
import jax
import jax.numpy as jnp
from jax import lax
from jax.sharding import PartitionSpec as P

D = 2048
CORES = 2

exponent_sharpness = 0.05
smoothing = 0.1
momentum_keep = 0.2


def on_device(features, memory, requests, owners, labels):
    group_count = lax.axis_size("group")
    region_count = lax.axis_size("region")
    layers = region_count // CORES
    block_rows, feat_width = memory.shape
    region = lax.axis_index("region")
    group = lax.axis_index("group")
    layer, core = region // CORES, region % CORES
    label_row = labels[0]

    def local_sums(which_core):
        row = jnp.arange(layers * block_rows, dtype=jnp.int32)
        value = (row // block_rows * CORES + which_core) * block_rows + row % block_rows
        match = (value[:, None] == label_row[None, :]).astype(jnp.bfloat16)
        return jnp.dot(match, features, preferred_element_type=jnp.float32)

    away = local_sums(1 - core).astype(jnp.bfloat16)
    sibling = lax.ppermute(away, "region", [(r, r ^ 1) for r in range(region_count)])

    blocks = [memory] + [
        lax.ppermute(memory, "group", [(g, g ^ k) for g in range(group_count)])
        for k in range(1, group_count)
    ]

    all_labels = labels
    step = 1
    while step < region_count:
        all_labels = jnp.concatenate(
            [
                all_labels,
                lax.ppermute(all_labels, "region", [(r, r ^ step) for r in range(region_count)]),
            ]
        )
        step *= 2

    chip_sums = (local_sums(core) + sibling.astype(jnp.float32)).astype(jnp.bfloat16)
    chip_sums = chip_sums.reshape(layers, block_rows, feat_width)

    halves = 2
    half_rows = block_rows // halves
    right = [None] * halves
    left = [None] * halves
    for hop in range(layers - 1):
        up = [
            (z * CORES + c, (z + 1) * CORES + c) for z in range(hop + 1) for c in range(CORES)
        ]
        down = [
            ((layers - 1 - z) * CORES + c, (layers - 2 - z) * CORES + c)
            for z in range(hop + 1)
            for c in range(CORES)
        ]
        up_target = jnp.clip(layers - 1 - hop + layer, 0, layers - 1)
        down_target = jnp.clip(hop - (layers - 1 - layer), 0, layers - 1)
        for h in range(halves):
            def own(target):
                return lax.dynamic_slice(
                    chip_sums, (target, h * half_rows, 0), (1, half_rows, feat_width)
                )[0]

            def joined(target, came):
                if came is None:
                    return own(target)
                return (own(target).astype(jnp.float32) + came.astype(jnp.float32)).astype(
                    jnp.bfloat16
                )

            right[h] = lax.ppermute(joined(up_target, right[h]), "region", up)
            left[h] = lax.ppermute(joined(down_target, left[h]), "region", down)

    wanted_owner = jnp.take(owners[0], requests[0], axis=0) ^ group
    chosen = []
    for k in range(wanted_owner.shape[0]):
        block = blocks[0]
        for j in range(1, group_count):
            block = jnp.where(wanted_owner[k] == j, blocks[j], block)
        chosen.append(block)
    candidates = jnp.concatenate(chosen)
    cand_count = candidates.shape[0]
    scores = (
        lax.dot_general(
            features, candidates, (((1,), (1,)), ((), ())), preferred_element_type=jnp.float32
        )
        / exponent_sharpness
    )
    shifted = scores - jnp.max(scores, axis=1, keepdims=True)
    expo = jnp.exp(shifted)
    likelihoods = expo / jnp.sum(expo, axis=1, keepdims=True)
    column = jnp.arange(cand_count, dtype=jnp.int32)
    target = (
        jnp.where(column < block_rows, (1.0 - smoothing) / block_rows, 0.0) + smoothing / cand_count
    ).astype(jnp.float32)
    logit_grad = ((likelihoods - target[None, :]) / exponent_sharpness).astype(jnp.bfloat16)
    feat_grad = jnp.dot(logit_grad, candidates, preferred_element_type=jnp.float32).astype(
        jnp.bfloat16
    )

    my_rows = region * block_rows + jnp.arange(block_rows, dtype=jnp.int32)
    counts = jnp.sum(
        (my_rows[:, None] == all_labels.reshape(-1)[None, :]).astype(jnp.float32), axis=1
    )
    own_sums = lax.dynamic_index_in_dim(chip_sums, layer, 0, keepdims=False).astype(jnp.float32)
    sums = (
        own_sums
        + jnp.concatenate(right).astype(jnp.float32)
        + jnp.concatenate(left).astype(jnp.float32)
    )
    old_rows = memory.astype(jnp.float32)
    averaged = sums / jnp.maximum(counts, 1.0)[:, None]
    mixed = jnp.where(
        counts[:, None] > 0, momentum_keep * old_rows + (1.0 - momentum_keep) * averaged, old_rows
    )
    scale = lax.rsqrt(jnp.mean(mixed * mixed, axis=1, keepdims=True) + 1e-06) * D ** (-0.5)
    new_memory = (mixed * scale).astype(jnp.bfloat16)
    return (feat_grad, new_memory)


def solution(mesh):
    placed = (
        P(("region", "group"), None),
        P(("region", "group"), None),
        P(("region", "group"), None),
        P("region", None),
        P(("region", "group"), None),
    )
    return jax.shard_map(
        on_device,
        mesh=mesh,
        in_specs=placed,
        out_specs=(P(("region", "group"), None), P(("region", "group"), None)),
        check_vma=False,
    )
```

```python
import functools

import jax
import jax.numpy as jnp
from jax import lax
from jax.experimental import pallas as pl
from jax.experimental.pallas import tpu as pltpu
from jax.sharding import PartitionSpec as P

D = 2048
CORES = 2
LANES = 128
HALVES = 2
EXTRA = 16
BASE = 8

exponent_sharpness = 0.05
smoothing = 0.1
momentum_keep = 0.2

VMEM = pl.BlockSpec(memory_space=pltpu.VMEM)
SMEM = pl.BlockSpec(memory_space=pltpu.SMEM)
ANY = pl.BlockSpec(memory_space=pl.ANY)
PARAMS = pltpu.CompilerParams(vmem_limit_bytes=32 * 2**20)


def write_sums(base, labels_ref, features_ref, block_rows, came, store):
    crop_count, feat_width = features_ref.shape
    half_rows = block_rows // HALVES
    slabs = feat_width // LANES
    value = base + lax.broadcasted_iota(jnp.int32, (block_rows, crop_count), 0)
    match = jnp.where(labels_ref[...] == value, 1.0, 0.0).astype(jnp.bfloat16)

    def put(h, first, part):
        if came is not None:
            part = part + came(h, first, part.shape[0]).astype(jnp.float32)
        store(h, first, part.astype(jnp.bfloat16))

    wide = 4
    for s in range(0, slabs, wide):
        part = jnp.dot(
            match,
            features_ref[:, s * LANES : (s + wide) * LANES],
            preferred_element_type=jnp.float32,
        )
        for h in range(HALVES):
            for i in range(wide):
                put(
                    h,
                    (s + i) * half_rows,
                    part[h * half_rows : (h + 1) * half_rows, i * LANES : (i + 1) * LANES],
                )
    counts = lax.dot_general(
        jnp.ones((EXTRA, crop_count), jnp.bfloat16),
        match,
        (((1,), (1,)), ((), ())),
        preferred_element_type=jnp.float32,
    )
    high = jnp.floor(counts * (1.0 / BASE))
    digit = lax.broadcasted_iota(jnp.int32, counts.shape, 0)
    digits = jnp.where(digit == 0, counts - BASE * high, jnp.where(digit == 1, high, 0.0))
    for h in range(HALVES):
        put(h, slabs * half_rows, digits)


def first_kernel(block_rows, base_ref, labels_ref, features_ref, *rest):
    came_ref, outs = (rest[0], rest[1:]) if len(rest) > HALVES else (None, rest)

    def store(h, first, part):
        outs[h][pl.ds(first, part.shape[0]), :] = part

    came = None
    if came_ref is not None:
        came = lambda h, first, rows: came_ref[h, pl.ds(first, rows), :]
    write_sums(base_ref[0], labels_ref, features_ref, block_rows, came, store)


def sent_first_kernel(block_rows, base_ref, labels_ref, features_ref, out_ref):
    def store(h, first, part):
        out_ref[h, pl.ds(first, part.shape[0]), :] = part

    write_sums(base_ref[0], labels_ref, features_ref, block_rows, None, store)


def sent_rest_kernel(block_rows, base_ref, labels_ref, features_ref, out_ref):
    def one(p, carry):
        def store(h, first, part):
            out_ref[p, h, pl.ds(first, part.shape[0]), :] = part

        write_sums(base_ref[p + 1], labels_ref, features_ref, block_rows, None, store)
        return carry

    lax.fori_loop(0, out_ref.shape[0], one, 0)


def all_kernel(block_rows, base_ref, labels_ref, features_ref, came_first_ref, came_rest_ref, out_ref):
    def first_store(h, first, part):
        out_ref[0, h, pl.ds(first, part.shape[0]), :] = part

    write_sums(
        base_ref[0],
        labels_ref,
        features_ref,
        block_rows,
        lambda h, first, rows: came_first_ref[h, pl.ds(first, rows), :],
        first_store,
    )

    def one(p, carry):
        def store(h, first, part):
            out_ref[p + 1, h, pl.ds(first, part.shape[0]), :] = part

        write_sums(
            base_ref[p + 1],
            labels_ref,
            features_ref,
            block_rows,
            lambda h, first, rows: came_rest_ref[p, h, pl.ds(first, rows), :],
            store,
        )
        return carry

    lax.fori_loop(0, came_rest_ref.shape[0], one, 0)


def update_kernel(memory_ref, own_ref, *rest):
    came_refs, out_ref, mixed_ref = rest[:-2], rest[-2], rest[-1]
    block_rows, feat_width = memory_ref.shape
    half_rows = block_rows // HALVES
    slabs = feat_width // LANES
    for h in range(HALVES):
        mine = came_refs[h::HALVES]

        def total(first, rows):
            t = own_ref[h, pl.ds(first, rows), :].astype(jnp.float32)
            for ref in mine:
                t = t + ref[pl.ds(first, rows), :].astype(jnp.float32)
            return t

        digits = total(slabs * half_rows, EXTRA)
        counts_row = digits[0:1, :] + BASE * digits[1:2, :]
        row = lax.broadcasted_iota(jnp.int32, (half_rows, LANES), 0) + h * half_rows
        lane = lax.broadcasted_iota(jnp.int32, (half_rows, LANES), 1)
        counts = jnp.sum(jnp.where(row == lane, counts_row, 0.0), axis=1, keepdims=True)
        seen = counts > 0
        divisor = jnp.maximum(counts, 1.0)
        squares = jnp.zeros((half_rows, LANES), jnp.float32)
        for s in range(slabs):
            old = memory_ref[pl.ds(h * half_rows, half_rows), pl.ds(s * LANES, LANES)].astype(
                jnp.float32
            )
            averaged = total(s * half_rows, half_rows) / divisor
            mixed = jnp.where(seen, momentum_keep * old + (1.0 - momentum_keep) * averaged, old)
            mixed_ref[:, pl.ds(s * LANES, LANES)] = mixed
            squares = squares + mixed * mixed
        mean = jnp.sum(squares, axis=1, keepdims=True) * (1.0 / feat_width)
        scale = lax.rsqrt(mean + 1e-06) * D ** (-0.5)
        out_ref[pl.ds(h * half_rows, half_rows), :] = (mixed_ref[...] * scale).astype(jnp.bfloat16)


def grad_kernel(wanted_ref, features_ref, *rest):
    out_ref, candidates_ref, sems = rest[-3:]
    blocks = rest[:-3]
    block_rows = blocks[0].shape[0]
    cand_count = candidates_ref.shape[0]
    wanted_count = cand_count // block_rows

    def copy(j, k):
        return pltpu.make_async_copy(
            blocks[j], candidates_ref.at[pl.ds(k * block_rows, block_rows), :], sems.at[k]
        )

    for k in range(wanted_count):
        for j in range(len(blocks)):
            @pl.when(wanted_ref[k] == j)
            def _():
                copy(j, k).start()
    for k in range(wanted_count):
        copy(0, k).wait()
    scores = (
        lax.dot_general(
            features_ref[...],
            candidates_ref[...],
            (((1,), (1,)), ((), ())),
            preferred_element_type=jnp.float32,
        )
        / exponent_sharpness
    )
    expo = jnp.exp(scores - jnp.max(scores, axis=1, keepdims=True))
    likelihoods = expo / jnp.sum(expo, axis=1, keepdims=True)
    column = lax.broadcasted_iota(jnp.int32, (1, cand_count), 1)
    target = jnp.where(column < block_rows, (1.0 - smoothing) / block_rows, 0.0) + (
        smoothing / cand_count
    )
    logit_grad = ((likelihoods - target) / exponent_sharpness).astype(jnp.bfloat16)
    wide = 512
    for n in range(0, out_ref.shape[1], wide):
        out_ref[:, n : n + wide] = jnp.dot(
            logit_grad, candidates_ref[:, n : n + wide], preferred_element_type=jnp.float32
        ).astype(jnp.bfloat16)


def on_device(features, memory, requests, owners, labels):
    group_count = lax.axis_size("group")
    region_count = lax.axis_size("region")
    layers = region_count // CORES
    crop_count, feat_width = features.shape
    block_rows = memory.shape[0]
    half_rows = block_rows // HALVES
    pay_rows = feat_width // LANES * half_rows + EXTRA
    region = lax.axis_index("region")
    group = lax.axis_index("group")
    layer, core = region // CORES, region % CORES
    below = layer < layers // 2
    bf16 = jnp.bfloat16

    place = jnp.arange(layers, dtype=jnp.int32)
    layer_order = jnp.where(below, layers - 1 - place, place)
    place_of = lambda t: jnp.where(below, layers - 1 - t, t)
    base_own = ((layer_order * CORES + core) * block_rows).astype(jnp.int32)
    base_away = ((layer_order * CORES + 1 - core) * block_rows).astype(jnp.int32)

    def cost(targets, came):
        rows = targets * block_rows
        return pl.CostEstimate(
            flops=2 * rows * crop_count * feat_width,
            bytes_accessed=2 * feat_width * (crop_count + rows * (1 + came)),
            transcendentals=0,
        )

    swap = [(r, r ^ 1) for r in range(region_count)]
    payload = jax.ShapeDtypeStruct((pay_rows, LANES), bf16)
    sent_first = pl.pallas_call(
        functools.partial(sent_first_kernel, block_rows),
        out_shape=jax.ShapeDtypeStruct((HALVES, pay_rows, LANES), bf16),
        in_specs=[SMEM, VMEM, VMEM],
        out_specs=VMEM,
        compiler_params=PARAMS,
        cost_estimate=cost(1, 0),
        name="away_first",
    )(base_away, labels, features)
    came_first = lax.ppermute(sent_first, "region", swap)
    sent_rest = pl.pallas_call(
        functools.partial(sent_rest_kernel, block_rows),
        out_shape=jax.ShapeDtypeStruct((layers - 1, HALVES, pay_rows, LANES), bf16),
        in_specs=[SMEM, VMEM, VMEM],
        out_specs=VMEM,
        compiler_params=PARAMS,
        cost_estimate=cost(layers - 1, 0),
        name="away_rest",
    )(base_away, labels, features)
    came_rest = lax.ppermute(sent_rest, "region", swap)
    first = pl.pallas_call(
        functools.partial(first_kernel, block_rows),
        out_shape=[payload] * HALVES,
        in_specs=[SMEM, VMEM, VMEM, VMEM],
        out_specs=[VMEM] * HALVES,
        compiler_params=PARAMS,
        cost_estimate=cost(1, 1),
        name="chip_first",
    )(base_own, labels, features, came_first)
    chip = pl.pallas_call(
        functools.partial(all_kernel, block_rows),
        out_shape=jax.ShapeDtypeStruct((layers, HALVES, pay_rows, LANES), bf16),
        in_specs=[SMEM, VMEM, VMEM, VMEM, VMEM],
        out_specs=VMEM,
        compiler_params=PARAMS,
        cost_estimate=cost(layers, 1),
        name="chip_all",
    )(base_own, labels, features, came_first, came_rest)

    sent_memory, chip = lax.optimization_barrier((memory, chip))
    blocks = [memory] + [
        lax.ppermute(sent_memory, "group", [(g, g ^ k) for g in range(group_count)])
        for k in range(1, group_count)
    ]

    even = [(r, ((r // CORES) ^ 1) * CORES + r % CORES) for r in range(region_count)]
    odd = []
    for z in range(1, layers - 1):
        other = z + 1 if z % 2 else z - 1
        odd += [(z * CORES + c, other * CORES + c) for c in range(CORES)]

    def own(target, h):
        at = place_of(jnp.clip(target, 0, layers - 1))
        return lax.dynamic_slice(chip, (at, h, 0, 0), (1, 1, pay_rows, LANES))[0, 0]

    def joined(target, h, came):
        return (own(target, h).astype(jnp.float32) + came.astype(jnp.float32)).astype(bf16)

    even_came = [None] * HALVES
    odd_came = [None] * HALVES
    for hop in range(layers - 1):
        up_target = layers - 1 - hop + layer
        down_target = hop - (layers - 1 - layer)
        even_target = jnp.where(layer % 2 == 0, up_target, down_target)
        odd_target = jnp.where(layer % 2 == 0, down_target, up_target)
        for h in range(HALVES):
            if hop == 0:
                even_next = first[h]
            elif hop == 1:
                even_next, even_came[h] = lax.optimization_barrier((chip[1, h], even_came[h]))
            else:
                even_next = joined(even_target, h, odd_came[h])
            if hop > 0:
                odd_came[h] = lax.ppermute(joined(odd_target, h, even_came[h]), "region", odd)
            even_came[h] = lax.ppermute(even_next, "region", even)

    wanted = (jnp.take(owners[0], requests[0], axis=0) ^ group).astype(jnp.int32)
    cand_count = wanted.shape[0] * block_rows
    feat_grad = pl.pallas_call(
        grad_kernel,
        out_shape=jax.ShapeDtypeStruct(features.shape, bf16),
        in_specs=[SMEM, VMEM] + [ANY] * group_count,
        out_specs=VMEM,
        scratch_shapes=[
            pltpu.VMEM((cand_count, feat_width), bf16),
            pltpu.SemaphoreType.DMA((wanted.shape[0],)),
        ],
        compiler_params=PARAMS,
        cost_estimate=pl.CostEstimate(
            flops=4 * crop_count * cand_count * feat_width,
            bytes_accessed=2 * feat_width * (2 * crop_count + cand_count),
            transcendentals=crop_count * cand_count,
        ),
        name="feat_grad",
    )(wanted, features, *blocks)

    mine = lax.dynamic_index_in_dim(chip, place_of(layer), 0, keepdims=False)
    new_memory = pl.pallas_call(
        update_kernel,
        out_shape=jax.ShapeDtypeStruct(memory.shape, bf16),
        in_specs=[VMEM] * (2 + 2 * HALVES),
        out_specs=VMEM,
        scratch_shapes=[pltpu.VMEM((half_rows, feat_width), jnp.float32)],
        compiler_params=PARAMS,
        cost_estimate=pl.CostEstimate(
            flops=10 * block_rows * feat_width,
            bytes_accessed=2 * block_rows * feat_width * 5,
            transcendentals=0,
        ),
        name="update",
    )(memory, mine, *even_came, *odd_came)
    return (feat_grad, new_memory)


def solution(mesh):
    placed = (
        P(("region", "group"), None),
        P(("region", "group"), None),
        P(("region", "group"), None),
        P("region", None),
        P(("region", "group"), None),
    )
    return jax.shard_map(
        on_device,
        mesh=mesh,
        in_specs=placed,
        out_specs=(P(("region", "group"), None), P(("region", "group"), None)),
        check_vma=False,
    )
```

```python
import functools

import jax
import jax.numpy as jnp
from jax import lax
from jax.experimental import pallas as pl
from jax.experimental.pallas import tpu as pltpu
from jax.sharding import PartitionSpec as P

D = 2048
CORES = 2
WIDE = 4
LANES = 128
HALVES = 2
EXTRA = 16
BASE = 8

exponent_sharpness = 0.05
smoothing = 0.1
momentum_keep = 0.2

VMEM = pl.BlockSpec(memory_space=pltpu.VMEM)
SMEM = pl.BlockSpec(memory_space=pltpu.SMEM)
PARAMS = pltpu.CompilerParams(vmem_limit_bytes=16 * 2**20)


def write_sums(base, labels_ref, features_ref, block_rows, came, store, ready=None):
    crop_count, feat_width = features_ref.shape
    half_rows = block_rows // HALVES
    slabs = feat_width // LANES
    value = base + lax.broadcasted_iota(jnp.int32, (block_rows, crop_count), 0)
    match = jnp.where(labels_ref[...] == value, 1.0, 0.0).astype(jnp.bfloat16)

    def put(h, first, part):
        if came is not None:
            part = part + came(h, first, part.shape[0]).astype(jnp.float32)
        store(h, first, part.astype(jnp.bfloat16))

    wide = WIDE
    for s in range(0, slabs, wide):
        if ready is not None:
            ready(s // wide)
        part = jnp.dot(
            match,
            features_ref[:, s * LANES : (s + wide) * LANES],
            preferred_element_type=jnp.float32,
        )
        for h in range(HALVES):
            for i in range(wide):
                put(
                    h,
                    (s + i) * half_rows,
                    part[h * half_rows : (h + 1) * half_rows, i * LANES : (i + 1) * LANES],
                )
    counts = lax.dot_general(
        jnp.ones((EXTRA, crop_count), jnp.bfloat16),
        match,
        (((1,), (1,)), ((), ())),
        preferred_element_type=jnp.float32,
    )
    high = jnp.floor(counts * (1.0 / BASE))
    digit = lax.broadcasted_iota(jnp.int32, counts.shape, 0)
    digits = jnp.where(digit == 0, counts - BASE * high, jnp.where(digit == 1, high, 0.0))
    for h in range(HALVES):
        put(h, slabs * half_rows, digits)


def layer_at(place, layers):
    layer = lax.axis_index("region") // CORES
    return jnp.where(layer < layers // 2, layers - 1 - place, place)


def base_at(place, layers, core, block_rows):
    return (layer_at(place, layers) * CORES + core) * block_rows


def block_of(ref, *at):
    def store(h, first, part):
        ref[(*at, h, pl.ds(first, part.shape[0]), slice(None))] = part

    return store


def came_at(ref, *at):
    return lambda h, first, rows: ref[(*at, h, pl.ds(first, rows), slice(None))]


def away_kernel(
    layers, block_rows, labels_hbm, features_hbm, first_ref, rest_ref, labels_ref, features_ref, sems
):
    columns = WIDE * LANES
    copies = [pltpu.make_async_copy(labels_hbm, labels_ref, sems.at[0])]
    for i in range(features_ref.shape[1] // columns):
        part = (slice(None), pl.ds(i * columns, columns))
        copies.append(
            pltpu.make_async_copy(features_hbm.at[part], features_ref.at[part], sems.at[i + 1])
        )
    for copy in copies:
        copy.start()
    copies[0].wait()
    core = 1 - lax.axis_index("region") % CORES
    write_sums(
        base_at(0, layers, core, block_rows),
        labels_ref,
        features_ref,
        block_rows,
        None,
        block_of(first_ref, 0),
        lambda i: copies[i + 1].wait(),
    )

    def one(p, carry):
        base = base_at(p + 1, layers, core, block_rows)
        write_sums(base, labels_ref, features_ref, block_rows, None, block_of(rest_ref, p))
        return carry

    lax.fori_loop(0, layers - 1, one, 0)


def chip_kernel(layers, block_rows, start, labels_ref, features_ref, came_ref, out_ref):
    core = lax.axis_index("region") % CORES

    def one(p, carry):
        base = base_at(p + start, layers, core, block_rows)
        write_sums(
            base, labels_ref, features_ref, block_rows, came_at(came_ref, p), block_of(out_ref, p)
        )
        return carry

    lax.fori_loop(0, out_ref.shape[0], one, 0)


def join_kernel(layers, hop, odd, first_ref, rest_ref, came_ref, out_ref):
    layer = lax.axis_index("region") // CORES
    up = (layer % 2 == 1) if odd else (layer % 2 == 0)
    target = jnp.where(up, layers - 1 - hop + layer, hop - (layers - 1 - layer))
    target = jnp.clip(target, 0, layers - 1)
    place = jnp.where(layer < layers // 2, layers - 1 - target, target)

    def add(mine):
        out_ref[0] = (
            mine.astype(jnp.float32) + came_ref[0].astype(jnp.float32)
        ).astype(jnp.bfloat16)

    @pl.when(place == 0)
    def _():
        add(first_ref[0])

    @pl.when(place > 0)
    def _():
        add(rest_ref[jnp.maximum(place - 1, 0)])


def join_first_kernel(first_ref, came_ref, rest_ref, out_ref, second_ref):
    out_ref[...] = (
        first_ref[...].astype(jnp.float32) + came_ref[...].astype(jnp.float32)
    ).astype(jnp.bfloat16)
    second_ref[0] = rest_ref[0]


def update_kernel(layers, memory_ref, rest_ref, *rest):
    layer = lax.axis_index("region") // CORES
    place = jnp.where(layer < layers // 2, layers - 1 - layer, layer) - 1
    came_refs, out_ref, mixed_ref = rest[:-2], rest[-2], rest[-1]
    block_rows, feat_width = memory_ref.shape
    half_rows = block_rows // HALVES
    slabs = feat_width // LANES
    for h in range(HALVES):

        def total(first, rows):
            t = rest_ref[place, h, pl.ds(first, rows), :].astype(jnp.float32)
            for ref in came_refs:
                t = t + ref[0, h, pl.ds(first, rows), :].astype(jnp.float32)
            return t

        digits = total(slabs * half_rows, EXTRA)
        counts_row = digits[0:1, :] + BASE * digits[1:2, :]
        row = lax.broadcasted_iota(jnp.int32, (half_rows, LANES), 0) + h * half_rows
        lane = lax.broadcasted_iota(jnp.int32, (half_rows, LANES), 1)
        counts = jnp.sum(jnp.where(row == lane, counts_row, 0.0), axis=1, keepdims=True)
        seen = counts > 0
        divisor = jnp.maximum(counts, 1.0)
        squares = jnp.zeros((half_rows, LANES), jnp.float32)
        for s in range(slabs):
            old = memory_ref[pl.ds(h * half_rows, half_rows), pl.ds(s * LANES, LANES)].astype(
                jnp.float32
            )
            averaged = total(s * half_rows, half_rows) / divisor
            mixed = jnp.where(seen, momentum_keep * old + (1.0 - momentum_keep) * averaged, old)
            mixed_ref[:, pl.ds(s * LANES, LANES)] = mixed
            squares = squares + mixed * mixed
        mean = jnp.sum(squares, axis=1, keepdims=True) * (1.0 / feat_width)
        scale = lax.rsqrt(mean + 1e-06) * D ** (-0.5)
        out_ref[pl.ds(h * half_rows, half_rows), :] = (mixed_ref[...] * scale).astype(jnp.bfloat16)


def grad_kernel(requests_ref, owners_ref, features_ref, *rest):
    group = lax.axis_index("group")
    out_ref, candidates_ref, sems = rest[-3:]
    blocks = rest[:-3]
    block_rows = blocks[0].shape[0]
    cand_count = candidates_ref.shape[0]
    wanted_count = cand_count // block_rows

    def copy(j, k):
        return pltpu.make_async_copy(
            blocks[j], candidates_ref.at[pl.ds(k * block_rows, block_rows), :], sems.at[k]
        )

    for k in range(wanted_count):
        place = owners_ref[0, requests_ref[0, k]] ^ group
        for j in range(len(blocks)):
            @pl.when(place == j)
            def _():
                copy(j, k).start()
    for k in range(wanted_count):
        copy(0, k).wait()
    scores = (
        lax.dot_general(
            features_ref[...],
            candidates_ref[...],
            (((1,), (1,)), ((), ())),
            preferred_element_type=jnp.float32,
        )
        / exponent_sharpness
    )
    expo = jnp.exp(scores - jnp.max(scores, axis=1, keepdims=True))
    likelihoods = expo / jnp.sum(expo, axis=1, keepdims=True)
    column = lax.broadcasted_iota(jnp.int32, (1, cand_count), 1)
    target = jnp.where(column < block_rows, (1.0 - smoothing) / block_rows, 0.0) + (
        smoothing / cand_count
    )
    logit_grad = ((likelihoods - target) / exponent_sharpness).astype(jnp.bfloat16)
    wide = 512
    for n in range(0, out_ref.shape[1], wide):
        out_ref[:, n : n + wide] = jnp.dot(
            logit_grad, candidates_ref[:, n : n + wide], preferred_element_type=jnp.float32
        ).astype(jnp.bfloat16)


def on_device(features, memory, requests, owners, labels):
    group_count = lax.axis_size("group")
    region_count = lax.axis_size("region")
    layers = region_count // CORES
    crop_count, feat_width = features.shape
    block_rows = memory.shape[0]
    half_rows = block_rows // HALVES
    pay_rows = feat_width // LANES * half_rows + EXTRA
    bf16 = jnp.bfloat16
    after = lax.optimization_barrier

    def call(kernel, name, out_shape, operands, flops, scratch=(), smem=0, any_from=None, params=PARAMS):
        outs = out_shape if isinstance(out_shape, list) else [out_shape]
        flat, tree = jax.tree.flatten(operands)
        specs = [SMEM if i < smem else VMEM for i in range(len(flat))]
        if any_from is not None:
            specs[any_from:] = [pl.BlockSpec(memory_space=pl.ANY)] * (len(flat) - any_from)
        return pl.pallas_call(
            kernel,
            out_shape=out_shape,
            in_specs=specs,
            out_specs=[VMEM] * len(outs) if isinstance(out_shape, list) else VMEM,
            scratch_shapes=list(scratch),
            compiler_params=params,
            cost_estimate=pl.CostEstimate(
                flops=flops,
                bytes_accessed=sum(2 * x.size for x in [*flat, *outs]),
                transcendentals=0,
            ),
            name=name,
        )(*flat)

    swap = [(r, r ^ 1) for r in range(region_count)]
    block_flops = 2 * block_rows * crop_count * feat_width
    part = functools.partial

    def payloads(count):
        return jax.ShapeDtypeStruct((count, HALVES, pay_rows, LANES), bf16)

    away_first, away_rest = call(
        part(away_kernel, layers, block_rows),
        "away",
        [payloads(1), payloads(layers - 1)],
        (labels, features),
        block_flops * layers,
        scratch=(
            pltpu.VMEM(labels.shape, labels.dtype),
            pltpu.VMEM(features.shape, bf16),
            pltpu.SemaphoreType.DMA((feat_width // (WIDE * LANES) + 1,)),
        ),
        any_from=0,
        params=pltpu.CompilerParams(vmem_limit_bytes=60 * 2**20),
    )
    came_first = lax.ppermute(away_first, "region", swap)
    first = call(
        part(chip_kernel, layers, block_rows, 0),
        "chip_first",
        payloads(1),
        (labels, features, came_first),
        block_flops,
    )
    first, away_rest, sent_memory = after((first, away_rest, memory))
    rest = call(
        part(chip_kernel, layers, block_rows, 1),
        "chip_rest",
        payloads(layers - 1),
        (labels, features, lax.ppermute(away_rest, "region", swap)),
        block_flops * (layers - 1),
    )

    blocks = {0: sent_memory}
    near = [k for k in range(1, group_count) if k & (k - 1) == 0]
    far = [k for k in range(1, group_count) if k & (k - 1)]

    def fetch(ks):
        for k in ks:
            bit = 1 << (k.bit_length() - 1)
            blocks[k] = lax.ppermute(
                blocks[k ^ bit], "group", [(g, g ^ bit) for g in range(group_count)]
            )

    even = [(r, ((r // CORES) ^ 1) * CORES + r % CORES) for r in range(region_count)]
    odd = []
    for z in range(1, layers - 1):
        other = z + 1 if z % 2 else z - 1
        odd += [(z * CORES + c, other * CORES + c) for c in range(CORES)]

    def joined(hop, is_odd, came):
        return call(
            part(join_kernel, layers, hop, is_odd),
            "join_odd" if is_odd else "join_even",
            payloads(1),
            (first, rest, came),
            HALVES * pay_rows * LANES,
        )

    even_came = lax.ppermute(first, "region", even)
    fetch(near)
    odd_next, even_next = call(
        join_first_kernel,
        "join_first",
        [payloads(1), payloads(1)],
        (first, even_came, rest),
        HALVES * pay_rows * LANES,
    )
    tied = after((even_next, odd_next, {k: blocks[k] for k in near}))
    even_next, odd_next = tied[:2]
    blocks.update(tied[2])
    odd_came = lax.ppermute(odd_next, "region", odd)
    even_came = lax.ppermute(even_next, "region", even)
    fetch(far)
    for hop in range(2, layers - 1):
        even_next, odd_next = joined(hop, False, odd_came), joined(hop, True, even_came)
        if hop == 2:
            tied = after((even_next, odd_next, {k: blocks[k] for k in far}))
            even_next, odd_next = tied[:2]
            blocks.update(tied[2])
        even_came = lax.ppermute(even_next, "region", even)
        odd_came = lax.ppermute(odd_next, "region", odd)

    cand_count = requests.shape[1] * block_rows
    feat_grad = call(
        grad_kernel,
        "feat_grad",
        jax.ShapeDtypeStruct(features.shape, bf16),
        (requests, owners, features, *[blocks[k] for k in range(group_count)]),
        4 * crop_count * cand_count * feat_width,
        scratch=(
            pltpu.VMEM((cand_count, feat_width), bf16),
            pltpu.SemaphoreType.DMA((requests.shape[1],)),
        ),
        smem=2,
        any_from=3,
    )

    new_memory = call(
        part(update_kernel, layers),
        "update",
        jax.ShapeDtypeStruct(memory.shape, bf16),
        (memory, rest, even_came, odd_came),
        10 * block_rows * feat_width,
        scratch=(pltpu.VMEM((half_rows, feat_width), jnp.float32),),
    )
    return (feat_grad, new_memory)


def solution(mesh):
    placed = (
        P(("region", "group"), None),
        P(("region", "group"), None),
        P(("region", "group"), None),
        P("region", None),
        P(("region", "group"), None),
    )
    return jax.shard_map(
        on_device,
        mesh=mesh,
        in_specs=placed,
        out_specs=(P(("region", "group"), None), P(("region", "group"), None)),
        check_vma=False,
    )
```

```python
import functools

import jax
import jax.numpy as jnp
from jax import lax
from jax.experimental import pallas as pl
from jax.experimental.pallas import tpu as pltpu
from jax.sharding import PartitionSpec as P

D = 2048
CORES = 2
WIDE = 4
LANES = 128
HALVES = 2
EXTRA = 16
BASE = 8

exponent_sharpness = 0.05
smoothing = 0.1
momentum_keep = 0.2

VMEM = pl.BlockSpec(memory_space=pltpu.VMEM)
SMEM = pl.BlockSpec(memory_space=pltpu.SMEM)
PARAMS = pltpu.CompilerParams(vmem_limit_bytes=16 * 2**20)


def write_sums(base, labels_ref, features_ref, block_rows, came, store, ready=None):
    crop_count, feat_width = features_ref.shape
    half_rows = block_rows // HALVES
    slabs = feat_width // LANES
    value = base + lax.broadcasted_iota(jnp.int32, (block_rows, crop_count), 0)
    match = jnp.where(labels_ref[...] == value, 1.0, 0.0).astype(jnp.bfloat16)

    def put(h, first, part):
        if came is not None:
            part = part + came(h, first, part.shape[0]).astype(jnp.float32)
        store(h, first, part.astype(jnp.bfloat16))

    wide = WIDE
    for s in range(0, slabs, wide):
        if ready is not None:
            ready(s // wide)
        part = jnp.dot(
            match,
            features_ref[:, s * LANES : (s + wide) * LANES],
            preferred_element_type=jnp.float32,
        )
        for h in range(HALVES):
            for i in range(wide):
                put(
                    h,
                    (s + i) * half_rows,
                    part[h * half_rows : (h + 1) * half_rows, i * LANES : (i + 1) * LANES],
                )
    counts = lax.dot_general(
        jnp.ones((EXTRA, crop_count), jnp.bfloat16),
        match,
        (((1,), (1,)), ((), ())),
        preferred_element_type=jnp.float32,
    )
    high = jnp.floor(counts * (1.0 / BASE))
    digit = lax.broadcasted_iota(jnp.int32, counts.shape, 0)
    digits = jnp.where(digit == 0, counts - BASE * high, jnp.where(digit == 1, high, 0.0))
    for h in range(HALVES):
        put(h, slabs * half_rows, digits)


def layer_at(place, layers):
    layer = lax.axis_index("region") // CORES
    return jnp.where(layer < layers // 2, layers - 1 - place, place)


def base_at(place, layers, core, block_rows):
    return (layer_at(place, layers) * CORES + core) * block_rows


def block_of(ref, *at):
    def store(h, first, part):
        ref[(*at, h, pl.ds(first, part.shape[0]), slice(None))] = part

    return store


def came_at(ref, *at):
    return lambda h, first, rows: ref[(*at, h, pl.ds(first, rows), slice(None))]


def away_first_kernel(
    layers, block_rows, labels_hbm, features_hbm, out_ref, labels_ref, features_ref, sems
):
    columns = WIDE * LANES
    copies = [pltpu.make_async_copy(labels_hbm, labels_ref, sems.at[0])]
    for i in range(features_ref.shape[1] // columns):
        part = (slice(None), pl.ds(i * columns, columns))
        copies.append(
            pltpu.make_async_copy(features_hbm.at[part], features_ref.at[part], sems.at[i + 1])
        )
    for copy in copies:
        copy.start()
    copies[0].wait()
    core = 1 - lax.axis_index("region") % CORES
    write_sums(
        base_at(0, layers, core, block_rows),
        labels_ref,
        features_ref,
        block_rows,
        None,
        block_of(out_ref, 0),
        lambda i: copies[i + 1].wait(),
    )


def away_rest_kernel(layers, block_rows, labels_ref, features_ref, out_ref):
    core = 1 - lax.axis_index("region") % CORES

    def one(p, carry):
        base = base_at(p + 1, layers, core, block_rows)
        write_sums(base, labels_ref, features_ref, block_rows, None, block_of(out_ref, p))
        return carry

    lax.fori_loop(0, layers - 1, one, 0)


def chip_first_kernel(layers, block_rows, labels_ref, features_ref, came_ref, *outs):
    base = base_at(0, layers, lax.axis_index("region") % CORES, block_rows)

    def store(h, first, part):
        outs[h][pl.ds(first, part.shape[0]), :] = part

    write_sums(base, labels_ref, features_ref, block_rows, came_at(came_ref, 0), store)


def chip_rest_kernel(layers, block_rows, labels_ref, features_ref, came_ref, second_ref, out_ref):
    core = lax.axis_index("region") % CORES

    def one(p, carry):
        base = base_at(p + 1, layers, core, block_rows)
        write_sums(
            base, labels_ref, features_ref, block_rows, came_at(came_ref, p), block_of(out_ref, p)
        )
        return carry

    lax.fori_loop(0, layers - 1, one, 0)
    second_ref[0] = out_ref[0]


def join_half_kernel(mine_ref, came_ref, out_ref):
    out_ref[...] = (
        mine_ref[...].astype(jnp.float32) + came_ref[...].astype(jnp.float32)
    ).astype(jnp.bfloat16)


def join_kernel(layers, hop, odd, *refs):
    first_refs, rest_ref, came_refs, out_ref = (
        refs[:HALVES],
        refs[HALVES],
        refs[HALVES + 1 : -1],
        refs[-1],
    )
    layer = lax.axis_index("region") // CORES
    up = (layer % 2 == 1) if odd else (layer % 2 == 0)
    target = jnp.where(up, layers - 1 - hop + layer, hop - (layers - 1 - layer))
    target = jnp.clip(target, 0, layers - 1)
    place = jnp.where(layer < layers // 2, layers - 1 - target, target)

    def add(mine):
        for h in range(HALVES):
            came = came_refs[h][...] if len(came_refs) > 1 else came_refs[0][0, h]
            out_ref[0, h] = (mine(h).astype(jnp.float32) + came.astype(jnp.float32)).astype(
                jnp.bfloat16
            )

    @pl.when(place == 0)
    def _():
        add(lambda h: first_refs[h][...])

    @pl.when(place > 0)
    def _():
        add(lambda h: rest_ref[jnp.maximum(place - 1, 0), h])


def update_kernel(layers, memory_ref, rest_ref, *rest):
    layer = lax.axis_index("region") // CORES
    place = jnp.where(layer < layers // 2, layers - 1 - layer, layer) - 1
    came_refs, out_ref, mixed_ref = rest[:-2], rest[-2], rest[-1]
    block_rows, feat_width = memory_ref.shape
    half_rows = block_rows // HALVES
    slabs = feat_width // LANES
    for h in range(HALVES):

        def total(first, rows):
            t = rest_ref[place, h, pl.ds(first, rows), :].astype(jnp.float32)
            for ref in came_refs:
                t = t + ref[0, h, pl.ds(first, rows), :].astype(jnp.float32)
            return t

        digits = total(slabs * half_rows, EXTRA)
        counts_row = digits[0:1, :] + BASE * digits[1:2, :]
        row = lax.broadcasted_iota(jnp.int32, (half_rows, LANES), 0) + h * half_rows
        lane = lax.broadcasted_iota(jnp.int32, (half_rows, LANES), 1)
        counts = jnp.sum(jnp.where(row == lane, counts_row, 0.0), axis=1, keepdims=True)
        seen = counts > 0
        divisor = jnp.maximum(counts, 1.0)
        squares = jnp.zeros((half_rows, LANES), jnp.float32)
        for s in range(slabs):
            old = memory_ref[pl.ds(h * half_rows, half_rows), pl.ds(s * LANES, LANES)].astype(
                jnp.float32
            )
            averaged = total(s * half_rows, half_rows) / divisor
            mixed = jnp.where(seen, momentum_keep * old + (1.0 - momentum_keep) * averaged, old)
            mixed_ref[:, pl.ds(s * LANES, LANES)] = mixed
            squares = squares + mixed * mixed
        mean = jnp.sum(squares, axis=1, keepdims=True) * (1.0 / feat_width)
        scale = lax.rsqrt(mean + 1e-06) * D ** (-0.5)
        out_ref[pl.ds(h * half_rows, half_rows), :] = (mixed_ref[...] * scale).astype(jnp.bfloat16)


def grad_kernel(requests_ref, owners_ref, features_ref, *rest):
    group = lax.axis_index("group")
    out_ref, candidates_ref, sems = rest[-3:]
    blocks = rest[:-3]
    block_rows = blocks[0].shape[0]
    cand_count = candidates_ref.shape[0]
    wanted_count = cand_count // block_rows

    def copy(j, k):
        return pltpu.make_async_copy(
            blocks[j], candidates_ref.at[pl.ds(k * block_rows, block_rows), :], sems.at[k]
        )

    for k in range(wanted_count):
        place = owners_ref[0, requests_ref[0, k]] ^ group
        for j in range(len(blocks)):
            @pl.when(place == j)
            def _():
                copy(j, k).start()
    for k in range(wanted_count):
        copy(0, k).wait()
    scores = (
        lax.dot_general(
            features_ref[...],
            candidates_ref[...],
            (((1,), (1,)), ((), ())),
            preferred_element_type=jnp.float32,
        )
        / exponent_sharpness
    )
    expo = jnp.exp(scores - jnp.max(scores, axis=1, keepdims=True))
    likelihoods = expo / jnp.sum(expo, axis=1, keepdims=True)
    column = lax.broadcasted_iota(jnp.int32, (1, cand_count), 1)
    target = jnp.where(column < block_rows, (1.0 - smoothing) / block_rows, 0.0) + (
        smoothing / cand_count
    )
    logit_grad = ((likelihoods - target) / exponent_sharpness).astype(jnp.bfloat16)
    wide = 512
    for n in range(0, out_ref.shape[1], wide):
        out_ref[:, n : n + wide] = jnp.dot(
            logit_grad, candidates_ref[:, n : n + wide], preferred_element_type=jnp.float32
        ).astype(jnp.bfloat16)


def on_device(features, memory, requests, owners, labels):
    group_count = lax.axis_size("group")
    region_count = lax.axis_size("region")
    layers = region_count // CORES
    crop_count, feat_width = features.shape
    block_rows = memory.shape[0]
    half_rows = block_rows // HALVES
    pay_rows = feat_width // LANES * half_rows + EXTRA
    bf16 = jnp.bfloat16
    after = lax.optimization_barrier

    def call(kernel, name, out_shape, operands, flops, scratch=(), smem=0, any_from=None, params=PARAMS):
        outs = out_shape if isinstance(out_shape, list) else [out_shape]
        flat, tree = jax.tree.flatten(operands)
        specs = [SMEM if i < smem else VMEM for i in range(len(flat))]
        if any_from is not None:
            specs[any_from:] = [pl.BlockSpec(memory_space=pl.ANY)] * (len(flat) - any_from)
        return pl.pallas_call(
            kernel,
            out_shape=out_shape,
            in_specs=specs,
            out_specs=[VMEM] * len(outs) if isinstance(out_shape, list) else VMEM,
            scratch_shapes=list(scratch),
            compiler_params=params,
            cost_estimate=pl.CostEstimate(
                flops=flops,
                bytes_accessed=sum(2 * x.size for x in [*flat, *outs]),
                transcendentals=0,
            ),
            name=name,
        )(*flat)

    swap = [(r, r ^ 1) for r in range(region_count)]
    block_flops = 2 * block_rows * crop_count * feat_width
    part = functools.partial

    def payloads(count):
        return jax.ShapeDtypeStruct((count, HALVES, pay_rows, LANES), bf16)

    away_first = call(
        part(away_first_kernel, layers, block_rows),
        "away_first",
        payloads(1),
        (labels, features),
        block_flops,
        scratch=(
            pltpu.VMEM(labels.shape, labels.dtype),
            pltpu.VMEM(features.shape, bf16),
            pltpu.SemaphoreType.DMA((feat_width // (WIDE * LANES) + 1,)),
        ),
        any_from=0,
        params=pltpu.CompilerParams(vmem_limit_bytes=60 * 2**20),
    )
    came_first = lax.ppermute(away_first, "region", swap)
    later_labels, away_first = after((labels, away_first))
    away_rest = call(
        part(away_rest_kernel, layers, block_rows),
        "away_rest",
        payloads(layers - 1),
        (later_labels, features),
        block_flops * (layers - 1),
    )
    first = call(
        part(chip_first_kernel, layers, block_rows),
        "chip_first",
        [jax.ShapeDtypeStruct((pay_rows, LANES), bf16)] * HALVES,
        (labels, features, came_first),
        block_flops,
    )
    first, away_rest, sent_memory = after((first, away_rest, memory))
    second, rest = call(
        part(chip_rest_kernel, layers, block_rows),
        "chip_rest",
        [payloads(1), payloads(layers - 1)],
        (labels, features, lax.ppermute(away_rest, "region", swap)),
        block_flops * (layers - 1),
    )

    blocks = {0: memory}

    def fetch(k, block):
        blocks[k] = lax.ppermute(block, "group", [(g, g ^ k) for g in range(group_count)])

    even = [(r, ((r // CORES) ^ 1) * CORES + r % CORES) for r in range(region_count)]
    odd = []
    for z in range(1, layers - 1):
        other = z + 1 if z % 2 else z - 1
        odd += [(z * CORES + c, other * CORES + c) for c in range(CORES)]

    def joined(hop, is_odd, came):
        return call(
            part(join_kernel, layers, hop, is_odd),
            "join_odd" if is_odd else "join_even",
            payloads(1),
            (*first, rest, *came),
            HALVES * pay_rows * LANES,
        )

    even_came = [lax.ppermute(x, "region", even) for x in first]
    for k in range(1, group_count):
        if k & (k - 1) == 0:
            fetch(k, sent_memory)
    odd_came = []
    for h in range(HALVES):
        leaves = call(
            join_half_kernel,
            "join_half",
            jax.ShapeDtypeStruct((pay_rows, LANES), bf16),
            (first[h], even_came[h]),
            pay_rows * LANES,
        )
        odd_came.append(lax.ppermute(leaves, "region", odd))
    later_memory, even_came[-1] = after((sent_memory, even_came[-1]))
    for k in range(1, group_count):
        if k & (k - 1):
            fetch(k, later_memory)
    even_came = [lax.ppermute(second, "region", even)]
    for hop in range(2, layers - 1):
        even_next, odd_next = joined(hop, False, odd_came), joined(hop, True, even_came)
        even_came = [lax.ppermute(even_next, "region", even)]
        odd_came = [lax.ppermute(odd_next, "region", odd)]

    cand_count = requests.shape[1] * block_rows
    feat_grad = call(
        grad_kernel,
        "feat_grad",
        jax.ShapeDtypeStruct(features.shape, bf16),
        (requests, owners, features, *[blocks[k] for k in range(group_count)]),
        4 * crop_count * cand_count * feat_width,
        scratch=(
            pltpu.VMEM((cand_count, feat_width), bf16),
            pltpu.SemaphoreType.DMA((requests.shape[1],)),
        ),
        smem=2,
        any_from=3,
    )

    new_memory = call(
        part(update_kernel, layers),
        "update",
        jax.ShapeDtypeStruct(memory.shape, bf16),
        (memory, rest, *even_came, *odd_came),
        10 * block_rows * feat_width,
        scratch=(pltpu.VMEM((half_rows, feat_width), jnp.float32),),
    )
    return (feat_grad, new_memory)


def solution(mesh):
    placed = (
        P(("region", "group"), None),
        P(("region", "group"), None),
        P(("region", "group"), None),
        P("region", None),
        P(("region", "group"), None),
    )
    return jax.shard_map(
        on_device,
        mesh=mesh,
        in_specs=placed,
        out_specs=(P(("region", "group"), None), P(("region", "group"), None)),
        check_vma=False,
    )
```

```python
import functools

import jax
import jax.numpy as jnp
from jax import lax
from jax.experimental import pallas as pl
from jax.experimental.pallas import tpu as pltpu
from jax.sharding import PartitionSpec as P

D = 2048
CORES = 2
WIDE = 4
LANES = 128
HALVES = 2
EXTRA = 16
BASE = 8

exponent_sharpness = 0.05
smoothing = 0.1
momentum_keep = 0.2

VMEM = pl.BlockSpec(memory_space=pltpu.VMEM)
SMEM = pl.BlockSpec(memory_space=pltpu.SMEM)
PARAMS = pltpu.CompilerParams(vmem_limit_bytes=16 * 2**20)


def write_sums(base, labels_ref, features_ref, block_rows, came, store):
    crop_count, feat_width = features_ref.shape
    half_rows = block_rows // HALVES
    slabs = feat_width // LANES
    value = base + lax.broadcasted_iota(jnp.int32, (block_rows, crop_count), 0)
    match = jnp.where(labels_ref[...] == value, 1.0, 0.0).astype(jnp.bfloat16)

    def put(h, first, part):
        if came is not None:
            part = part + came(h, first, part.shape[0]).astype(jnp.float32)
        store(h, first, part.astype(jnp.bfloat16))

    for s in range(0, slabs, WIDE):
        part = jnp.dot(
            match,
            features_ref[:, s * LANES : (s + WIDE) * LANES],
            preferred_element_type=jnp.float32,
        )
        for h in range(HALVES):
            for i in range(WIDE):
                put(
                    h,
                    (s + i) * half_rows,
                    part[h * half_rows : (h + 1) * half_rows, i * LANES : (i + 1) * LANES],
                )
    counts = lax.dot_general(
        jnp.ones((EXTRA, crop_count), jnp.bfloat16),
        match,
        (((1,), (1,)), ((), ())),
        preferred_element_type=jnp.float32,
    )
    high = jnp.floor(counts * (1.0 / BASE))
    digit = lax.broadcasted_iota(jnp.int32, counts.shape, 0)
    digits = jnp.where(digit == 0, counts - BASE * high, jnp.where(digit == 1, high, 0.0))
    for h in range(HALVES):
        put(h, slabs * half_rows, digits)


def layer_at(place, layers):
    layer = lax.axis_index("region") // CORES
    return jnp.where(layer < layers // 2, layers - 1 - place, place)


def base_at(place, layers, core, block_rows):
    return (layer_at(place, layers) * CORES + core) * block_rows


def block_of(ref, *at):
    def store(h, first, part):
        ref[(*at, h, pl.ds(first, part.shape[0]), slice(None))] = part

    return store


def came_at(ref, *at):
    return lambda h, first, rows: ref[(*at, h, pl.ds(first, rows), slice(None))]


def away_first_kernel(layers, block_rows, labels_ref, features_ref, out_ref):
    core = 1 - lax.axis_index("region") % CORES
    base = base_at(0, layers, core, block_rows)
    write_sums(base, labels_ref, features_ref, block_rows, None, block_of(out_ref, 0))


def away_rest_kernel(layers, block_rows, labels_ref, features_ref, out_ref):
    core = 1 - lax.axis_index("region") % CORES

    def one(p, carry):
        base = base_at(p + 1, layers, core, block_rows)
        write_sums(base, labels_ref, features_ref, block_rows, None, block_of(out_ref, p))
        return carry

    lax.fori_loop(0, layers - 1, one, 0)


def chip_first_kernel(layers, block_rows, labels_ref, features_ref, came_ref, *outs):
    base = base_at(0, layers, lax.axis_index("region") % CORES, block_rows)

    def store(h, first, part):
        outs[h][pl.ds(first, part.shape[0]), :] = part

    write_sums(base, labels_ref, features_ref, block_rows, came_at(came_ref, 0), store)


def chip_rest_kernel(layers, block_rows, labels_ref, features_ref, came_ref, second_ref, out_ref):
    core = lax.axis_index("region") % CORES

    def one(p, carry):
        base = base_at(p + 1, layers, core, block_rows)
        write_sums(
            base, labels_ref, features_ref, block_rows, came_at(came_ref, p), block_of(out_ref, p)
        )
        return carry

    lax.fori_loop(0, layers - 1, one, 0)
    second_ref[0] = out_ref[0]


def has_odd(layers):
    layer = lax.axis_index("region") // CORES
    return (layer > 0) & (layer < layers - 1)


def join_half_kernel(mine_ref, came_ref, out_ref):
    out_ref[...] = (
        mine_ref[...].astype(jnp.float32) + came_ref[...].astype(jnp.float32)
    ).astype(jnp.bfloat16)


def join_kernel(layers, hop, odd, *refs):
    first_refs, rest_ref, came_refs, out_ref = (
        refs[:HALVES],
        refs[HALVES],
        refs[HALVES + 1 : -1],
        refs[-1],
    )
    layer = lax.axis_index("region") // CORES
    up = (layer % 2 == 1) if odd else (layer % 2 == 0)
    target = jnp.where(up, layers - 1 - hop + layer, hop - (layers - 1 - layer))
    target = jnp.clip(target, 0, layers - 1)
    place = jnp.where(layer < layers // 2, layers - 1 - target, target)

    def add(mine):
        for h in range(HALVES):
            came = came_refs[h][...] if len(came_refs) > 1 else came_refs[0][0, h]
            came = came.astype(jnp.float32)
            if not odd:
                came = jnp.where(has_odd(layers), came, 0.0)
            out_ref[0, h] = (mine(h).astype(jnp.float32) + came).astype(jnp.bfloat16)

    @pl.when(place == 0)
    def _():
        add(lambda h: first_refs[h][...])

    @pl.when(place > 0)
    def _():
        add(lambda h: rest_ref[jnp.maximum(place - 1, 0), h])


def update_kernel(layers, memory_ref, rest_ref, *rest):
    layer = lax.axis_index("region") // CORES
    place = jnp.where(layer < layers // 2, layers - 1 - layer, layer) - 1
    came_refs, out_ref, mixed_ref = rest[:-2], rest[-2], rest[-1]
    linked = has_odd(layers)
    block_rows, feat_width = memory_ref.shape
    half_rows = block_rows // HALVES
    slabs = feat_width // LANES
    for h in range(HALVES):

        def total(first, rows):
            t = rest_ref[place, h, pl.ds(first, rows), :].astype(jnp.float32)
            even, odd = (ref[0, h, pl.ds(first, rows), :].astype(jnp.float32) for ref in came_refs)
            t = t + even + jnp.where(linked, odd, 0.0)
            return t

        digits = total(slabs * half_rows, EXTRA)
        counts_row = digits[0:1, :] + BASE * digits[1:2, :]
        row = lax.broadcasted_iota(jnp.int32, (half_rows, LANES), 0) + h * half_rows
        lane = lax.broadcasted_iota(jnp.int32, (half_rows, LANES), 1)
        counts = jnp.sum(jnp.where(row == lane, counts_row, 0.0), axis=1, keepdims=True)
        seen = counts > 0
        divisor = jnp.maximum(counts, 1.0)
        squares = jnp.zeros((half_rows, LANES), jnp.float32)
        for s in range(slabs):
            old = memory_ref[pl.ds(h * half_rows, half_rows), pl.ds(s * LANES, LANES)].astype(
                jnp.float32
            )
            averaged = total(s * half_rows, half_rows) / divisor
            mixed = jnp.where(seen, momentum_keep * old + (1.0 - momentum_keep) * averaged, old)
            mixed_ref[:, pl.ds(s * LANES, LANES)] = mixed
            squares = squares + mixed * mixed
        mean = jnp.sum(squares, axis=1, keepdims=True) * (1.0 / feat_width)
        scale = lax.rsqrt(mean + 1e-06) * D ** (-0.5)
        out_ref[pl.ds(h * half_rows, half_rows), :] = (mixed_ref[...] * scale).astype(jnp.bfloat16)


def grad_kernel(requests_ref, owners_ref, features_ref, *rest):
    group = lax.axis_index("group")
    out_ref, candidates_ref, sems = rest[-3:]
    blocks = rest[:-3]
    block_rows = blocks[0].shape[0]
    cand_count = candidates_ref.shape[0]
    wanted_count = cand_count // block_rows

    def copy(j, k):
        return pltpu.make_async_copy(
            blocks[j], candidates_ref.at[pl.ds(k * block_rows, block_rows), :], sems.at[k]
        )

    for k in range(wanted_count):
        place = owners_ref[0, requests_ref[0, k]] ^ group
        for j in range(len(blocks)):
            @pl.when(place == j)
            def _():
                copy(j, k).start()
    for k in range(wanted_count):
        copy(0, k).wait()
    scores = (
        lax.dot_general(
            features_ref[...],
            candidates_ref[...],
            (((1,), (1,)), ((), ())),
            preferred_element_type=jnp.float32,
        )
        / exponent_sharpness
    )
    expo = jnp.exp(scores - jnp.max(scores, axis=1, keepdims=True))
    likelihoods = expo / jnp.sum(expo, axis=1, keepdims=True)
    column = lax.broadcasted_iota(jnp.int32, (1, cand_count), 1)
    target = jnp.where(column < block_rows, (1.0 - smoothing) / block_rows, 0.0) + (
        smoothing / cand_count
    )
    logit_grad = ((likelihoods - target) / exponent_sharpness).astype(jnp.bfloat16)
    wide = 512
    for n in range(0, out_ref.shape[1], wide):
        out_ref[:, n : n + wide] = jnp.dot(
            logit_grad, candidates_ref[:, n : n + wide], preferred_element_type=jnp.float32
        ).astype(jnp.bfloat16)


def on_device(features, memory, requests, owners, labels):
    group_count = lax.axis_size("group")
    region_count = lax.axis_size("region")
    layers = region_count // CORES
    crop_count, feat_width = features.shape
    block_rows = memory.shape[0]
    half_rows = block_rows // HALVES
    pay_rows = feat_width // LANES * half_rows + EXTRA
    bf16 = jnp.bfloat16
    after = lax.optimization_barrier

    def call(kernel, name, out_shape, operands, flops, scratch=(), smem=0, any_from=None):
        outs = out_shape if isinstance(out_shape, list) else [out_shape]
        flat, tree = jax.tree.flatten(operands)
        specs = [SMEM if i < smem else VMEM for i in range(len(flat))]
        if any_from is not None:
            specs[any_from:] = [pl.BlockSpec(memory_space=pl.ANY)] * (len(flat) - any_from)
        return pl.pallas_call(
            kernel,
            out_shape=out_shape,
            in_specs=specs,
            out_specs=[VMEM] * len(outs) if isinstance(out_shape, list) else VMEM,
            scratch_shapes=list(scratch),
            compiler_params=PARAMS,
            cost_estimate=pl.CostEstimate(
                flops=flops,
                bytes_accessed=sum(2 * x.size for x in [*flat, *outs]),
                transcendentals=0,
            ),
            name=name,
        )(*flat)

    swap = [(r, r ^ 1) for r in range(region_count)]
    block_flops = 2 * block_rows * crop_count * feat_width
    part = functools.partial

    def payloads(count):
        return jax.ShapeDtypeStruct((count, HALVES, pay_rows, LANES), bf16)

    away_first = call(
        part(away_first_kernel, layers, block_rows),
        "away_first",
        payloads(1),
        (labels, features),
        block_flops,
    )
    came_first = lax.ppermute(away_first, "region", swap)
    later_labels, away_first = after((labels, away_first))
    away_rest = call(
        part(away_rest_kernel, layers, block_rows),
        "away_rest",
        payloads(layers - 1),
        (later_labels, features),
        block_flops * (layers - 1),
    )
    first = call(
        part(chip_first_kernel, layers, block_rows),
        "chip_first",
        [jax.ShapeDtypeStruct((pay_rows, LANES), bf16)] * HALVES,
        (labels, features, came_first),
        block_flops,
    )
    first, away_rest, sent_memory = after((first, away_rest, memory))
    second, rest = call(
        part(chip_rest_kernel, layers, block_rows),
        "chip_rest",
        [payloads(1), payloads(layers - 1)],
        (labels, features, lax.ppermute(away_rest, "region", swap)),
        block_flops * (layers - 1),
    )

    blocks = {0: memory}

    def fetch(k, block):
        blocks[k] = lax.ppermute(block, "group", [(g, g ^ k) for g in range(group_count)])

    even = [(r, ((r // CORES) ^ 1) * CORES + r % CORES) for r in range(region_count)]
    odd = []
    for z in range(1, layers - 1):
        other = z + 1 if z % 2 else z - 1
        odd += [(z * CORES + c, other * CORES + c) for c in range(CORES)]
    for z in (0, layers - 1):
        odd += [(z * CORES + c, z * CORES + (c ^ 1)) for c in range(CORES)]

    def joined(hop, is_odd, came):
        return call(
            part(join_kernel, layers, hop, is_odd),
            "join_odd" if is_odd else "join_even",
            payloads(1),
            (*first, rest, *came),
            HALVES * pay_rows * LANES,
        )

    even_came = [lax.ppermute(x, "region", even) for x in first]
    for k in range(1, group_count):
        if k & (k - 1) == 0:
            fetch(k, sent_memory)
    odd_came = []
    for h in range(HALVES):
        leaves = call(
            join_half_kernel,
            "join_half",
            jax.ShapeDtypeStruct((pay_rows, LANES), bf16),
            (first[h], even_came[h]),
            pay_rows * LANES,
        )
        odd_came.append(lax.ppermute(leaves, "region", odd))
    even_came = [lax.ppermute(second, "region", even)]
    for hop in range(2, layers - 1):
        even_next = joined(hop, False, odd_came)
        if hop == 2:
            even_next, sent_memory, near = after((even_next, sent_memory, dict(blocks)))
            blocks.update(near)
            for k in range(1, group_count):
                if k & (k - 1):
                    fetch(k, sent_memory)
        odd_next = joined(hop, True, even_came)
        even_came = [lax.ppermute(even_next, "region", even)]
        odd_came = [lax.ppermute(odd_next, "region", odd)]

    cand_count = requests.shape[1] * block_rows
    feat_grad = call(
        grad_kernel,
        "feat_grad",
        jax.ShapeDtypeStruct(features.shape, bf16),
        (requests, owners, features, *[blocks[k] for k in range(group_count)]),
        4 * crop_count * cand_count * feat_width,
        scratch=(
            pltpu.VMEM((cand_count, feat_width), bf16),
            pltpu.SemaphoreType.DMA((requests.shape[1],)),
        ),
        smem=2,
        any_from=3,
    )

    new_memory = call(
        part(update_kernel, layers),
        "update",
        jax.ShapeDtypeStruct(memory.shape, bf16),
        (memory, rest, *even_came, *odd_came),
        10 * block_rows * feat_width,
        scratch=(pltpu.VMEM((half_rows, feat_width), jnp.float32),),
    )
    return (feat_grad, new_memory)


def solution(mesh):
    placed = (
        P(("region", "group"), None),
        P(("region", "group"), None),
        P(("region", "group"), None),
        P("region", None),
        P(("region", "group"), None),
    )
    return jax.shard_map(
        on_device,
        mesh=mesh,
        in_specs=placed,
        out_specs=(P(("region", "group"), None), P(("region", "group"), None)),
        check_vma=False,
    )
```

```python
import functools

import jax
import jax.numpy as jnp
from jax import lax
from jax.experimental import pallas as pl
from jax.experimental.pallas import tpu as pltpu
from jax.sharding import PartitionSpec as P

D = 2048
CORES = 2
WIDE = 4
LANES = 128
HALVES = 2
EXTRA = 16
BASE = 8

exponent_sharpness = 0.05
smoothing = 0.1
momentum_keep = 0.2

VMEM = pl.BlockSpec(memory_space=pltpu.VMEM)
SMEM = pl.BlockSpec(memory_space=pltpu.SMEM)
PARAMS = pltpu.CompilerParams(vmem_limit_bytes=16 * 2**20)


def write_sums(base, labels_ref, features_ref, block_rows, came, store):
    crop_count, feat_width = features_ref.shape
    half_rows = block_rows // HALVES
    slabs = feat_width // LANES
    value = base + lax.broadcasted_iota(jnp.int32, (block_rows, crop_count), 0)
    match = jnp.where(labels_ref[...] == value, 1.0, 0.0).astype(jnp.bfloat16)

    def put(h, first, part):
        if came is not None:
            part = part + came(h, first, part.shape[0]).astype(jnp.float32)
        store(h, first, part.astype(jnp.bfloat16))

    for s in range(0, slabs, WIDE):
        part = jnp.dot(
            match,
            features_ref[:, s * LANES : (s + WIDE) * LANES],
            preferred_element_type=jnp.float32,
        )
        for h in range(HALVES):
            for i in range(WIDE):
                put(
                    h,
                    (s + i) * half_rows,
                    part[h * half_rows : (h + 1) * half_rows, i * LANES : (i + 1) * LANES],
                )
    counts = lax.dot_general(
        jnp.ones((EXTRA, crop_count), jnp.bfloat16),
        match,
        (((1,), (1,)), ((), ())),
        preferred_element_type=jnp.float32,
    )
    high = jnp.floor(counts * (1.0 / BASE))
    digit = lax.broadcasted_iota(jnp.int32, counts.shape, 0)
    digits = jnp.where(digit == 0, counts - BASE * high, jnp.where(digit == 1, high, 0.0))
    for h in range(HALVES):
        put(h, slabs * half_rows, digits)


def layer_at(place, layers):
    layer = lax.axis_index("region") // CORES
    return jnp.where(layer < layers // 2, layers - 1 - place, place)


def base_at(place, layers, core, block_rows):
    return (layer_at(place, layers) * CORES + core) * block_rows


def block_of(ref, *at):
    def store(h, first, part):
        ref[(*at, h, pl.ds(first, part.shape[0]), slice(None))] = part

    return store


def came_at(ref, *at):
    return lambda h, first, rows: ref[(*at, h, pl.ds(first, rows), slice(None))]


def away_first_kernel(layers, block_rows, labels_ref, features_ref, out_ref):
    core = 1 - lax.axis_index("region") % CORES
    base = base_at(0, layers, core, block_rows)
    write_sums(base, labels_ref, features_ref, block_rows, None, block_of(out_ref, 0))


def away_rest_kernel(layers, block_rows, labels_ref, features_ref, out_ref):
    core = 1 - lax.axis_index("region") % CORES

    def one(p, carry):
        base = base_at(p + 1, layers, core, block_rows)
        write_sums(base, labels_ref, features_ref, block_rows, None, block_of(out_ref, p))
        return carry

    lax.fori_loop(0, layers - 1, one, 0)


def chip_first_kernel(layers, block_rows, labels_ref, features_ref, came_ref, *outs):
    base = base_at(0, layers, lax.axis_index("region") % CORES, block_rows)

    def store(h, first, part):
        outs[h][pl.ds(first, part.shape[0]), :] = part

    write_sums(base, labels_ref, features_ref, block_rows, came_at(came_ref, 0), store)


def chip_rest_kernel(layers, block_rows, labels_ref, features_ref, came_ref, second_ref, out_ref):
    core = lax.axis_index("region") % CORES

    def one(p, carry):
        base = base_at(p + 1, layers, core, block_rows)
        write_sums(
            base, labels_ref, features_ref, block_rows, came_at(came_ref, p), block_of(out_ref, p)
        )
        return carry

    lax.fori_loop(0, layers - 1, one, 0)
    second_ref[0] = out_ref[0]


def has_odd(layers):
    layer = lax.axis_index("region") // CORES
    return (layer > 0) & (layer < layers - 1)


def join_half_kernel(mine_ref, came_ref, out_ref):
    out_ref[...] = (
        mine_ref[...].astype(jnp.float32) + came_ref[...].astype(jnp.float32)
    ).astype(jnp.bfloat16)


def join_kernel(layers, hop, odd, *refs):
    first_refs, rest_ref, came_refs, out_ref = (
        refs[:HALVES],
        refs[HALVES],
        refs[HALVES + 1 : -1],
        refs[-1],
    )
    layer = lax.axis_index("region") // CORES
    up = (layer % 2 == 1) if odd else (layer % 2 == 0)
    target = jnp.where(up, layers - 1 - hop + layer, hop - (layers - 1 - layer))
    target = jnp.clip(target, 0, layers - 1)
    place = jnp.where(layer < layers // 2, layers - 1 - target, target)

    def add(mine):
        for h in range(HALVES):
            came = came_refs[h][...] if len(came_refs) > 1 else came_refs[0][0, h]
            came = came.astype(jnp.float32)
            if not odd:
                came = jnp.where(has_odd(layers), came, 0.0)
            out_ref[0, h] = (mine(h).astype(jnp.float32) + came).astype(jnp.bfloat16)

    @pl.when(place == 0)
    def _():
        add(lambda h: first_refs[h][...])

    @pl.when(place > 0)
    def _():
        add(lambda h: rest_ref[jnp.maximum(place - 1, 0), h])


def update_kernel(layers, memory_ref, rest_ref, *rest):
    layer = lax.axis_index("region") // CORES
    place = jnp.where(layer < layers // 2, layers - 1 - layer, layer) - 1
    came_refs, out_ref, mixed_ref = rest[:-2], rest[-2], rest[-1]
    linked = has_odd(layers)
    block_rows, feat_width = memory_ref.shape
    half_rows = block_rows // HALVES
    slabs = feat_width // LANES
    for h in range(HALVES):

        def total(first, rows):
            t = rest_ref[place, h, pl.ds(first, rows), :].astype(jnp.float32)
            even, odd = (ref[0, h, pl.ds(first, rows), :].astype(jnp.float32) for ref in came_refs)
            t = t + even + jnp.where(linked, odd, 0.0)
            return t

        digits = total(slabs * half_rows, EXTRA)
        counts_row = digits[0:1, :] + BASE * digits[1:2, :]
        row = lax.broadcasted_iota(jnp.int32, (half_rows, LANES), 0) + h * half_rows
        lane = lax.broadcasted_iota(jnp.int32, (half_rows, LANES), 1)
        counts = jnp.sum(jnp.where(row == lane, counts_row, 0.0), axis=1, keepdims=True)
        seen = counts > 0
        share = (1.0 - momentum_keep) / jnp.maximum(counts, 1.0)
        squares = jnp.zeros((half_rows, LANES), jnp.float32)
        for s in range(slabs):
            old = memory_ref[pl.ds(h * half_rows, half_rows), pl.ds(s * LANES, LANES)].astype(
                jnp.float32
            )
            added = total(s * half_rows, half_rows) * share
            mixed = jnp.where(seen, momentum_keep * old + added, old)
            mixed_ref[:, pl.ds(s * LANES, LANES)] = mixed
            squares = squares + mixed * mixed
        mean = jnp.sum(squares, axis=1, keepdims=True) * (1.0 / feat_width)
        scale = lax.rsqrt(mean + 1e-06) * D ** (-0.5)
        out_ref[pl.ds(h * half_rows, half_rows), :] = (mixed_ref[...] * scale).astype(jnp.bfloat16)


def grad_kernel(requests_ref, owners_ref, features_ref, *rest):
    group = lax.axis_index("group")
    out_ref, candidates_ref, sems = rest[-3:]
    blocks = rest[:-3]
    block_rows = blocks[0].shape[0]
    cand_count = candidates_ref.shape[0]
    wanted_count = cand_count // block_rows

    def copy(j, k):
        return pltpu.make_async_copy(
            blocks[j], candidates_ref.at[pl.ds(k * block_rows, block_rows), :], sems.at[k]
        )

    for k in range(wanted_count):
        place = owners_ref[0, requests_ref[0, k]] ^ group
        for j in range(len(blocks)):
            @pl.when(place == j)
            def _():
                copy(j, k).start()
    for k in range(wanted_count):
        copy(0, k).wait()
    scores = (
        lax.dot_general(
            features_ref[...],
            candidates_ref[...],
            (((1,), (1,)), ((), ())),
            preferred_element_type=jnp.float32,
        )
        / exponent_sharpness
    )
    expo = jnp.exp(scores - jnp.max(scores, axis=1, keepdims=True))
    likelihoods = expo / jnp.sum(expo, axis=1, keepdims=True)
    column = lax.broadcasted_iota(jnp.int32, (1, cand_count), 1)
    target = jnp.where(column < block_rows, (1.0 - smoothing) / block_rows, 0.0) + (
        smoothing / cand_count
    )
    logit_grad = ((likelihoods - target) / exponent_sharpness).astype(jnp.bfloat16)
    wide = 512
    for n in range(0, out_ref.shape[1], wide):
        out_ref[:, n : n + wide] = jnp.dot(
            logit_grad, candidates_ref[:, n : n + wide], preferred_element_type=jnp.float32
        ).astype(jnp.bfloat16)


def on_device(features, memory, requests, owners, labels):
    group_count = lax.axis_size("group")
    region_count = lax.axis_size("region")
    layers = region_count // CORES
    crop_count, feat_width = features.shape
    block_rows = memory.shape[0]
    half_rows = block_rows // HALVES
    pay_rows = feat_width // LANES * half_rows + EXTRA
    bf16 = jnp.bfloat16
    after = lax.optimization_barrier

    def call(kernel, name, out_shape, operands, flops, scratch=(), smem=0, any_from=None):
        outs = out_shape if isinstance(out_shape, list) else [out_shape]
        flat, tree = jax.tree.flatten(operands)
        specs = [SMEM if i < smem else VMEM for i in range(len(flat))]
        if any_from is not None:
            specs[any_from:] = [pl.BlockSpec(memory_space=pl.ANY)] * (len(flat) - any_from)
        return pl.pallas_call(
            kernel,
            out_shape=out_shape,
            in_specs=specs,
            out_specs=[VMEM] * len(outs) if isinstance(out_shape, list) else VMEM,
            scratch_shapes=list(scratch),
            compiler_params=PARAMS,
            cost_estimate=pl.CostEstimate(
                flops=flops,
                bytes_accessed=sum(2 * x.size for x in [*flat, *outs]),
                transcendentals=0,
            ),
            name=name,
        )(*flat)

    swap = [(r, r ^ 1) for r in range(region_count)]
    block_flops = 2 * block_rows * crop_count * feat_width
    part = functools.partial

    def payloads(count):
        return jax.ShapeDtypeStruct((count, HALVES, pay_rows, LANES), bf16)

    away_first = call(
        part(away_first_kernel, layers, block_rows),
        "away_first",
        payloads(1),
        (labels, features),
        block_flops,
    )
    came_first = lax.ppermute(away_first, "region", swap)
    later_labels, away_first = after((labels, away_first))
    away_rest = call(
        part(away_rest_kernel, layers, block_rows),
        "away_rest",
        payloads(layers - 1),
        (later_labels, features),
        block_flops * (layers - 1),
    )
    came_first, away_rest = after((came_first, away_rest))
    first = call(
        part(chip_first_kernel, layers, block_rows),
        "chip_first",
        [jax.ShapeDtypeStruct((pay_rows, LANES), bf16)] * HALVES,
        (labels, features, came_first),
        block_flops,
    )
    first, sent_memory = after((first, memory))
    second, rest = call(
        part(chip_rest_kernel, layers, block_rows),
        "chip_rest",
        [payloads(1), payloads(layers - 1)],
        (labels, features, lax.ppermute(away_rest, "region", swap)),
        block_flops * (layers - 1),
    )

    blocks = {0: memory}

    def fetch(k, step, block):
        blocks[k] = lax.ppermute(block, "group", [(g, g ^ step) for g in range(group_count)])

    even = [(r, ((r // CORES) ^ 1) * CORES + r % CORES) for r in range(region_count)]
    odd = []
    for z in range(1, layers - 1):
        other = z + 1 if z % 2 else z - 1
        odd += [(z * CORES + c, other * CORES + c) for c in range(CORES)]
    for z in (0, layers - 1):
        odd += [(z * CORES + c, z * CORES + (c ^ 1)) for c in range(CORES)]

    def joined(hop, is_odd, came):
        return call(
            part(join_kernel, layers, hop, is_odd),
            "join_odd" if is_odd else "join_even",
            payloads(1),
            (*first, rest, *came),
            HALVES * pay_rows * LANES,
        )

    even_came = [lax.ppermute(x, "region", even) for x in first]
    for k in range(1, group_count):
        if k & (k - 1) == 0:
            fetch(k, k, sent_memory)
    odd_came = []
    for h in range(HALVES):
        leaves = call(
            join_half_kernel,
            "join_half",
            jax.ShapeDtypeStruct((pay_rows, LANES), bf16),
            (first[h], even_came[h]),
            pay_rows * LANES,
        )
        odd_came.append(lax.ppermute(leaves, "region", odd))
    near, odd_came[0] = after((dict(blocks), odd_came[0]))
    blocks.update(near)
    for k in range(1, group_count):
        if k & (k - 1):
            bit = 1 << (k.bit_length() - 1)
            fetch(k, bit, blocks[k ^ bit])
    even_came = [lax.ppermute(second, "region", even)]
    for hop in range(2, layers - 1):
        even_next = joined(hop, False, odd_came)
        odd_next = joined(hop, True, even_came)
        even_came = [lax.ppermute(even_next, "region", even)]
        odd_came = [lax.ppermute(odd_next, "region", odd)]

    cand_count = requests.shape[1] * block_rows
    feat_grad = call(
        grad_kernel,
        "feat_grad",
        jax.ShapeDtypeStruct(features.shape, bf16),
        (requests, owners, features, *[blocks[k] for k in range(group_count)]),
        4 * crop_count * cand_count * feat_width,
        scratch=(
            pltpu.VMEM((cand_count, feat_width), bf16),
            pltpu.SemaphoreType.DMA((requests.shape[1],)),
        ),
        smem=2,
        any_from=3,
    )

    new_memory = call(
        part(update_kernel, layers),
        "update",
        jax.ShapeDtypeStruct(memory.shape, bf16),
        (memory, rest, *even_came, *odd_came),
        10 * block_rows * feat_width,
        scratch=(pltpu.VMEM((half_rows, feat_width), jnp.float32),),
    )
    return (feat_grad, new_memory)


def solution(mesh):
    placed = (
        P(("region", "group"), None),
        P(("region", "group"), None),
        P(("region", "group"), None),
        P("region", None),
        P(("region", "group"), None),
    )
    return jax.shard_map(
        on_device,
        mesh=mesh,
        in_specs=placed,
        out_specs=(P(("region", "group"), None), P(("region", "group"), None)),
        check_vma=False,
    )
```

```python
import functools

import jax
import jax.numpy as jnp
from jax import lax
from jax.experimental import pallas as pl
from jax.experimental.pallas import tpu as pltpu
from jax.sharding import PartitionSpec as P

D = 2048
CORES = 2
WIDE = 4
LANES = 128
HALVES = 2
EXTRA = 16
BASE = 8

exponent_sharpness = 0.05
smoothing = 0.1
momentum_keep = 0.2

VMEM = pl.BlockSpec(memory_space=pltpu.VMEM)
SMEM = pl.BlockSpec(memory_space=pltpu.SMEM)
PARAMS = pltpu.CompilerParams(vmem_limit_bytes=16 * 2**20)


def write_sums(base, labels_ref, features_ref, block_rows, came, store):
    crop_count, feat_width = features_ref.shape
    half_rows = block_rows // HALVES
    slabs = feat_width // LANES
    value = base + lax.broadcasted_iota(jnp.int32, (block_rows, crop_count), 0)
    match = jnp.where(labels_ref[...] == value, 1.0, 0.0).astype(jnp.bfloat16)

    def put(h, first, part):
        if came is not None:
            part = part + came(h, first, part.shape[0]).astype(jnp.float32)
        store(h, first, part.astype(jnp.bfloat16))

    for s in range(0, slabs, WIDE):
        part = jnp.dot(
            match,
            features_ref[:, s * LANES : (s + WIDE) * LANES],
            preferred_element_type=jnp.float32,
        )
        for h in range(HALVES):
            for i in range(WIDE):
                put(
                    h,
                    (s + i) * half_rows,
                    part[h * half_rows : (h + 1) * half_rows, i * LANES : (i + 1) * LANES],
                )
    counts = lax.dot_general(
        jnp.ones((EXTRA, crop_count), jnp.bfloat16),
        match,
        (((1,), (1,)), ((), ())),
        preferred_element_type=jnp.float32,
    )
    high = jnp.floor(counts * (1.0 / BASE))
    digit = lax.broadcasted_iota(jnp.int32, counts.shape, 0)
    digits = jnp.where(digit == 0, counts - BASE * high, jnp.where(digit == 1, high, 0.0))
    for h in range(HALVES):
        put(h, slabs * half_rows, digits)


def layer_at(place, layers):
    layer = lax.axis_index("region") // CORES
    return jnp.where(layer < layers // 2, layers - 1 - place, place)


def base_at(place, layers, core, block_rows):
    return (layer_at(place, layers) * CORES + core) * block_rows


def block_of(ref, *at):
    def store(h, first, part):
        ref[(*at, h, pl.ds(first, part.shape[0]), slice(None))] = part

    return store


def came_at(ref, *at):
    return lambda h, first, rows: ref[(*at, h, pl.ds(first, rows), slice(None))]


def away_first_kernel(layers, block_rows, labels_ref, features_ref, early_ref, out_ref):
    core = 1 - lax.axis_index("region") % CORES
    base = base_at(0, layers, core, block_rows)
    write_sums(base, labels_ref, features_ref, block_rows, None, block_of(out_ref, 0))


def away_rest_kernel(layers, block_rows, labels_ref, features_ref, out_ref):
    core = 1 - lax.axis_index("region") % CORES

    def one(p, carry):
        base = base_at(p + 1, layers, core, block_rows)
        write_sums(base, labels_ref, features_ref, block_rows, None, block_of(out_ref, p))
        return carry

    lax.fori_loop(0, layers - 1, one, 0)


def chip_first_kernel(layers, block_rows, labels_ref, features_ref, came_ref, *outs):
    base = base_at(0, layers, lax.axis_index("region") % CORES, block_rows)

    def store(h, first, part):
        outs[h][pl.ds(first, part.shape[0]), :] = part

    write_sums(base, labels_ref, features_ref, block_rows, came_at(came_ref, 0), store)


def chip_rest_kernel(layers, block_rows, labels_ref, features_ref, came_ref, second_ref, out_ref):
    core = lax.axis_index("region") % CORES

    def one(p, carry):
        base = base_at(p + 1, layers, core, block_rows)
        write_sums(
            base, labels_ref, features_ref, block_rows, came_at(came_ref, p), block_of(out_ref, p)
        )
        return carry

    lax.fori_loop(0, layers - 1, one, 0)
    second_ref[0] = out_ref[0]


def has_odd(layers):
    layer = lax.axis_index("region") // CORES
    return (layer > 0) & (layer < layers - 1)


def join_half_kernel(mine_ref, came_ref, out_ref):
    out_ref[...] = (
        mine_ref[...].astype(jnp.float32) + came_ref[...].astype(jnp.float32)
    ).astype(jnp.bfloat16)


def join_kernel(layers, hop, odd, *refs):
    first_refs, rest_ref, came_refs, out_ref = (
        refs[:HALVES],
        refs[HALVES],
        refs[HALVES + 1 : -1],
        refs[-1],
    )
    layer = lax.axis_index("region") // CORES
    up = (layer % 2 == 1) if odd else (layer % 2 == 0)
    target = jnp.where(up, layers - 1 - hop + layer, hop - (layers - 1 - layer))
    target = jnp.clip(target, 0, layers - 1)
    place = jnp.where(layer < layers // 2, layers - 1 - target, target)

    def add(mine):
        for h in range(HALVES):
            came = came_refs[h][...] if len(came_refs) > 1 else came_refs[0][0, h]
            came = came.astype(jnp.float32)
            if not odd:
                came = jnp.where(has_odd(layers), came, 0.0)
            out_ref[0, h] = (mine(h).astype(jnp.float32) + came).astype(jnp.bfloat16)

    @pl.when(place == 0)
    def _():
        add(lambda h: first_refs[h][...])

    @pl.when(place > 0)
    def _():
        add(lambda h: rest_ref[jnp.maximum(place - 1, 0), h])


def update_kernel(layers, memory_ref, rest_ref, *rest):
    layer = lax.axis_index("region") // CORES
    place = jnp.where(layer < layers // 2, layers - 1 - layer, layer) - 1
    came_refs, out_ref, mixed_ref = rest[:-2], rest[-2], rest[-1]
    linked = has_odd(layers)
    block_rows, feat_width = memory_ref.shape
    half_rows = block_rows // HALVES
    slabs = feat_width // LANES
    for h in range(HALVES):

        def total(first, rows):
            t = rest_ref[place, h, pl.ds(first, rows), :].astype(jnp.float32)
            even, odd = (ref[0, h, pl.ds(first, rows), :].astype(jnp.float32) for ref in came_refs)
            t = t + even + jnp.where(linked, odd, 0.0)
            return t

        digits = total(slabs * half_rows, EXTRA)
        counts_row = digits[0:1, :] + BASE * digits[1:2, :]
        row = lax.broadcasted_iota(jnp.int32, (half_rows, LANES), 0) + h * half_rows
        lane = lax.broadcasted_iota(jnp.int32, (half_rows, LANES), 1)
        counts = jnp.sum(jnp.where(row == lane, counts_row, 0.0), axis=1, keepdims=True)
        seen = counts > 0
        share = (1.0 - momentum_keep) / jnp.maximum(counts, 1.0)
        squares = jnp.zeros((half_rows, LANES), jnp.float32)
        for s in range(slabs):
            old = memory_ref[pl.ds(h * half_rows, half_rows), pl.ds(s * LANES, LANES)].astype(
                jnp.float32
            )
            added = total(s * half_rows, half_rows) * share
            mixed = jnp.where(seen, momentum_keep * old + added, old)
            mixed_ref[:, pl.ds(s * LANES, LANES)] = mixed
            squares = squares + mixed * mixed
        mean = jnp.sum(squares, axis=1, keepdims=True) * (1.0 / feat_width)
        scale = lax.rsqrt(mean + 1e-06) * D ** (-0.5)
        out_ref[pl.ds(h * half_rows, half_rows), :] = (mixed_ref[...] * scale).astype(jnp.bfloat16)


def grad_kernel(requests_ref, owners_ref, features_ref, *rest):
    group = lax.axis_index("group")
    out_ref, candidates_ref, sems = rest[-3:]
    blocks = rest[:-3]
    block_rows = blocks[0].shape[0]
    cand_count = candidates_ref.shape[0]
    wanted_count = cand_count // block_rows

    def copy(j, k):
        return pltpu.make_async_copy(
            blocks[j], candidates_ref.at[pl.ds(k * block_rows, block_rows), :], sems.at[k]
        )

    for k in range(wanted_count):
        place = owners_ref[0, requests_ref[0, k]] ^ group
        for j in range(len(blocks)):
            @pl.when(place == j)
            def _():
                copy(j, k).start()
    for k in range(wanted_count):
        copy(0, k).wait()
    scores = (
        lax.dot_general(
            features_ref[...],
            candidates_ref[...],
            (((1,), (1,)), ((), ())),
            preferred_element_type=jnp.float32,
        )
        / exponent_sharpness
    )
    expo = jnp.exp(scores - jnp.max(scores, axis=1, keepdims=True))
    likelihoods = expo / jnp.sum(expo, axis=1, keepdims=True)
    column = lax.broadcasted_iota(jnp.int32, (1, cand_count), 1)
    target = jnp.where(column < block_rows, (1.0 - smoothing) / block_rows, 0.0) + (
        smoothing / cand_count
    )
    logit_grad = ((likelihoods - target) / exponent_sharpness).astype(jnp.bfloat16)
    wide = 512
    for n in range(0, out_ref.shape[1], wide):
        out_ref[:, n : n + wide] = jnp.dot(
            logit_grad, candidates_ref[:, n : n + wide], preferred_element_type=jnp.float32
        ).astype(jnp.bfloat16)


def on_device(features, memory, requests, owners, labels):
    group_count = lax.axis_size("group")
    region_count = lax.axis_size("region")
    layers = region_count // CORES
    crop_count, feat_width = features.shape
    block_rows = memory.shape[0]
    half_rows = block_rows // HALVES
    pay_rows = feat_width // LANES * half_rows + EXTRA
    bf16 = jnp.bfloat16
    after = lax.optimization_barrier

    def call(kernel, name, out_shape, operands, flops, scratch=(), smem=0, any_from=None):
        outs = out_shape if isinstance(out_shape, list) else [out_shape]
        flat, tree = jax.tree.flatten(operands)
        specs = [SMEM if i < smem else VMEM for i in range(len(flat))]
        if any_from is not None:
            specs[any_from:] = [pl.BlockSpec(memory_space=pl.ANY)] * (len(flat) - any_from)
        return pl.pallas_call(
            kernel,
            out_shape=out_shape,
            in_specs=specs,
            out_specs=[VMEM] * len(outs) if isinstance(out_shape, list) else VMEM,
            scratch_shapes=list(scratch),
            compiler_params=PARAMS,
            cost_estimate=pl.CostEstimate(
                flops=flops,
                bytes_accessed=sum(2 * x.size for x in [*flat, *outs]),
                transcendentals=0,
            ),
            name=name,
        )(*flat)

    even = [(r, ((r // CORES) ^ 1) * CORES + r % CORES) for r in range(region_count)]
    odd = []
    for z in range(1, layers - 1):
        other = z + 1 if z % 2 else z - 1
        odd += [(z * CORES + c, other * CORES + c) for c in range(CORES)]
    for z in (0, layers - 1):
        odd += [(z * CORES + c, z * CORES + (c ^ 1)) for c in range(CORES)]

    early = lax.ppermute(requests, "region", even)

    swap = [(r, r ^ 1) for r in range(region_count)]
    block_flops = 2 * block_rows * crop_count * feat_width
    part = functools.partial

    def payloads(count):
        return jax.ShapeDtypeStruct((count, HALVES, pay_rows, LANES), bf16)

    away_first = call(
        part(away_first_kernel, layers, block_rows),
        "away_first",
        payloads(1),
        (labels, features, early),
        block_flops,
    )
    came_first = lax.ppermute(away_first, "region", swap)
    later_labels, away_first = after((labels, away_first))
    away_rest = call(
        part(away_rest_kernel, layers, block_rows),
        "away_rest",
        payloads(layers - 1),
        (later_labels, features),
        block_flops * (layers - 1),
    )
    came_first, away_rest = after((came_first, away_rest))
    first = call(
        part(chip_first_kernel, layers, block_rows),
        "chip_first",
        [jax.ShapeDtypeStruct((pay_rows, LANES), bf16)] * HALVES,
        (labels, features, came_first),
        block_flops,
    )
    first, sent_memory = after((first, memory))
    second, rest = call(
        part(chip_rest_kernel, layers, block_rows),
        "chip_rest",
        [payloads(1), payloads(layers - 1)],
        (labels, features, lax.ppermute(away_rest, "region", swap)),
        block_flops * (layers - 1),
    )

    blocks = {0: memory}

    def fetch(k, step, block):
        blocks[k] = lax.ppermute(block, "group", [(g, g ^ step) for g in range(group_count)])

    def joined(hop, is_odd, came):
        return call(
            part(join_kernel, layers, hop, is_odd),
            "join_odd" if is_odd else "join_even",
            payloads(1),
            (*first, rest, *came),
            HALVES * pay_rows * LANES,
        )

    even_came = [lax.ppermute(x, "region", even) for x in first]
    for k in range(1, group_count):
        if k & (k - 1) == 0:
            fetch(k, k, sent_memory)
    odd_came = []
    for h in range(HALVES):
        leaves = call(
            join_half_kernel,
            "join_half",
            jax.ShapeDtypeStruct((pay_rows, LANES), bf16),
            (first[h], even_came[h]),
            pay_rows * LANES,
        )
        odd_came.append(lax.ppermute(leaves, "region", odd))
    near, odd_came[0] = after((dict(blocks), odd_came[0]))
    blocks.update(near)
    for k in range(1, group_count):
        if k & (k - 1):
            bit = 1 << (k.bit_length() - 1)
            fetch(k, bit, blocks[k ^ bit])
    even_came = [lax.ppermute(second, "region", even)]
    for hop in range(2, layers - 1):
        even_next = joined(hop, False, odd_came)
        odd_next = joined(hop, True, even_came)
        even_came = [lax.ppermute(even_next, "region", even)]
        odd_came = [lax.ppermute(odd_next, "region", odd)]

    cand_count = requests.shape[1] * block_rows
    feat_grad = call(
        grad_kernel,
        "feat_grad",
        jax.ShapeDtypeStruct(features.shape, bf16),
        (requests, owners, features, *[blocks[k] for k in range(group_count)]),
        4 * crop_count * cand_count * feat_width,
        scratch=(
            pltpu.VMEM((cand_count, feat_width), bf16),
            pltpu.SemaphoreType.DMA((requests.shape[1],)),
        ),
        smem=2,
        any_from=3,
    )

    new_memory = call(
        part(update_kernel, layers),
        "update",
        jax.ShapeDtypeStruct(memory.shape, bf16),
        (memory, rest, *even_came, *odd_came),
        10 * block_rows * feat_width,
        scratch=(pltpu.VMEM((half_rows, feat_width), jnp.float32),),
    )
    return (feat_grad, new_memory)


def solution(mesh):
    placed = (
        P(("region", "group"), None),
        P(("region", "group"), None),
        P(("region", "group"), None),
        P("region", None),
        P(("region", "group"), None),
    )
    return jax.shard_map(
        on_device,
        mesh=mesh,
        in_specs=placed,
        out_specs=(P(("region", "group"), None), P(("region", "group"), None)),
        check_vma=False,
    )
```

```python
import functools

import jax
import jax.numpy as jnp
from jax import lax
from jax.experimental import pallas as pl
from jax.experimental.pallas import tpu as pltpu
from jax.sharding import PartitionSpec as P

D = 2048
CORES = 2
WIDE = 4
LANES = 128
HALVES = 2
EXTRA = 16
BASE = 8

exponent_sharpness = 0.05
smoothing = 0.1
momentum_keep = 0.2

VMEM = pl.BlockSpec(memory_space=pltpu.VMEM)
SMEM = pl.BlockSpec(memory_space=pltpu.SMEM)
PARAMS = pltpu.CompilerParams(vmem_limit_bytes=16 * 2**20)


def match_of(base, labels_ref, block_rows):
    value = base + lax.broadcasted_iota(jnp.int32, (block_rows, labels_ref.shape[1]), 0)
    return jnp.where(labels_ref[...] == value, 1.0, 0.0).astype(jnp.bfloat16)


def write_sums(base, labels_ref, features_ref, block_rows, came, store):
    crop_count, feat_width = features_ref.shape
    half_rows = block_rows // HALVES
    slabs = feat_width // LANES
    match = labels_ref[...] if base is None else match_of(base, labels_ref, block_rows)

    def put(h, first, part):
        if came is not None:
            part = part + came(h, first, part.shape[0]).astype(jnp.float32)
        store(h, first, part.astype(jnp.bfloat16))

    for s in range(0, slabs, WIDE):
        part = jnp.dot(
            match,
            features_ref[:, s * LANES : (s + WIDE) * LANES],
            preferred_element_type=jnp.float32,
        )
        for h in range(HALVES):
            for i in range(WIDE):
                put(
                    h,
                    (s + i) * half_rows,
                    part[h * half_rows : (h + 1) * half_rows, i * LANES : (i + 1) * LANES],
                )
    counts = lax.dot_general(
        jnp.ones((EXTRA, crop_count), jnp.bfloat16),
        match,
        (((1,), (1,)), ((), ())),
        preferred_element_type=jnp.float32,
    )
    high = jnp.floor(counts * (1.0 / BASE))
    digit = lax.broadcasted_iota(jnp.int32, counts.shape, 0)
    digits = jnp.where(digit == 0, counts - BASE * high, jnp.where(digit == 1, high, 0.0))
    for h in range(HALVES):
        put(h, slabs * half_rows, digits)


def layer_at(place, layers):
    layer = lax.axis_index("region") // CORES
    return jnp.where(layer < layers // 2, layers - 1 - place, place)


def base_at(place, layers, core, block_rows):
    return (layer_at(place, layers) * CORES + core) * block_rows


def block_of(ref, *at):
    def store(h, first, part):
        ref[(*at, h, pl.ds(first, part.shape[0]), slice(None))] = part

    return store


def came_at(ref, *at):
    return lambda h, first, rows: ref[(*at, h, pl.ds(first, rows), slice(None))]


def match_kernel(layers, block_rows, labels_ref, out_ref):
    core = 1 - lax.axis_index("region") % CORES
    out_ref[...] = match_of(base_at(0, layers, core, block_rows), labels_ref, block_rows)


def away_first_kernel(block_rows, match_ref, features_ref, out_ref):
    write_sums(None, match_ref, features_ref, block_rows, None, block_of(out_ref, 0))


def away_rest_kernel(layers, block_rows, labels_ref, features_ref, out_ref):
    core = 1 - lax.axis_index("region") % CORES

    def one(p, carry):
        base = base_at(p + 1, layers, core, block_rows)
        write_sums(base, labels_ref, features_ref, block_rows, None, block_of(out_ref, p))
        return carry

    lax.fori_loop(0, layers - 1, one, 0)


def chip_first_kernel(layers, block_rows, labels_ref, features_ref, came_ref, *outs):
    base = base_at(0, layers, lax.axis_index("region") % CORES, block_rows)

    def store(h, first, part):
        outs[h][pl.ds(first, part.shape[0]), :] = part

    write_sums(base, labels_ref, features_ref, block_rows, came_at(came_ref, 0), store)


def chip_rest_kernel(layers, block_rows, labels_ref, features_ref, came_ref, second_ref, out_ref):
    core = lax.axis_index("region") % CORES

    def one(p, carry):
        base = base_at(p + 1, layers, core, block_rows)
        write_sums(
            base, labels_ref, features_ref, block_rows, came_at(came_ref, p), block_of(out_ref, p)
        )
        return carry

    lax.fori_loop(0, layers - 1, one, 0)
    second_ref[0] = out_ref[0]


def has_odd(layers):
    layer = lax.axis_index("region") // CORES
    return (layer > 0) & (layer < layers - 1)


def join_half_kernel(mine_ref, came_ref, out_ref):
    out_ref[...] = (
        mine_ref[...].astype(jnp.float32) + came_ref[...].astype(jnp.float32)
    ).astype(jnp.bfloat16)


def join_kernel(layers, hop, odd, *refs):
    first_refs, rest_ref, came_refs, out_ref = (
        refs[:HALVES],
        refs[HALVES],
        refs[HALVES + 1 : -1],
        refs[-1],
    )
    layer = lax.axis_index("region") // CORES
    up = (layer % 2 == 1) if odd else (layer % 2 == 0)
    target = jnp.where(up, layers - 1 - hop + layer, hop - (layers - 1 - layer))
    target = jnp.clip(target, 0, layers - 1)
    place = jnp.where(layer < layers // 2, layers - 1 - target, target)

    def add(mine):
        for h in range(HALVES):
            came = came_refs[h][...] if len(came_refs) > 1 else came_refs[0][0, h]
            came = came.astype(jnp.float32)
            if not odd:
                came = jnp.where(has_odd(layers), came, 0.0)
            out_ref[0, h] = (mine(h).astype(jnp.float32) + came).astype(jnp.bfloat16)

    @pl.when(place == 0)
    def _():
        add(lambda h: first_refs[h][...])

    @pl.when(place > 0)
    def _():
        add(lambda h: rest_ref[jnp.maximum(place - 1, 0), h])


def update_kernel(layers, memory_ref, rest_ref, *rest):
    layer = lax.axis_index("region") // CORES
    place = jnp.where(layer < layers // 2, layers - 1 - layer, layer) - 1
    came_refs, (out_hbm, mixed_ref, out_ref, sems) = rest[:-4], rest[-4:]
    copies = []
    linked = has_odd(layers)
    block_rows, feat_width = memory_ref.shape
    half_rows = block_rows // HALVES
    slabs = feat_width // LANES
    for h in range(HALVES):

        def total(first, rows):
            t = rest_ref[place, h, pl.ds(first, rows), :].astype(jnp.float32)
            even, odd = (ref[0, h, pl.ds(first, rows), :].astype(jnp.float32) for ref in came_refs)
            t = t + even + jnp.where(linked, odd, 0.0)
            return t

        digits = total(slabs * half_rows, EXTRA)
        counts_row = digits[0:1, :] + BASE * digits[1:2, :]
        row = lax.broadcasted_iota(jnp.int32, (half_rows, LANES), 0) + h * half_rows
        lane = lax.broadcasted_iota(jnp.int32, (half_rows, LANES), 1)
        counts = jnp.sum(jnp.where(row == lane, counts_row, 0.0), axis=1, keepdims=True)
        seen = counts > 0
        share = (1.0 - momentum_keep) / jnp.maximum(counts, 1.0)
        squares = jnp.zeros((half_rows, LANES), jnp.float32)
        for s in range(slabs):
            old = memory_ref[pl.ds(h * half_rows, half_rows), pl.ds(s * LANES, LANES)].astype(
                jnp.float32
            )
            added = total(s * half_rows, half_rows) * share
            mixed = jnp.where(seen, momentum_keep * old + added, old)
            mixed_ref[:, pl.ds(s * LANES, LANES)] = mixed
            squares = squares + mixed * mixed
        mean = jnp.sum(squares, axis=1, keepdims=True) * (1.0 / feat_width)
        scale = lax.rsqrt(mean + 1e-06) * D ** (-0.5)
        rows = pl.ds(h * half_rows, half_rows)
        out_ref[rows, :] = (mixed_ref[...] * scale).astype(jnp.bfloat16)
        copies.append(
            pltpu.make_async_copy(out_ref.at[rows, :], out_hbm.at[rows, :], sems.at[h])
        )
        copies[h].start()
    for copy in copies:
        copy.wait()


def grad_kernel(requests_ref, owners_ref, features_ref, *rest):
    group = lax.axis_index("group")
    out_ref, candidates_ref, sems = rest[-3:]
    blocks = rest[:-3]
    block_rows = blocks[0].shape[0]
    cand_count = candidates_ref.shape[0]
    wanted_count = cand_count // block_rows

    def copy(j, k):
        return pltpu.make_async_copy(
            blocks[j], candidates_ref.at[pl.ds(k * block_rows, block_rows), :], sems.at[k]
        )

    for k in range(wanted_count):
        place = owners_ref[0, requests_ref[0, k]] ^ group
        for j in range(len(blocks)):
            @pl.when(place == j)
            def _():
                copy(j, k).start()
    for k in range(wanted_count):
        copy(0, k).wait()
    scores = (
        lax.dot_general(
            features_ref[...],
            candidates_ref[...],
            (((1,), (1,)), ((), ())),
            preferred_element_type=jnp.float32,
        )
        / exponent_sharpness
    )
    expo = jnp.exp(scores - jnp.max(scores, axis=1, keepdims=True))
    likelihoods = expo / jnp.sum(expo, axis=1, keepdims=True)
    column = lax.broadcasted_iota(jnp.int32, (1, cand_count), 1)
    target = jnp.where(column < block_rows, (1.0 - smoothing) / block_rows, 0.0) + (
        smoothing / cand_count
    )
    logit_grad = ((likelihoods - target) / exponent_sharpness).astype(jnp.bfloat16)
    wide = 512
    for n in range(0, out_ref.shape[1], wide):
        out_ref[:, n : n + wide] = jnp.dot(
            logit_grad, candidates_ref[:, n : n + wide], preferred_element_type=jnp.float32
        ).astype(jnp.bfloat16)


def on_device(features, memory, requests, owners, labels):
    group_count = lax.axis_size("group")
    region_count = lax.axis_size("region")
    layers = region_count // CORES
    crop_count, feat_width = features.shape
    block_rows = memory.shape[0]
    half_rows = block_rows // HALVES
    pay_rows = feat_width // LANES * half_rows + EXTRA
    bf16 = jnp.bfloat16
    after = lax.optimization_barrier

    def call(kernel, name, out_shape, operands, flops, scratch=(), smem=0, any_from=None, out_from_vmem=True):
        outs = out_shape if isinstance(out_shape, list) else [out_shape]
        flat, tree = jax.tree.flatten(operands)
        specs = [SMEM if i < smem else VMEM for i in range(len(flat))]
        if any_from is not None:
            specs[any_from:] = [pl.BlockSpec(memory_space=pl.ANY)] * (len(flat) - any_from)
        out_spec = VMEM if out_from_vmem else pl.BlockSpec(memory_space=pl.ANY)
        return pl.pallas_call(
            kernel,
            out_shape=out_shape,
            in_specs=specs,
            out_specs=[out_spec] * len(outs) if isinstance(out_shape, list) else out_spec,
            scratch_shapes=list(scratch),
            compiler_params=PARAMS,
            cost_estimate=pl.CostEstimate(
                flops=flops,
                bytes_accessed=sum(2 * x.size for x in [*flat, *outs]),
                transcendentals=0,
            ),
            name=name,
        )(*flat)

    swap = [(r, r ^ 1) for r in range(region_count)]
    block_flops = 2 * block_rows * crop_count * feat_width
    part = functools.partial

    def payloads(count):
        return jax.ShapeDtypeStruct((count, HALVES, pay_rows, LANES), bf16)

    match_first = call(
        part(match_kernel, layers, block_rows),
        "match_first",
        jax.ShapeDtypeStruct((block_rows, crop_count), bf16),
        (labels,),
        10**9,
    )
    away_first = call(
        part(away_first_kernel, block_rows),
        "away_first",
        payloads(1),
        (match_first, features),
        block_flops,
    )
    came_first = lax.ppermute(away_first, "region", swap)
    later_labels, away_first = after((labels, away_first))
    away_rest = call(
        part(away_rest_kernel, layers, block_rows),
        "away_rest",
        payloads(layers - 1),
        (later_labels, features),
        block_flops * (layers - 1),
    )
    came_first, away_rest = after((came_first, away_rest))
    first = call(
        part(chip_first_kernel, layers, block_rows),
        "chip_first",
        [jax.ShapeDtypeStruct((pay_rows, LANES), bf16)] * HALVES,
        (labels, features, came_first),
        block_flops,
    )
    first, sent_memory = after((first, memory))
    second, rest = call(
        part(chip_rest_kernel, layers, block_rows),
        "chip_rest",
        [payloads(1), payloads(layers - 1)],
        (labels, features, lax.ppermute(away_rest, "region", swap)),
        block_flops * (layers - 1),
    )

    blocks = {0: memory}

    def fetch(k, step, block):
        blocks[k] = lax.ppermute(block, "group", [(g, g ^ step) for g in range(group_count)])

    even = [(r, ((r // CORES) ^ 1) * CORES + r % CORES) for r in range(region_count)]
    odd = []
    for z in range(1, layers - 1):
        other = z + 1 if z % 2 else z - 1
        odd += [(z * CORES + c, other * CORES + c) for c in range(CORES)]
    for z in (0, layers - 1):
        odd += [(z * CORES + c, z * CORES + (c ^ 1)) for c in range(CORES)]

    def joined(hop, is_odd, came):
        return call(
            part(join_kernel, layers, hop, is_odd),
            "join_odd" if is_odd else "join_even",
            payloads(1),
            (*first, rest, *came),
            HALVES * pay_rows * LANES,
        )

    even_came = [lax.ppermute(x, "region", even) for x in first]
    for k in range(1, group_count):
        if k & (k - 1) == 0:
            fetch(k, k, sent_memory)
    odd_came = []
    for h in range(HALVES):
        leaves = call(
            join_half_kernel,
            "join_half",
            jax.ShapeDtypeStruct((pay_rows, LANES), bf16),
            (first[h], even_came[h]),
            pay_rows * LANES,
        )
        odd_came.append(lax.ppermute(leaves, "region", odd))
    near, odd_came[0] = after((dict(blocks), odd_came[0]))
    blocks.update(near)
    for k in range(1, group_count):
        if k & (k - 1):
            bit = 1 << (k.bit_length() - 1)
            fetch(k, bit, blocks[k ^ bit])
    even_came = [lax.ppermute(second, "region", even)]
    for hop in range(2, layers - 1):
        even_next = joined(hop, False, odd_came)
        odd_next = joined(hop, True, even_came)
        even_came = [lax.ppermute(even_next, "region", even)]
        odd_came = [lax.ppermute(odd_next, "region", odd)]

    cand_count = requests.shape[1] * block_rows
    feat_grad = call(
        grad_kernel,
        "feat_grad",
        jax.ShapeDtypeStruct(features.shape, bf16),
        (requests, owners, features, *[blocks[k] for k in range(group_count)]),
        4 * crop_count * cand_count * feat_width,
        scratch=(
            pltpu.VMEM((cand_count, feat_width), bf16),
            pltpu.SemaphoreType.DMA((requests.shape[1],)),
        ),
        smem=2,
        any_from=3,
    )

    new_memory = call(
        part(update_kernel, layers),
        "update",
        jax.ShapeDtypeStruct(memory.shape, bf16),
        (memory, rest, *even_came, *odd_came),
        10 * block_rows * feat_width,
        scratch=(
            pltpu.VMEM((half_rows, feat_width), jnp.float32),
            pltpu.VMEM(memory.shape, bf16),
            pltpu.SemaphoreType.DMA((HALVES,)),
        ),
        out_from_vmem=False,
    )
    return (feat_grad, new_memory)


def solution(mesh):
    placed = (
        P(("region", "group"), None),
        P(("region", "group"), None),
        P(("region", "group"), None),
        P("region", None),
        P(("region", "group"), None),
    )
    return jax.shard_map(
        on_device,
        mesh=mesh,
        in_specs=placed,
        out_specs=(P(("region", "group"), None), P(("region", "group"), None)),
        check_vma=False,
    )
```

```python
import functools

import jax
import jax.numpy as jnp
from jax import lax
from jax.experimental import pallas as pl
from jax.experimental.pallas import tpu as pltpu
from jax.sharding import PartitionSpec as P

D = 2048
CORES = 2
WIDE = 4
LANES = 128
HALVES = 2
EXTRA = 16
BASE = 8

exponent_sharpness = 0.05
smoothing = 0.1
momentum_keep = 0.2

VMEM = pl.BlockSpec(memory_space=pltpu.VMEM)
SMEM = pl.BlockSpec(memory_space=pltpu.SMEM)
PARAMS = pltpu.CompilerParams(vmem_limit_bytes=16 * 2**20)


def match_of(base, labels_ref, block_rows):
    value = base + lax.broadcasted_iota(jnp.int32, (block_rows, labels_ref.shape[1]), 0)
    return jnp.where(labels_ref[...] == value, 1.0, 0.0).astype(jnp.bfloat16)


def write_sums(base, labels_ref, features_ref, block_rows, came, store, only=None):
    crop_count, feat_width = features_ref.shape
    half_rows = block_rows // HALVES
    slabs = feat_width // LANES
    halves = range(HALVES) if only is None else (only,)
    match = labels_ref[...] if base is None else match_of(base, labels_ref, block_rows)

    def put(h, first, part):
        if came is not None:
            part = part + came(h, first, part.shape[0]).astype(jnp.float32)
        store(h, first, part.astype(jnp.bfloat16))

    for s in range(0, slabs, WIDE):
        rows = match if only is None else match[only * half_rows : (only + 1) * half_rows]
        part = jnp.dot(
            rows,
            features_ref[:, s * LANES : (s + WIDE) * LANES],
            preferred_element_type=jnp.float32,
        )
        for h in halves:
            at = (h - halves[0]) * half_rows
            for i in range(WIDE):
                put(
                    h,
                    (s + i) * half_rows,
                    part[at : at + half_rows, i * LANES : (i + 1) * LANES],
                )
    counts = lax.dot_general(
        jnp.ones((EXTRA, crop_count), jnp.bfloat16),
        match,
        (((1,), (1,)), ((), ())),
        preferred_element_type=jnp.float32,
    )
    high = jnp.floor(counts * (1.0 / BASE))
    digit = lax.broadcasted_iota(jnp.int32, counts.shape, 0)
    digits = jnp.where(digit == 0, counts - BASE * high, jnp.where(digit == 1, high, 0.0))
    for h in halves:
        put(h, slabs * half_rows, digits)


def layer_at(place, layers):
    layer = lax.axis_index("region") // CORES
    return jnp.where(layer < layers // 2, layers - 1 - place, place)


def base_at(place, layers, core, block_rows):
    return (layer_at(place, layers) * CORES + core) * block_rows


def block_of(ref, *at):
    def store(h, first, part):
        ref[(*at, h, pl.ds(first, part.shape[0]), slice(None))] = part

    return store


def came_at(ref, *at):
    return lambda h, first, rows: ref[(*at, h, pl.ds(first, rows), slice(None))]


def match_kernel(layers, block_rows, labels_ref, out_ref):
    core = 1 - lax.axis_index("region") % CORES
    out_ref[...] = match_of(base_at(0, layers, core, block_rows), labels_ref, block_rows)


def away_first_kernel(block_rows, match_ref, features_ref, out_ref):
    write_sums(None, match_ref, features_ref, block_rows, None, block_of(out_ref, 0))


def away_rest_kernel(layers, block_rows, labels_ref, features_ref, out_ref):
    core = 1 - lax.axis_index("region") % CORES

    def one(p, carry):
        base = base_at(p + 1, layers, core, block_rows)
        write_sums(base, labels_ref, features_ref, block_rows, None, block_of(out_ref, p))
        return carry

    lax.fori_loop(0, layers - 1, one, 0)


def chip_first_kernel(layers, block_rows, labels_ref, features_ref, came_ref, *outs):
    base = base_at(0, layers, lax.axis_index("region") % CORES, block_rows)

    def store(h, first, part):
        outs[h][pl.ds(first, part.shape[0]), :] = part

    def write():
        write_sums(base, labels_ref, features_ref, block_rows, came_at(came_ref, 0), store)

    if layers == 4:
        pl.when(jnp.logical_not(has_odd(layers)))(write)
    else:
        write()


def chip_rest_kernel(layers, block_rows, labels_ref, features_ref, came_ref, second_ref, out_ref):
    core = lax.axis_index("region") % CORES

    def one(p, carry):
        base = base_at(p + 1, layers, core, block_rows)
        write_sums(
            base, labels_ref, features_ref, block_rows, came_at(came_ref, p), block_of(out_ref, p)
        )
        return carry

    lax.fori_loop(0, layers - 1, one, 0)
    second_ref[0] = out_ref[0]


def has_odd(layers):
    layer = lax.axis_index("region") // CORES
    return (layer > 0) & (layer < layers - 1)


def join_half_kernel(mine_ref, came_ref, out_ref):
    out_ref[...] = (
        mine_ref[...].astype(jnp.float32) + came_ref[...].astype(jnp.float32)
    ).astype(jnp.bfloat16)


def join_first_kernel(layers, block_rows, h, labels_ref, features_ref, sibling_ref, came_ref, out_ref):
    base = base_at(0, layers, lax.axis_index("region") % CORES, block_rows)

    def came(_, first, rows):
        part = pl.ds(first, rows)
        return sibling_ref[0, h, part, :].astype(jnp.float32) + came_ref[part, :].astype(jnp.float32)

    def store(_, first, part):
        out_ref[pl.ds(first, part.shape[0]), :] = part

    @pl.when(has_odd(layers))
    def _():
        write_sums(base, labels_ref, features_ref, block_rows, came, store, only=h)


def join_kernel(layers, hop, odd, *refs):
    first_refs, rest_ref, came_refs, out_ref = (
        refs[:HALVES],
        refs[HALVES],
        refs[HALVES + 1 : -1],
        refs[-1],
    )
    layer = lax.axis_index("region") // CORES
    up = (layer % 2 == 1) if odd else (layer % 2 == 0)
    target = jnp.where(up, layers - 1 - hop + layer, hop - (layers - 1 - layer))
    target = jnp.clip(target, 0, layers - 1)
    place = jnp.where(layer < layers // 2, layers - 1 - target, target)

    def add(mine):
        for h in range(HALVES):
            came = came_refs[h][...] if len(came_refs) > 1 else came_refs[0][0, h]
            came = came.astype(jnp.float32)
            if not odd:
                came = jnp.where(has_odd(layers), came, 0.0)
            out_ref[0, h] = (mine(h).astype(jnp.float32) + came).astype(jnp.bfloat16)

    @pl.when(place == 0)
    def _():
        add(lambda h: first_refs[h][...])

    @pl.when(place > 0)
    def _():
        add(lambda h: rest_ref[jnp.maximum(place - 1, 0), h])


def update_kernel(layers, memory_ref, rest_ref, *rest):
    layer = lax.axis_index("region") // CORES
    place = jnp.where(layer < layers // 2, layers - 1 - layer, layer) - 1
    came_refs, (out_hbm, mixed_ref, out_ref, sems) = rest[:-4], rest[-4:]
    copies = []
    linked = has_odd(layers)
    block_rows, feat_width = memory_ref.shape
    half_rows = block_rows // HALVES
    slabs = feat_width // LANES
    for h in range(HALVES):

        def total(first, rows):
            t = rest_ref[place, h, pl.ds(first, rows), :].astype(jnp.float32)
            even, odd = (ref[0, h, pl.ds(first, rows), :].astype(jnp.float32) for ref in came_refs)
            t = t + even + jnp.where(linked, odd, 0.0)
            return t

        digits = total(slabs * half_rows, EXTRA)
        counts_row = digits[0:1, :] + BASE * digits[1:2, :]
        row = lax.broadcasted_iota(jnp.int32, (half_rows, LANES), 0) + h * half_rows
        lane = lax.broadcasted_iota(jnp.int32, (half_rows, LANES), 1)
        counts = jnp.sum(jnp.where(row == lane, counts_row, 0.0), axis=1, keepdims=True)
        seen = counts > 0
        share = (1.0 - momentum_keep) / jnp.maximum(counts, 1.0)
        squares = jnp.zeros((half_rows, LANES), jnp.float32)
        for s in range(slabs):
            old = memory_ref[pl.ds(h * half_rows, half_rows), pl.ds(s * LANES, LANES)].astype(
                jnp.float32
            )
            added = total(s * half_rows, half_rows) * share
            mixed = jnp.where(seen, momentum_keep * old + added, old)
            mixed_ref[:, pl.ds(s * LANES, LANES)] = mixed
            squares = squares + mixed * mixed
        mean = jnp.sum(squares, axis=1, keepdims=True) * (1.0 / feat_width)
        scale = lax.rsqrt(mean + 1e-06) * D ** (-0.5)
        rows = pl.ds(h * half_rows, half_rows)
        out_ref[rows, :] = (mixed_ref[...] * scale).astype(jnp.bfloat16)
        copies.append(
            pltpu.make_async_copy(out_ref.at[rows, :], out_hbm.at[rows, :], sems.at[h])
        )
        copies[h].start()
    for copy in copies:
        copy.wait()


def grad_kernel(requests_ref, owners_ref, features_ref, *rest):
    group = lax.axis_index("group")
    out_ref, candidates_ref, sems = rest[-3:]
    blocks = rest[:-3]
    block_rows = blocks[0].shape[0]
    cand_count = candidates_ref.shape[0]
    wanted_count = cand_count // block_rows

    def copy(j, k):
        return pltpu.make_async_copy(
            blocks[j], candidates_ref.at[pl.ds(k * block_rows, block_rows), :], sems.at[k]
        )

    for k in range(wanted_count):
        place = owners_ref[0, requests_ref[0, k]] ^ group
        for j in range(len(blocks)):
            @pl.when(place == j)
            def _():
                copy(j, k).start()
    for k in range(wanted_count):
        copy(0, k).wait()
    scores = (
        lax.dot_general(
            features_ref[...],
            candidates_ref[...],
            (((1,), (1,)), ((), ())),
            preferred_element_type=jnp.float32,
        )
        / exponent_sharpness
    )
    expo = jnp.exp(scores - jnp.max(scores, axis=1, keepdims=True))
    likelihoods = expo / jnp.sum(expo, axis=1, keepdims=True)
    column = lax.broadcasted_iota(jnp.int32, (1, cand_count), 1)
    target = jnp.where(column < block_rows, (1.0 - smoothing) / block_rows, 0.0) + (
        smoothing / cand_count
    )
    logit_grad = ((likelihoods - target) / exponent_sharpness).astype(jnp.bfloat16)
    wide = 512
    for n in range(0, out_ref.shape[1], wide):
        out_ref[:, n : n + wide] = jnp.dot(
            logit_grad, candidates_ref[:, n : n + wide], preferred_element_type=jnp.float32
        ).astype(jnp.bfloat16)


def on_device(features, memory, requests, owners, labels):
    group_count = lax.axis_size("group")
    region_count = lax.axis_size("region")
    layers = region_count // CORES
    crop_count, feat_width = features.shape
    block_rows = memory.shape[0]
    half_rows = block_rows // HALVES
    pay_rows = feat_width // LANES * half_rows + EXTRA
    bf16 = jnp.bfloat16
    after = lax.optimization_barrier

    def call(kernel, name, out_shape, operands, flops, scratch=(), smem=0, any_from=None, out_from_vmem=True):
        outs = out_shape if isinstance(out_shape, list) else [out_shape]
        flat, tree = jax.tree.flatten(operands)
        specs = [SMEM if i < smem else VMEM for i in range(len(flat))]
        if any_from is not None:
            specs[any_from:] = [pl.BlockSpec(memory_space=pl.ANY)] * (len(flat) - any_from)
        out_spec = VMEM if out_from_vmem else pl.BlockSpec(memory_space=pl.ANY)
        return pl.pallas_call(
            kernel,
            out_shape=out_shape,
            in_specs=specs,
            out_specs=[out_spec] * len(outs) if isinstance(out_shape, list) else out_spec,
            scratch_shapes=list(scratch),
            compiler_params=PARAMS,
            cost_estimate=pl.CostEstimate(
                flops=flops,
                bytes_accessed=sum(2 * x.size for x in [*flat, *outs]),
                transcendentals=0,
            ),
            name=name,
        )(*flat)

    swap = [(r, r ^ 1) for r in range(region_count)]
    block_flops = 2 * block_rows * crop_count * feat_width
    part = functools.partial

    def payloads(count):
        return jax.ShapeDtypeStruct((count, HALVES, pay_rows, LANES), bf16)

    match_first = call(
        part(match_kernel, layers, block_rows),
        "match_first",
        jax.ShapeDtypeStruct((block_rows, crop_count), bf16),
        (labels,),
        10**9,
    )
    away_first = call(
        part(away_first_kernel, block_rows),
        "away_first",
        payloads(1),
        (match_first, features),
        block_flops,
    )
    came_first = lax.ppermute(away_first, "region", swap)
    later_labels, away_first = after((labels, away_first))
    away_rest = call(
        part(away_rest_kernel, layers, block_rows),
        "away_rest",
        payloads(layers - 1),
        (later_labels, features),
        block_flops * (layers - 1),
    )
    came_first, away_rest = after((came_first, away_rest))
    first = call(
        part(chip_first_kernel, layers, block_rows),
        "chip_first",
        [jax.ShapeDtypeStruct((pay_rows, LANES), bf16)] * HALVES,
        (labels, features, came_first),
        block_flops,
    )
    first, sent_memory = after((first, memory))
    second, rest = call(
        part(chip_rest_kernel, layers, block_rows),
        "chip_rest",
        [payloads(1), payloads(layers - 1)],
        (labels, features, lax.ppermute(away_rest, "region", swap)),
        block_flops * (layers - 1),
    )

    blocks = {0: memory}

    def fetch(k, step, block):
        blocks[k] = lax.ppermute(block, "group", [(g, g ^ step) for g in range(group_count)])

    even = [(r, ((r // CORES) ^ 1) * CORES + r % CORES) for r in range(region_count)]
    odd = []
    for z in range(1, layers - 1):
        other = z + 1 if z % 2 else z - 1
        odd += [(z * CORES + c, other * CORES + c) for c in range(CORES)]
    for z in (0, layers - 1):
        odd += [(z * CORES + c, z * CORES + (c ^ 1)) for c in range(CORES)]

    def joined(hop, is_odd, came):
        return call(
            part(join_kernel, layers, hop, is_odd),
            "join_odd" if is_odd else "join_even",
            payloads(1),
            (*first, rest, *came),
            HALVES * pay_rows * LANES,
        )

    even_came = [lax.ppermute(x, "region", even) for x in first]
    for k in range(1, group_count):
        if k & (k - 1) == 0:
            fetch(k, k, sent_memory)
    odd_came = []
    for h in range(HALVES):
        if layers == 4:
            kernel = part(join_first_kernel, layers, block_rows, h)
            operands = (labels, features, came_first, even_came[h])
        else:
            kernel, operands = join_half_kernel, (first[h], even_came[h])
        leaves = call(
            kernel,
            "join_half",
            jax.ShapeDtypeStruct((pay_rows, LANES), bf16),
            operands,
            pay_rows * LANES,
        )
        odd_came.append(lax.ppermute(leaves, "region", odd))
    near, odd_came[0] = after((dict(blocks), odd_came[0]))
    blocks.update(near)
    for k in range(1, group_count):
        if k & (k - 1):
            bit = 1 << (k.bit_length() - 1)
            fetch(k, bit, blocks[k ^ bit])
    even_came = [lax.ppermute(second, "region", even)]
    for hop in range(2, layers - 1):
        even_next = joined(hop, False, odd_came)
        odd_next = joined(hop, True, even_came)
        even_came = [lax.ppermute(even_next, "region", even)]
        odd_came = [lax.ppermute(odd_next, "region", odd)]

    cand_count = requests.shape[1] * block_rows
    feat_grad = call(
        grad_kernel,
        "feat_grad",
        jax.ShapeDtypeStruct(features.shape, bf16),
        (requests, owners, features, *[blocks[k] for k in range(group_count)]),
        4 * crop_count * cand_count * feat_width,
        scratch=(
            pltpu.VMEM((cand_count, feat_width), bf16),
            pltpu.SemaphoreType.DMA((requests.shape[1],)),
        ),
        smem=2,
        any_from=3,
    )

    new_memory = call(
        part(update_kernel, layers),
        "update",
        jax.ShapeDtypeStruct(memory.shape, bf16),
        (memory, rest, *even_came, *odd_came),
        10 * block_rows * feat_width,
        scratch=(
            pltpu.VMEM((half_rows, feat_width), jnp.float32),
            pltpu.VMEM(memory.shape, bf16),
            pltpu.SemaphoreType.DMA((HALVES,)),
        ),
        out_from_vmem=False,
    )
    return (feat_grad, new_memory)


def solution(mesh):
    placed = (
        P(("region", "group"), None),
        P(("region", "group"), None),
        P(("region", "group"), None),
        P("region", None),
        P(("region", "group"), None),
    )
    return jax.shard_map(
        on_device,
        mesh=mesh,
        in_specs=placed,
        out_specs=(P(("region", "group"), None), P(("region", "group"), None)),
        check_vma=False,
    )
```

```python
import functools

import jax
import jax.numpy as jnp
from jax import lax
from jax.experimental import pallas as pl
from jax.experimental.pallas import tpu as pltpu
from jax.sharding import PartitionSpec as P

D = 2048
CORES = 2
WIDE = 4
LANES = 128
HALVES = 2
EXTRA = 16
BASE = 8

exponent_sharpness = 0.05
smoothing = 0.1
momentum_keep = 0.2

VMEM = pl.BlockSpec(memory_space=pltpu.VMEM)
SMEM = pl.BlockSpec(memory_space=pltpu.SMEM)
PARAMS = pltpu.CompilerParams(vmem_limit_bytes=16 * 2**20)


def match_of(base, labels_ref, block_rows):
    value = base + lax.broadcasted_iota(jnp.int32, (block_rows, labels_ref.shape[1]), 0)
    return jnp.where(labels_ref[...] == value, 1.0, 0.0).astype(jnp.bfloat16)


def write_sums(base, labels_ref, features_ref, block_rows, came, store, only=None):
    crop_count, feat_width = features_ref.shape
    half_rows = block_rows // HALVES
    slabs = feat_width // LANES
    halves = range(HALVES) if only is None else (only,)
    match = labels_ref[...] if base is None else match_of(base, labels_ref, block_rows)

    def put(h, first, part):
        if came is not None:
            part = part + came(h, first, part.shape[0]).astype(jnp.float32)
        store(h, first, part.astype(jnp.bfloat16))

    for s in range(0, slabs, WIDE):
        rows = match if only is None else match[only * half_rows : (only + 1) * half_rows]
        part = jnp.dot(
            rows,
            features_ref[:, s * LANES : (s + WIDE) * LANES],
            preferred_element_type=jnp.float32,
        )
        for h in halves:
            at = (h - halves[0]) * half_rows
            for i in range(WIDE):
                put(
                    h,
                    (s + i) * half_rows,
                    part[at : at + half_rows, i * LANES : (i + 1) * LANES],
                )
    counts = lax.dot_general(
        jnp.ones((EXTRA, crop_count), jnp.bfloat16),
        match,
        (((1,), (1,)), ((), ())),
        preferred_element_type=jnp.float32,
    )
    high = jnp.floor(counts * (1.0 / BASE))
    digit = lax.broadcasted_iota(jnp.int32, counts.shape, 0)
    digits = jnp.where(digit == 0, counts - BASE * high, jnp.where(digit == 1, high, 0.0))
    for h in halves:
        put(h, slabs * half_rows, digits)


def layer_at(place, layers):
    layer = lax.axis_index("region") // CORES
    return jnp.where(layer < layers // 2, layers - 1 - place, place)


def base_at(place, layers, core, block_rows):
    return (layer_at(place, layers) * CORES + core) * block_rows


def block_of(ref, *at):
    def store(h, first, part):
        ref[(*at, h, pl.ds(first, part.shape[0]), slice(None))] = part

    return store


def came_at(ref, *at):
    return lambda h, first, rows: ref[(*at, h, pl.ds(first, rows), slice(None))]


def match_kernel(layers, block_rows, labels_ref, out_ref):
    core = 1 - lax.axis_index("region") % CORES
    out_ref[...] = match_of(base_at(0, layers, core, block_rows), labels_ref, block_rows)


def away_first_kernel(block_rows, match_ref, features_ref, out_ref):
    write_sums(None, match_ref, features_ref, block_rows, None, block_of(out_ref, 0))


def away_rest_kernel(layers, block_rows, labels_ref, features_ref, out_ref):
    core = 1 - lax.axis_index("region") % CORES

    def one(p, carry):
        base = base_at(p + 1, layers, core, block_rows)
        write_sums(base, labels_ref, features_ref, block_rows, None, block_of(out_ref, p))
        return carry

    lax.fori_loop(0, layers - 1, one, 0)


def chip_first_kernel(layers, block_rows, labels_ref, features_ref, came_ref, *outs):
    base = base_at(0, layers, lax.axis_index("region") % CORES, block_rows)

    def store(h, first, part):
        outs[h][pl.ds(first, part.shape[0]), :] = part

    def write():
        write_sums(base, labels_ref, features_ref, block_rows, came_at(came_ref, 0), store)

    if layers == 4:
        pl.when(jnp.logical_not(has_odd(layers)))(write)
    else:
        write()


def chip_rest_kernel(layers, block_rows, labels_ref, features_ref, came_ref, second_ref, out_ref):
    core = lax.axis_index("region") % CORES

    def one(p, carry):
        base = base_at(p + 1, layers, core, block_rows)
        write_sums(
            base, labels_ref, features_ref, block_rows, came_at(came_ref, p), block_of(out_ref, p)
        )
        return carry

    lax.fori_loop(0, layers - 1, one, 0)
    second_ref[0] = out_ref[0]


def has_odd(layers):
    layer = lax.axis_index("region") // CORES
    return (layer > 0) & (layer < layers - 1)


def join_half_kernel(mine_ref, came_ref, out_ref):
    out_ref[...] = (
        mine_ref[...].astype(jnp.float32) + came_ref[...].astype(jnp.float32)
    ).astype(jnp.bfloat16)


def join_first_kernel(layers, block_rows, h, labels_ref, features_ref, sibling_ref, came_ref, out_ref):
    base = base_at(0, layers, lax.axis_index("region") % CORES, block_rows)

    def came(_, first, rows):
        part = pl.ds(first, rows)
        return sibling_ref[0, h, part, :].astype(jnp.float32) + came_ref[part, :].astype(jnp.float32)

    def store(_, first, part):
        out_ref[pl.ds(first, part.shape[0]), :] = part

    @pl.when(has_odd(layers))
    def _():
        write_sums(base, labels_ref, features_ref, block_rows, came, store, only=h)


def join_kernel(layers, hop, odd, *refs):
    first_refs, rest_ref, came_refs, out_ref = (
        refs[:HALVES],
        refs[HALVES],
        refs[HALVES + 1 : -1],
        refs[-1],
    )
    layer = lax.axis_index("region") // CORES
    up = (layer % 2 == 1) if odd else (layer % 2 == 0)
    target = jnp.where(up, layers - 1 - hop + layer, hop - (layers - 1 - layer))
    target = jnp.clip(target, 0, layers - 1)
    place = jnp.where(layer < layers // 2, layers - 1 - target, target)

    def add(mine):
        for h in range(HALVES):
            came = came_refs[h][...] if len(came_refs) > 1 else came_refs[0][0, h]
            came = came.astype(jnp.float32)
            if not odd:
                came = jnp.where(has_odd(layers), came, 0.0)
            out_ref[0, h] = (mine(h).astype(jnp.float32) + came).astype(jnp.bfloat16)

    @pl.when(place == 0)
    def _():
        add(lambda h: first_refs[h][...])

    @pl.when(place > 0)
    def _():
        add(lambda h: rest_ref[jnp.maximum(place - 1, 0), h])


def update_kernel(layers, memory_ref, rest_ref, *rest):
    layer = lax.axis_index("region") // CORES
    place = jnp.where(layer < layers // 2, layers - 1 - layer, layer) - 1
    came_refs, (out_hbm, mixed_ref, out_ref, sems) = rest[:-4], rest[-4:]
    copies = []
    linked = has_odd(layers)
    block_rows, feat_width = memory_ref.shape
    half_rows = block_rows // HALVES
    slabs = feat_width // LANES
    for h in range(HALVES):

        def total(first, rows):
            t = rest_ref[place, h, pl.ds(first, rows), :].astype(jnp.float32)
            even, odd = (ref[0, h, pl.ds(first, rows), :].astype(jnp.float32) for ref in came_refs)
            t = t + even + jnp.where(linked, odd, 0.0)
            return t

        digits = total(slabs * half_rows, EXTRA)
        counts_row = digits[0:1, :] + BASE * digits[1:2, :]
        row = lax.broadcasted_iota(jnp.int32, (half_rows, LANES), 0) + h * half_rows
        lane = lax.broadcasted_iota(jnp.int32, (half_rows, LANES), 1)
        counts = jnp.sum(jnp.where(row == lane, counts_row, 0.0), axis=1, keepdims=True)
        seen = counts > 0
        share = jnp.where(seen, (1.0 - momentum_keep) / jnp.maximum(counts, 1.0), 0.0)
        share = jnp.broadcast_to(share, (half_rows, LANES))
        keep = jnp.broadcast_to(jnp.where(seen, momentum_keep, 1.0), (half_rows, LANES))
        squares = jnp.zeros((half_rows, LANES), jnp.float32)
        for s in range(slabs):
            old = memory_ref[pl.ds(h * half_rows, half_rows), pl.ds(s * LANES, LANES)].astype(
                jnp.float32
            )
            mixed = keep * old + share * total(s * half_rows, half_rows)
            mixed_ref[:, pl.ds(s * LANES, LANES)] = mixed
            squares = squares + mixed * mixed
        mean = jnp.sum(squares, axis=1, keepdims=True) * (1.0 / feat_width)
        scale = lax.rsqrt(mean + 1e-06) * D ** (-0.5)
        rows = pl.ds(h * half_rows, half_rows)
        scale = jnp.broadcast_to(scale, (half_rows, LANES))
        for s in range(slabs):
            columns = pl.ds(s * LANES, LANES)
            out_ref[rows, columns] = (mixed_ref[:, columns] * scale).astype(jnp.bfloat16)
        copies.append(
            pltpu.make_async_copy(out_ref.at[rows, :], out_hbm.at[rows, :], sems.at[h])
        )
        copies[h].start()
    for copy in copies:
        copy.wait()


def grad_kernel(requests_ref, owners_ref, features_ref, *rest):
    group = lax.axis_index("group")
    out_ref, candidates_ref, sems = rest[-3:]
    blocks = rest[:-3]
    block_rows = blocks[0].shape[0]
    cand_count = candidates_ref.shape[0]
    wanted_count = cand_count // block_rows

    def copy(j, k):
        return pltpu.make_async_copy(
            blocks[j], candidates_ref.at[pl.ds(k * block_rows, block_rows), :], sems.at[k]
        )

    for k in range(wanted_count):
        place = owners_ref[0, requests_ref[0, k]] ^ group
        for j in range(len(blocks)):
            @pl.when(place == j)
            def _():
                copy(j, k).start()
    for k in range(wanted_count):
        copy(0, k).wait()
    scores = (
        lax.dot_general(
            features_ref[...],
            candidates_ref[...],
            (((1,), (1,)), ((), ())),
            preferred_element_type=jnp.float32,
        )
        / exponent_sharpness
    )
    expo = jnp.exp(scores - jnp.max(scores, axis=1, keepdims=True))
    likelihoods = expo / jnp.sum(expo, axis=1, keepdims=True)
    column = lax.broadcasted_iota(jnp.int32, (1, cand_count), 1)
    target = jnp.where(column < block_rows, (1.0 - smoothing) / block_rows, 0.0) + (
        smoothing / cand_count
    )
    logit_grad = ((likelihoods - target) / exponent_sharpness).astype(jnp.bfloat16)
    wide = 512
    for n in range(0, out_ref.shape[1], wide):
        out_ref[:, n : n + wide] = jnp.dot(
            logit_grad, candidates_ref[:, n : n + wide], preferred_element_type=jnp.float32
        ).astype(jnp.bfloat16)


def on_device(features, memory, requests, owners, labels):
    group_count = lax.axis_size("group")
    region_count = lax.axis_size("region")
    layers = region_count // CORES
    crop_count, feat_width = features.shape
    block_rows = memory.shape[0]
    half_rows = block_rows // HALVES
    pay_rows = feat_width // LANES * half_rows + EXTRA
    bf16 = jnp.bfloat16
    after = lax.optimization_barrier

    def call(kernel, name, out_shape, operands, flops, scratch=(), smem=0, any_from=None, out_from_vmem=True):
        outs = out_shape if isinstance(out_shape, list) else [out_shape]
        flat, tree = jax.tree.flatten(operands)
        specs = [SMEM if i < smem else VMEM for i in range(len(flat))]
        if any_from is not None:
            specs[any_from:] = [pl.BlockSpec(memory_space=pl.ANY)] * (len(flat) - any_from)
        out_spec = VMEM if out_from_vmem else pl.BlockSpec(memory_space=pl.ANY)
        return pl.pallas_call(
            kernel,
            out_shape=out_shape,
            in_specs=specs,
            out_specs=[out_spec] * len(outs) if isinstance(out_shape, list) else out_spec,
            scratch_shapes=list(scratch),
            compiler_params=PARAMS,
            cost_estimate=pl.CostEstimate(
                flops=flops,
                bytes_accessed=sum(2 * x.size for x in [*flat, *outs]),
                transcendentals=0,
            ),
            name=name,
        )(*flat)

    swap = [(r, r ^ 1) for r in range(region_count)]
    block_flops = 2 * block_rows * crop_count * feat_width
    part = functools.partial

    def payloads(count):
        return jax.ShapeDtypeStruct((count, HALVES, pay_rows, LANES), bf16)

    match_first = call(
        part(match_kernel, layers, block_rows),
        "match_first",
        jax.ShapeDtypeStruct((block_rows, crop_count), bf16),
        (labels,),
        10**9,
    )
    away_first = call(
        part(away_first_kernel, block_rows),
        "away_first",
        payloads(1),
        (match_first, features),
        block_flops,
    )
    came_first = lax.ppermute(away_first, "region", swap)
    later_labels, away_first = after((labels, away_first))
    away_rest = call(
        part(away_rest_kernel, layers, block_rows),
        "away_rest",
        payloads(layers - 1),
        (later_labels, features),
        block_flops * (layers - 1),
    )
    came_first, away_rest = after((came_first, away_rest))
    first = call(
        part(chip_first_kernel, layers, block_rows),
        "chip_first",
        [jax.ShapeDtypeStruct((pay_rows, LANES), bf16)] * HALVES,
        (labels, features, came_first),
        block_flops,
    )
    first, sent_memory = after((first, memory))
    second, rest = call(
        part(chip_rest_kernel, layers, block_rows),
        "chip_rest",
        [payloads(1), payloads(layers - 1)],
        (labels, features, lax.ppermute(away_rest, "region", swap)),
        block_flops * (layers - 1),
    )

    blocks = {0: memory}

    def fetch(k, step, block):
        blocks[k] = lax.ppermute(block, "group", [(g, g ^ step) for g in range(group_count)])

    even = [(r, ((r // CORES) ^ 1) * CORES + r % CORES) for r in range(region_count)]
    odd = []
    for z in range(1, layers - 1):
        other = z + 1 if z % 2 else z - 1
        odd += [(z * CORES + c, other * CORES + c) for c in range(CORES)]
    for z in (0, layers - 1):
        odd += [(z * CORES + c, z * CORES + (c ^ 1)) for c in range(CORES)]

    def joined(hop, is_odd, came):
        return call(
            part(join_kernel, layers, hop, is_odd),
            "join_odd" if is_odd else "join_even",
            payloads(1),
            (*first, rest, *came),
            HALVES * pay_rows * LANES,
        )

    even_came = [lax.ppermute(x, "region", even) for x in first]
    for k in range(1, group_count):
        if k & (k - 1) == 0:
            fetch(k, k, sent_memory)
    odd_came = []
    for h in range(HALVES):
        if layers == 4:
            kernel = part(join_first_kernel, layers, block_rows, h)
            operands = (labels, features, came_first, even_came[h])
        else:
            kernel, operands = join_half_kernel, (first[h], even_came[h])
        leaves = call(
            kernel,
            "join_half",
            jax.ShapeDtypeStruct((pay_rows, LANES), bf16),
            operands,
            pay_rows * LANES,
        )
        odd_came.append(lax.ppermute(leaves, "region", odd))
    near, odd_came[0] = after((dict(blocks), odd_came[0]))
    blocks.update(near)
    for k in range(1, group_count):
        if k & (k - 1):
            bit = 1 << (k.bit_length() - 1)
            fetch(k, bit, blocks[k ^ bit])
    even_came = [lax.ppermute(second, "region", even)]
    for hop in range(2, layers - 1):
        even_next = joined(hop, False, odd_came)
        odd_next = joined(hop, True, even_came)
        even_came = [lax.ppermute(even_next, "region", even)]
        odd_came = [lax.ppermute(odd_next, "region", odd)]

    cand_count = requests.shape[1] * block_rows
    feat_grad = call(
        grad_kernel,
        "feat_grad",
        jax.ShapeDtypeStruct(features.shape, bf16),
        (requests, owners, features, *[blocks[k] for k in range(group_count)]),
        4 * crop_count * cand_count * feat_width,
        scratch=(
            pltpu.VMEM((cand_count, feat_width), bf16),
            pltpu.SemaphoreType.DMA((requests.shape[1],)),
        ),
        smem=2,
        any_from=3,
    )

    new_memory = call(
        part(update_kernel, layers),
        "update",
        jax.ShapeDtypeStruct(memory.shape, bf16),
        (memory, rest, *even_came, *odd_came),
        10 * block_rows * feat_width,
        scratch=(
            pltpu.VMEM((half_rows, feat_width), jnp.float32),
            pltpu.VMEM(memory.shape, bf16),
            pltpu.SemaphoreType.DMA((HALVES,)),
        ),
        out_from_vmem=False,
    )
    return (feat_grad, new_memory)


def solution(mesh):
    placed = (
        P(("region", "group"), None),
        P(("region", "group"), None),
        P(("region", "group"), None),
        P("region", None),
        P(("region", "group"), None),
    )
    return jax.shard_map(
        on_device,
        mesh=mesh,
        in_specs=placed,
        out_specs=(P(("region", "group"), None), P(("region", "group"), None)),
        check_vma=False,
    )
```

```python
import functools

import jax
import jax.numpy as jnp
from jax import lax
from jax.experimental import pallas as pl
from jax.experimental.pallas import tpu as pltpu
from jax.sharding import PartitionSpec as P

D = 2048
CORES = 2
WIDE = 4
LANES = 128
HALVES = 2
EXTRA = 16
BASE = 8

exponent_sharpness = 0.05
smoothing = 0.1
momentum_keep = 0.2

VMEM = pl.BlockSpec(memory_space=pltpu.VMEM)
SMEM = pl.BlockSpec(memory_space=pltpu.SMEM)
PARAMS = pltpu.CompilerParams(vmem_limit_bytes=16 * 2**20)


def match_of(base, labels_ref, block_rows):
    value = base + lax.broadcasted_iota(jnp.int32, (block_rows, labels_ref.shape[1]), 0)
    return jnp.where(labels_ref[...] == value, 1.0, 0.0).astype(jnp.bfloat16)


def write_sums(base, labels_ref, features_ref, block_rows, came, store, only=None):
    crop_count, feat_width = features_ref.shape
    half_rows = block_rows // HALVES
    slabs = feat_width // LANES
    halves = range(HALVES) if only is None else (only,)
    match = labels_ref[...] if base is None else match_of(base, labels_ref, block_rows)

    def put(h, first, part):
        if came is not None:
            part = part + came(h, first, part.shape[0]).astype(jnp.float32)
        store(h, first, part.astype(jnp.bfloat16))

    for s in range(0, slabs, WIDE):
        rows = match if only is None else match[only * half_rows : (only + 1) * half_rows]
        part = jnp.dot(
            rows,
            features_ref[:, s * LANES : (s + WIDE) * LANES],
            preferred_element_type=jnp.float32,
        )
        for h in halves:
            at = (h - halves[0]) * half_rows
            for i in range(WIDE):
                put(
                    h,
                    (s + i) * half_rows,
                    part[at : at + half_rows, i * LANES : (i + 1) * LANES],
                )
    counts = lax.dot_general(
        jnp.ones((EXTRA, crop_count), jnp.bfloat16),
        match,
        (((1,), (1,)), ((), ())),
        preferred_element_type=jnp.float32,
    )
    high = jnp.floor(counts * (1.0 / BASE))
    digit = lax.broadcasted_iota(jnp.int32, counts.shape, 0)
    digits = jnp.where(digit == 0, counts - BASE * high, jnp.where(digit == 1, high, 0.0))
    for h in halves:
        put(h, slabs * half_rows, digits)


def layer_at(place, layers):
    layer = lax.axis_index("region") // CORES
    return jnp.where(layer < layers // 2, layers - 1 - place, place)


def base_at(place, layers, core, block_rows):
    return (layer_at(place, layers) * CORES + core) * block_rows


def block_of(ref, *at):
    def store(h, first, part):
        ref[(*at, h, pl.ds(first, part.shape[0]), slice(None))] = part

    return store


def came_at(ref, *at):
    return lambda h, first, rows: ref[(*at, h, pl.ds(first, rows), slice(None))]


def match_kernel(layers, block_rows, labels_ref, out_ref):
    core = 1 - lax.axis_index("region") % CORES
    out_ref[...] = match_of(base_at(0, layers, core, block_rows), labels_ref, block_rows)


def away_first_kernel(block_rows, match_ref, features_ref, out_ref):
    write_sums(None, match_ref, features_ref, block_rows, None, block_of(out_ref, 0))


def away_rest_kernel(layers, block_rows, labels_ref, features_ref, out_ref):
    core = 1 - lax.axis_index("region") % CORES

    def one(p, carry):
        base = base_at(p + 1, layers, core, block_rows)
        write_sums(base, labels_ref, features_ref, block_rows, None, block_of(out_ref, p))
        return carry

    lax.fori_loop(0, layers - 1, one, 0)


def chip_first_kernel(layers, block_rows, labels_ref, features_ref, came_ref, *outs):
    base = base_at(0, layers, lax.axis_index("region") % CORES, block_rows)

    def store(h, first, part):
        outs[h][pl.ds(first, part.shape[0]), :] = part

    def write():
        write_sums(base, labels_ref, features_ref, block_rows, came_at(came_ref, 0), store)

    if layers == 4:
        pl.when(jnp.logical_not(has_odd(layers)))(write)
    else:
        write()


def chip_rest_kernel(layers, block_rows, labels_ref, features_ref, came_ref, second_ref, out_ref):
    core = lax.axis_index("region") % CORES

    def one(p, carry):
        base = base_at(p + 1, layers, core, block_rows)
        write_sums(
            base, labels_ref, features_ref, block_rows, came_at(came_ref, p), block_of(out_ref, p)
        )
        return carry

    lax.fori_loop(0, layers - 1, one, 0)
    second_ref[0] = out_ref[0]


def has_odd(layers):
    layer = lax.axis_index("region") // CORES
    return (layer > 0) & (layer < layers - 1)


def join_half_kernel(mine_ref, came_ref, out_ref):
    out_ref[...] = (
        mine_ref[...].astype(jnp.float32) + came_ref[...].astype(jnp.float32)
    ).astype(jnp.bfloat16)


def join_first_kernel(layers, block_rows, h, labels_ref, features_ref, sibling_ref, came_ref, out_ref):
    base = base_at(0, layers, lax.axis_index("region") % CORES, block_rows)

    def came(_, first, rows):
        part = pl.ds(first, rows)
        return sibling_ref[0, h, part, :].astype(jnp.float32) + came_ref[part, :].astype(jnp.float32)

    def store(_, first, part):
        out_ref[pl.ds(first, part.shape[0]), :] = part

    @pl.when(has_odd(layers))
    def _():
        write_sums(base, labels_ref, features_ref, block_rows, came, store, only=h)


def join_second_kernel(h, mine_ref, came_ref, out_ref):
    out_ref[...] = (
        mine_ref[0, h].astype(jnp.float32) + came_ref[0, h].astype(jnp.float32)
    ).astype(jnp.bfloat16)


def join_kernel(layers, hop, odd, *refs):
    first_refs, rest_ref, came_refs, out_ref = (
        refs[:HALVES],
        refs[HALVES],
        refs[HALVES + 1 : -1],
        refs[-1],
    )
    layer = lax.axis_index("region") // CORES
    up = (layer % 2 == 1) if odd else (layer % 2 == 0)
    target = jnp.where(up, layers - 1 - hop + layer, hop - (layers - 1 - layer))
    target = jnp.clip(target, 0, layers - 1)
    place = jnp.where(layer < layers // 2, layers - 1 - target, target)

    def add(mine):
        for h in range(HALVES):
            came = came_refs[h][...] if len(came_refs) > 1 else came_refs[0][0, h]
            came = came.astype(jnp.float32)
            if not odd:
                came = jnp.where(has_odd(layers), came, 0.0)
            out_ref[0, h] = (mine(h).astype(jnp.float32) + came).astype(jnp.bfloat16)

    @pl.when(place == 0)
    def _():
        add(lambda h: first_refs[h][...])

    @pl.when(place > 0)
    def _():
        add(lambda h: rest_ref[jnp.maximum(place - 1, 0), h])


def update_kernel(layers, h, memory_ref, rest_ref, even_ref, odd_ref, *rest):
    out_hbm, mixed_ref, out_ref, sem = rest[-4:]
    layer = lax.axis_index("region") // CORES
    place = jnp.where(layer < layers // 2, layers - 1 - layer, layer) - 1
    linked = has_odd(layers)
    block_rows, feat_width = memory_ref.shape
    half_rows = block_rows // HALVES
    slabs = feat_width // LANES
    half = pl.ds(h * half_rows, half_rows)

    def total(first, rows):
        part = pl.ds(first, rows)
        mine = rest_ref[place, h, part, :].astype(jnp.float32)
        even = even_ref[0, h, part, :].astype(jnp.float32)
        odd = odd_ref[part, :] if len(odd_ref.shape) == 2 else odd_ref[0, h, part, :]
        return mine + even + jnp.where(linked, odd.astype(jnp.float32), 0.0)

    digits = total(slabs * half_rows, EXTRA)
    counts_row = digits[0:1, :] + BASE * digits[1:2, :]
    row = lax.broadcasted_iota(jnp.int32, (half_rows, LANES), 0) + h * half_rows
    lane = lax.broadcasted_iota(jnp.int32, (half_rows, LANES), 1)
    counts = jnp.sum(jnp.where(row == lane, counts_row, 0.0), axis=1, keepdims=True)
    seen = counts > 0
    share = jnp.where(seen, (1.0 - momentum_keep) / jnp.maximum(counts, 1.0), 0.0)
    share = jnp.broadcast_to(share, (half_rows, LANES))
    keep = jnp.broadcast_to(jnp.where(seen, momentum_keep, 1.0), (half_rows, LANES))
    squares = jnp.zeros((half_rows, LANES), jnp.float32)
    for s in range(slabs):
        old = memory_ref[half, pl.ds(s * LANES, LANES)].astype(jnp.float32)
        mixed = keep * old + share * total(s * half_rows, half_rows)
        mixed_ref[:, pl.ds(s * LANES, LANES)] = mixed
        squares = squares + mixed * mixed
    mean = jnp.sum(squares, axis=1, keepdims=True) * (1.0 / feat_width)
    scale = lax.rsqrt(mean + 1e-06) * D ** (-0.5)
    scale = jnp.broadcast_to(scale, (half_rows, LANES))
    for s in range(slabs):
        columns = pl.ds(s * LANES, LANES)
        out_ref[:, columns] = (mixed_ref[:, columns] * scale).astype(jnp.bfloat16)
    copy = pltpu.make_async_copy(out_ref, out_hbm.at[half, :], sem)
    copy.start()
    copy.wait()


def grad_kernel(requests_ref, owners_ref, features_ref, *rest):
    group = lax.axis_index("group")
    out_ref, candidates_ref, sems = rest[-3:]
    blocks = rest[:-3]
    block_rows = blocks[0].shape[0]
    cand_count = candidates_ref.shape[0]
    wanted_count = cand_count // block_rows

    def copy(j, k):
        return pltpu.make_async_copy(
            blocks[j], candidates_ref.at[pl.ds(k * block_rows, block_rows), :], sems.at[k]
        )

    for k in range(wanted_count):
        place = owners_ref[0, requests_ref[0, k]] ^ group
        for j in range(len(blocks)):
            @pl.when(place == j)
            def _():
                copy(j, k).start()
    for k in range(wanted_count):
        copy(0, k).wait()
    scores = (
        lax.dot_general(
            features_ref[...],
            candidates_ref[...],
            (((1,), (1,)), ((), ())),
            preferred_element_type=jnp.float32,
        )
        / exponent_sharpness
    )
    expo = jnp.exp(scores - jnp.max(scores, axis=1, keepdims=True))
    likelihoods = expo / jnp.sum(expo, axis=1, keepdims=True)
    column = lax.broadcasted_iota(jnp.int32, (1, cand_count), 1)
    target = jnp.where(column < block_rows, (1.0 - smoothing) / block_rows, 0.0) + (
        smoothing / cand_count
    )
    logit_grad = ((likelihoods - target) / exponent_sharpness).astype(jnp.bfloat16)
    wide = 512
    for n in range(0, out_ref.shape[1], wide):
        out_ref[:, n : n + wide] = jnp.dot(
            logit_grad, candidates_ref[:, n : n + wide], preferred_element_type=jnp.float32
        ).astype(jnp.bfloat16)


def on_device(features, memory, requests, owners, labels):
    group_count = lax.axis_size("group")
    region_count = lax.axis_size("region")
    layers = region_count // CORES
    crop_count, feat_width = features.shape
    block_rows = memory.shape[0]
    half_rows = block_rows // HALVES
    pay_rows = feat_width // LANES * half_rows + EXTRA
    bf16 = jnp.bfloat16
    after = lax.optimization_barrier

    def call(kernel, name, out_shape, operands, flops, scratch=(), smem=0, any_from=None, out_from_vmem=True, aliases={}):
        outs = out_shape if isinstance(out_shape, list) else [out_shape]
        flat, tree = jax.tree.flatten(operands)
        specs = [SMEM if i < smem else VMEM for i in range(len(flat))]
        if any_from is not None:
            specs[any_from:] = [pl.BlockSpec(memory_space=pl.ANY)] * (len(flat) - any_from)
        out_spec = VMEM if out_from_vmem else pl.BlockSpec(memory_space=pl.ANY)
        return pl.pallas_call(
            kernel,
            out_shape=out_shape,
            in_specs=specs,
            out_specs=[out_spec] * len(outs) if isinstance(out_shape, list) else out_spec,
            scratch_shapes=list(scratch),
            input_output_aliases=aliases,
            compiler_params=PARAMS,
            cost_estimate=pl.CostEstimate(
                flops=flops,
                bytes_accessed=sum(2 * x.size for x in [*flat, *outs]),
                transcendentals=0,
            ),
            name=name,
        )(*flat)

    swap = [(r, r ^ 1) for r in range(region_count)]
    block_flops = 2 * block_rows * crop_count * feat_width
    part = functools.partial

    def payloads(count):
        return jax.ShapeDtypeStruct((count, HALVES, pay_rows, LANES), bf16)

    match_first = call(
        part(match_kernel, layers, block_rows),
        "match_first",
        jax.ShapeDtypeStruct((block_rows, crop_count), bf16),
        (labels,),
        10**9,
    )
    away_first = call(
        part(away_first_kernel, block_rows),
        "away_first",
        payloads(1),
        (match_first, features),
        block_flops,
    )
    came_first = lax.ppermute(away_first, "region", swap)
    later_labels, away_first = after((labels, away_first))
    away_rest = call(
        part(away_rest_kernel, layers, block_rows),
        "away_rest",
        payloads(layers - 1),
        (later_labels, features),
        block_flops * (layers - 1),
    )
    came_first, away_rest = after((came_first, away_rest))
    first = call(
        part(chip_first_kernel, layers, block_rows),
        "chip_first",
        [jax.ShapeDtypeStruct((pay_rows, LANES), bf16)] * HALVES,
        (labels, features, came_first),
        block_flops,
    )
    first, sent_memory = after((first, memory))
    second, rest = call(
        part(chip_rest_kernel, layers, block_rows),
        "chip_rest",
        [payloads(1), payloads(layers - 1)],
        (labels, features, lax.ppermute(away_rest, "region", swap)),
        block_flops * (layers - 1),
    )

    blocks = {0: memory}

    def fetch(k, step, block):
        blocks[k] = lax.ppermute(block, "group", [(g, g ^ step) for g in range(group_count)])

    even = [(r, ((r // CORES) ^ 1) * CORES + r % CORES) for r in range(region_count)]
    odd = []
    for z in range(1, layers - 1):
        other = z + 1 if z % 2 else z - 1
        odd += [(z * CORES + c, other * CORES + c) for c in range(CORES)]
    for z in (0, layers - 1):
        odd += [(z * CORES + c, z * CORES + (c ^ 1)) for c in range(CORES)]

    def joined(hop, is_odd, came):
        return call(
            part(join_kernel, layers, hop, is_odd),
            "join_odd" if is_odd else "join_even",
            payloads(1),
            (*first, rest, *came),
            HALVES * pay_rows * LANES,
        )

    even_came = [lax.ppermute(x, "region", even) for x in first]
    for k in range(1, group_count):
        if k & (k - 1) == 0:
            fetch(k, k, sent_memory)
    odd_came = []
    for h in range(HALVES):
        if layers == 4:
            kernel = part(join_first_kernel, layers, block_rows, h)
            operands = (labels, features, came_first, even_came[h])
        else:
            kernel, operands = join_half_kernel, (first[h], even_came[h])
        leaves = call(
            kernel,
            "join_half",
            jax.ShapeDtypeStruct((pay_rows, LANES), bf16),
            operands,
            pay_rows * LANES,
        )
        odd_came.append(lax.ppermute(leaves, "region", odd))
    near, odd_came[0] = after((dict(blocks), odd_came[0]))
    blocks.update(near)
    for k in range(1, group_count):
        if k & (k - 1):
            bit = 1 << (k.bit_length() - 1)
            fetch(k, bit, blocks[k ^ bit])
    even_came = [lax.ppermute(second, "region", even)]
    for hop in range(2, layers - 1):
        even_next = joined(hop, False, odd_came)
        if hop == 2:
            odd_came = []
            for h in range(HALVES):
                leaves = call(
                    part(join_second_kernel, h),
                    "join_second",
                    jax.ShapeDtypeStruct((pay_rows, LANES), bf16),
                    (second, *even_came),
                    10**9,
                )
                odd_came.append(lax.ppermute(leaves, "region", odd))
        else:
            odd_came = [lax.ppermute(joined(hop, True, even_came), "region", odd)]
        even_came = [lax.ppermute(even_next, "region", even)]

    cand_count = requests.shape[1] * block_rows
    feat_grad = call(
        grad_kernel,
        "feat_grad",
        jax.ShapeDtypeStruct(features.shape, bf16),
        (requests, owners, features, *[blocks[k] for k in range(group_count)]),
        4 * crop_count * cand_count * feat_width,
        scratch=(
            pltpu.VMEM((cand_count, feat_width), bf16),
            pltpu.SemaphoreType.DMA((requests.shape[1],)),
        ),
        smem=2,
        any_from=3,
    )

    new_memory = None
    for h in range(HALVES):
        before = () if new_memory is None else (new_memory,)
        new_memory = call(
            part(update_kernel, layers, h),
            "update",
            jax.ShapeDtypeStruct(memory.shape, bf16),
            (memory, rest, even_came[0], odd_came[h if len(odd_came) > 1 else 0], *before),
            5 * block_rows * feat_width,
            scratch=(
                pltpu.VMEM((half_rows, feat_width), jnp.float32),
                pltpu.VMEM((half_rows, feat_width), bf16),
                pltpu.SemaphoreType.DMA,
            ),
            any_from=4,
            out_from_vmem=False,
            aliases={4: 0} if before else {},
        )
    return (feat_grad, new_memory)


def solution(mesh):
    placed = (
        P(("region", "group"), None),
        P(("region", "group"), None),
        P(("region", "group"), None),
        P("region", None),
        P(("region", "group"), None),
    )
    return jax.shard_map(
        on_device,
        mesh=mesh,
        in_specs=placed,
        out_specs=(P(("region", "group"), None), P(("region", "group"), None)),
        check_vma=False,
    )
```

```python
import functools

import jax
import jax.numpy as jnp
from jax import lax
from jax.experimental import pallas as pl
from jax.experimental.pallas import tpu as pltpu
from jax.sharding import PartitionSpec as P

D = 2048
CORES = 2
WIDE = 4
LANES = 128
HALVES = 2
EXTRA = 16
BASE = 8

exponent_sharpness = 0.05
smoothing = 0.1
momentum_keep = 0.2

VMEM = pl.BlockSpec(memory_space=pltpu.VMEM)
SMEM = pl.BlockSpec(memory_space=pltpu.SMEM)
PARAMS = pltpu.CompilerParams(vmem_limit_bytes=16 * 2**20)


def match_of(base, labels_ref, block_rows):
    value = base + lax.broadcasted_iota(jnp.int32, (block_rows, labels_ref.shape[1]), 0)
    return jnp.where(labels_ref[...] == value, 1.0, 0.0).astype(jnp.bfloat16)


def write_sums(base, labels_ref, features_ref, block_rows, came, store, only=None):
    crop_count, feat_width = features_ref.shape
    half_rows = block_rows // HALVES
    slabs = feat_width // LANES
    halves = range(HALVES) if only is None else (only,)
    match = labels_ref[...] if base is None else match_of(base, labels_ref, block_rows)

    def put(h, first, part):
        if came is not None:
            part = part + came(h, first, part.shape[0]).astype(jnp.float32)
        store(h, first, part.astype(jnp.bfloat16))

    for s in range(0, slabs, WIDE):
        rows = match if only is None else match[only * half_rows : (only + 1) * half_rows]
        part = jnp.dot(
            rows,
            features_ref[:, s * LANES : (s + WIDE) * LANES],
            preferred_element_type=jnp.float32,
        )
        for h in halves:
            at = (h - halves[0]) * half_rows
            for i in range(WIDE):
                put(
                    h,
                    (s + i) * half_rows,
                    part[at : at + half_rows, i * LANES : (i + 1) * LANES],
                )
    counts = lax.dot_general(
        jnp.ones((EXTRA, crop_count), jnp.bfloat16),
        match,
        (((1,), (1,)), ((), ())),
        preferred_element_type=jnp.float32,
    )
    high = jnp.floor(counts * (1.0 / BASE))
    digit = lax.broadcasted_iota(jnp.int32, counts.shape, 0)
    digits = jnp.where(digit == 0, counts - BASE * high, jnp.where(digit == 1, high, 0.0))
    for h in halves:
        put(h, slabs * half_rows, digits)


def layer_at(place, layers):
    layer = lax.axis_index("region") // CORES
    return jnp.where(layer < layers // 2, layers - 1 - place, place)


def base_at(place, layers, core, block_rows):
    return (layer_at(place, layers) * CORES + core) * block_rows


def block_of(ref, *at):
    def store(h, first, part):
        ref[(*at, h, pl.ds(first, part.shape[0]), slice(None))] = part

    return store


def came_at(ref, *at):
    return lambda h, first, rows: ref[(*at, h, pl.ds(first, rows), slice(None))]


def match_kernel(layers, block_rows, labels_ref, out_ref):
    core = 1 - lax.axis_index("region") % CORES
    out_ref[...] = match_of(base_at(0, layers, core, block_rows), labels_ref, block_rows)


def away_first_kernel(block_rows, match_ref, features_ref, out_ref):
    write_sums(None, match_ref, features_ref, block_rows, None, block_of(out_ref, 0))


def away_rest_kernel(layers, block_rows, labels_ref, features_ref, out_ref):
    core = 1 - lax.axis_index("region") % CORES

    def one(p, carry):
        base = base_at(p + 1, layers, core, block_rows)
        write_sums(base, labels_ref, features_ref, block_rows, None, block_of(out_ref, p))
        return carry

    lax.fori_loop(0, layers - 1, one, 0)


def chip_first_kernel(layers, block_rows, labels_ref, features_ref, came_ref, *outs):
    base = base_at(0, layers, lax.axis_index("region") % CORES, block_rows)

    def store(h, first, part):
        outs[h][pl.ds(first, part.shape[0]), :] = part

    def write():
        write_sums(base, labels_ref, features_ref, block_rows, came_at(came_ref, 0), store)

    if layers == 4:
        pl.when(jnp.logical_not(has_odd(layers)))(write)
    else:
        write()


def chip_rest_kernel(layers, block_rows, labels_ref, features_ref, came_ref, second_ref, out_ref):
    core = lax.axis_index("region") % CORES

    def one(p, carry):
        base = base_at(p + 1, layers, core, block_rows)
        write_sums(
            base, labels_ref, features_ref, block_rows, came_at(came_ref, p), block_of(out_ref, p)
        )
        return carry

    lax.fori_loop(0, layers - 1, one, 0)
    second_ref[0] = out_ref[0]


def has_odd(layers):
    layer = lax.axis_index("region") // CORES
    return (layer > 0) & (layer < layers - 1)


def join_half_kernel(mine_ref, came_ref, out_ref):
    out_ref[...] = (
        mine_ref[...].astype(jnp.float32) + came_ref[...].astype(jnp.float32)
    ).astype(jnp.bfloat16)


def join_first_kernel(layers, block_rows, h, labels_ref, features_ref, sibling_ref, came_ref, out_ref):
    base = base_at(0, layers, lax.axis_index("region") % CORES, block_rows)

    def came(_, first, rows):
        part = pl.ds(first, rows)
        return sibling_ref[0, h, part, :].astype(jnp.float32) + came_ref[part, :].astype(jnp.float32)

    def store(_, first, part):
        out_ref[pl.ds(first, part.shape[0]), :] = part

    @pl.when(has_odd(layers))
    def _():
        write_sums(base, labels_ref, features_ref, block_rows, came, store, only=h)


def join_second_kernel(h, mine_ref, came_ref, out_ref):
    out_ref[...] = (
        mine_ref[0, h].astype(jnp.float32) + came_ref[0, h].astype(jnp.float32)
    ).astype(jnp.bfloat16)


def join_kernel(layers, hop, odd, *refs):
    first_refs, rest_ref, came_refs, out_ref = (
        refs[:HALVES],
        refs[HALVES],
        refs[HALVES + 1 : -1],
        refs[-1],
    )
    layer = lax.axis_index("region") // CORES
    up = (layer % 2 == 1) if odd else (layer % 2 == 0)
    target = jnp.where(up, layers - 1 - hop + layer, hop - (layers - 1 - layer))
    target = jnp.clip(target, 0, layers - 1)
    place = jnp.where(layer < layers // 2, layers - 1 - target, target)

    def add(mine):
        for h in range(HALVES):
            came = came_refs[h][...] if len(came_refs) > 1 else came_refs[0][0, h]
            came = came.astype(jnp.float32)
            if not odd:
                came = jnp.where(has_odd(layers), came, 0.0)
            out_ref[0, h] = (mine(h).astype(jnp.float32) + came).astype(jnp.bfloat16)

    @pl.when(place == 0)
    def _():
        add(lambda h: first_refs[h][...])

    @pl.when(place > 0)
    def _():
        add(lambda h: rest_ref[jnp.maximum(place - 1, 0), h])


def update_kernel(layers, h, memory_ref, rest_ref, even_ref, odd_ref, *rest):
    out_hbm, mixed_ref, out_ref, sem = rest[-4:]
    layer = lax.axis_index("region") // CORES
    place = jnp.where(layer < layers // 2, layers - 1 - layer, layer) - 1
    linked = has_odd(layers)
    block_rows, feat_width = memory_ref.shape
    half_rows = block_rows // HALVES
    slabs = feat_width // LANES
    half = pl.ds(h * half_rows, half_rows)

    def total(first, rows):
        part = pl.ds(first, rows)
        mine = rest_ref[place, h, part, :].astype(jnp.float32)
        even = even_ref[0, h, part, :].astype(jnp.float32)
        odd = odd_ref[part, :] if len(odd_ref.shape) == 2 else odd_ref[0, h, part, :]
        return mine + even + jnp.where(linked, odd.astype(jnp.float32), 0.0)

    digits = total(slabs * half_rows, EXTRA)
    counts_row = digits[0:1, :] + BASE * digits[1:2, :]
    row = lax.broadcasted_iota(jnp.int32, (half_rows, LANES), 0) + h * half_rows
    lane = lax.broadcasted_iota(jnp.int32, (half_rows, LANES), 1)
    counts = jnp.sum(jnp.where(row == lane, counts_row, 0.0), axis=1, keepdims=True)
    seen = counts > 0
    share = jnp.where(seen, (1.0 - momentum_keep) / jnp.maximum(counts, 1.0), 0.0)
    share = jnp.broadcast_to(share, (half_rows, LANES))
    keep = jnp.broadcast_to(jnp.where(seen, momentum_keep, 1.0), (half_rows, LANES))
    squares = jnp.zeros((half_rows, LANES), jnp.float32)
    for s in range(slabs):
        old = memory_ref[half, pl.ds(s * LANES, LANES)].astype(jnp.float32)
        mixed = keep * old + share * total(s * half_rows, half_rows)
        mixed_ref[:, pl.ds(s * LANES, LANES)] = mixed
        squares = squares + mixed * mixed
    mean = jnp.sum(squares, axis=1, keepdims=True) * (1.0 / feat_width)
    scale = lax.rsqrt(mean + 1e-06) * D ** (-0.5)
    copies = []
    for i in range(half_rows // EXTRA):
        rows = pl.ds(i * EXTRA, EXTRA)
        rows_scale = jnp.broadcast_to(scale[i * EXTRA : (i + 1) * EXTRA], (EXTRA, LANES))
        for s in range(slabs):
            columns = pl.ds(s * LANES, LANES)
            out_ref[rows, columns] = (mixed_ref[rows, columns] * rows_scale).astype(jnp.bfloat16)
        copies.append(
            pltpu.make_async_copy(
                out_ref.at[rows, :],
                out_hbm.at[pl.ds(h * half_rows + i * EXTRA, EXTRA), :],
                sem.at[i],
            )
        )
        copies[i].start()
    for copy in copies:
        copy.wait()


def grad_kernel(requests_ref, owners_ref, features_ref, *rest):
    group = lax.axis_index("group")
    out_ref, candidates_ref, sems = rest[-3:]
    blocks = rest[:-3]
    block_rows = blocks[0].shape[0]
    cand_count = candidates_ref.shape[0]
    wanted_count = cand_count // block_rows

    def copy(j, k):
        return pltpu.make_async_copy(
            blocks[j], candidates_ref.at[pl.ds(k * block_rows, block_rows), :], sems.at[k]
        )

    for k in range(wanted_count):
        place = owners_ref[0, requests_ref[0, k]] ^ group
        for j in range(len(blocks)):
            @pl.when(place == j)
            def _():
                copy(j, k).start()
    for k in range(wanted_count):
        copy(0, k).wait()
    scores = (
        lax.dot_general(
            features_ref[...],
            candidates_ref[...],
            (((1,), (1,)), ((), ())),
            preferred_element_type=jnp.float32,
        )
        / exponent_sharpness
    )
    expo = jnp.exp(scores - jnp.max(scores, axis=1, keepdims=True))
    likelihoods = expo / jnp.sum(expo, axis=1, keepdims=True)
    column = lax.broadcasted_iota(jnp.int32, (1, cand_count), 1)
    target = jnp.where(column < block_rows, (1.0 - smoothing) / block_rows, 0.0) + (
        smoothing / cand_count
    )
    logit_grad = ((likelihoods - target) / exponent_sharpness).astype(jnp.bfloat16)
    wide = 512
    for n in range(0, out_ref.shape[1], wide):
        out_ref[:, n : n + wide] = jnp.dot(
            logit_grad, candidates_ref[:, n : n + wide], preferred_element_type=jnp.float32
        ).astype(jnp.bfloat16)


def on_device(features, memory, requests, owners, labels):
    group_count = lax.axis_size("group")
    region_count = lax.axis_size("region")
    layers = region_count // CORES
    crop_count, feat_width = features.shape
    block_rows = memory.shape[0]
    half_rows = block_rows // HALVES
    pay_rows = feat_width // LANES * half_rows + EXTRA
    bf16 = jnp.bfloat16
    after = lax.optimization_barrier

    def call(kernel, name, out_shape, operands, flops, scratch=(), smem=0, any_from=None, out_from_vmem=True, aliases={}):
        outs = out_shape if isinstance(out_shape, list) else [out_shape]
        flat, tree = jax.tree.flatten(operands)
        specs = [SMEM if i < smem else VMEM for i in range(len(flat))]
        if any_from is not None:
            specs[any_from:] = [pl.BlockSpec(memory_space=pl.ANY)] * (len(flat) - any_from)
        out_spec = VMEM if out_from_vmem else pl.BlockSpec(memory_space=pl.ANY)
        return pl.pallas_call(
            kernel,
            out_shape=out_shape,
            in_specs=specs,
            out_specs=[out_spec] * len(outs) if isinstance(out_shape, list) else out_spec,
            scratch_shapes=list(scratch),
            input_output_aliases=aliases,
            compiler_params=PARAMS,
            cost_estimate=pl.CostEstimate(
                flops=flops,
                bytes_accessed=sum(2 * x.size for x in [*flat, *outs]),
                transcendentals=0,
            ),
            name=name,
        )(*flat)

    swap = [(r, r ^ 1) for r in range(region_count)]
    block_flops = 2 * block_rows * crop_count * feat_width
    part = functools.partial

    def payloads(count):
        return jax.ShapeDtypeStruct((count, HALVES, pay_rows, LANES), bf16)

    match_first = call(
        part(match_kernel, layers, block_rows),
        "match_first",
        jax.ShapeDtypeStruct((block_rows, crop_count), bf16),
        (labels,),
        10**9,
    )
    away_first = call(
        part(away_first_kernel, block_rows),
        "away_first",
        payloads(1),
        (match_first, features),
        block_flops,
    )
    came_first = lax.ppermute(away_first, "region", swap)
    later_labels, away_first = after((labels, away_first))
    away_rest = call(
        part(away_rest_kernel, layers, block_rows),
        "away_rest",
        payloads(layers - 1),
        (later_labels, features),
        block_flops * (layers - 1),
    )
    came_first, away_rest = after((came_first, away_rest))
    first = call(
        part(chip_first_kernel, layers, block_rows),
        "chip_first",
        [jax.ShapeDtypeStruct((pay_rows, LANES), bf16)] * HALVES,
        (labels, features, came_first),
        block_flops,
    )
    first, sent_memory = after((first, memory))
    second, rest = call(
        part(chip_rest_kernel, layers, block_rows),
        "chip_rest",
        [payloads(1), payloads(layers - 1)],
        (labels, features, lax.ppermute(away_rest, "region", swap)),
        block_flops * (layers - 1),
    )

    blocks = {0: memory}

    def fetch(k, step, block):
        blocks[k] = lax.ppermute(block, "group", [(g, g ^ step) for g in range(group_count)])

    even = [(r, ((r // CORES) ^ 1) * CORES + r % CORES) for r in range(region_count)]
    odd = []
    for z in range(1, layers - 1):
        other = z + 1 if z % 2 else z - 1
        odd += [(z * CORES + c, other * CORES + c) for c in range(CORES)]
    for z in (0, layers - 1):
        odd += [(z * CORES + c, z * CORES + (c ^ 1)) for c in range(CORES)]

    def joined(hop, is_odd, came):
        return call(
            part(join_kernel, layers, hop, is_odd),
            "join_odd" if is_odd else "join_even",
            payloads(1),
            (*first, rest, *came),
            HALVES * pay_rows * LANES,
        )

    even_came = [lax.ppermute(x, "region", even) for x in first]
    for k in range(1, group_count):
        if k & (k - 1) == 0:
            fetch(k, k, sent_memory)
    odd_came = []
    for h in range(HALVES):
        if layers == 4:
            kernel = part(join_first_kernel, layers, block_rows, h)
            operands = (labels, features, came_first, even_came[h])
        else:
            kernel, operands = join_half_kernel, (first[h], even_came[h])
        leaves = call(
            kernel,
            "join_half",
            jax.ShapeDtypeStruct((pay_rows, LANES), bf16),
            operands,
            pay_rows * LANES,
        )
        odd_came.append(lax.ppermute(leaves, "region", odd))
    near, odd_came[0] = after((dict(blocks), odd_came[0]))
    blocks.update(near)
    for k in range(1, group_count):
        if k & (k - 1):
            bit = 1 << (k.bit_length() - 1)
            fetch(k, bit, blocks[k ^ bit])
    even_came = [lax.ppermute(second, "region", even)]
    for hop in range(2, layers - 1):
        even_next = joined(hop, False, odd_came)
        if hop == 2:
            odd_came = []
            for h in range(HALVES):
                leaves = call(
                    part(join_second_kernel, h),
                    "join_second",
                    jax.ShapeDtypeStruct((pay_rows, LANES), bf16),
                    (second, *even_came),
                    10**9,
                )
                odd_came.append(lax.ppermute(leaves, "region", odd))
        else:
            odd_came = [lax.ppermute(joined(hop, True, even_came), "region", odd)]
        even_came = [lax.ppermute(even_next, "region", even)]

    cand_count = requests.shape[1] * block_rows
    feat_grad = call(
        grad_kernel,
        "feat_grad",
        jax.ShapeDtypeStruct(features.shape, bf16),
        (requests, owners, features, *[blocks[k] for k in range(group_count)]),
        4 * crop_count * cand_count * feat_width,
        scratch=(
            pltpu.VMEM((cand_count, feat_width), bf16),
            pltpu.SemaphoreType.DMA((requests.shape[1],)),
        ),
        smem=2,
        any_from=3,
    )

    new_memory = None
    for h in range(HALVES):
        before = () if new_memory is None else (new_memory,)
        new_memory = call(
            part(update_kernel, layers, h),
            "update",
            jax.ShapeDtypeStruct(memory.shape, bf16),
            (memory, rest, even_came[0], odd_came[h if len(odd_came) > 1 else 0], *before),
            5 * block_rows * feat_width,
            scratch=(
                pltpu.VMEM((half_rows, feat_width), jnp.float32),
                pltpu.VMEM((half_rows, feat_width), bf16),
                pltpu.SemaphoreType.DMA((half_rows // EXTRA,)),
            ),
            any_from=4,
            out_from_vmem=False,
            aliases={4: 0} if before else {},
        )
    return (feat_grad, new_memory)


def solution(mesh):
    placed = (
        P(("region", "group"), None),
        P(("region", "group"), None),
        P(("region", "group"), None),
        P("region", None),
        P(("region", "group"), None),
    )
    return jax.shard_map(
        on_device,
        mesh=mesh,
        in_specs=placed,
        out_specs=(P(("region", "group"), None), P(("region", "group"), None)),
        check_vma=False,
    )
```

```python
import functools

import jax
import jax.numpy as jnp
from jax import lax
from jax.experimental import pallas as pl
from jax.experimental.pallas import tpu as pltpu
from jax.sharding import PartitionSpec as P

D = 2048
CORES = 2
WIDE = 4
LANES = 128
HALVES = 2
EXTRA = 16
BASE = 8

exponent_sharpness = 0.05
smoothing = 0.1
momentum_keep = 0.2

VMEM = pl.BlockSpec(memory_space=pltpu.VMEM)
SMEM = pl.BlockSpec(memory_space=pltpu.SMEM)
PARAMS = pltpu.CompilerParams(vmem_limit_bytes=16 * 2**20)


def match_of(base, labels_ref, block_rows):
    value = base + lax.broadcasted_iota(jnp.int32, (block_rows, labels_ref.shape[1]), 0)
    return jnp.where(labels_ref[...] == value, 1.0, 0.0).astype(jnp.bfloat16)


def write_sums(base, labels_ref, features_ref, block_rows, came, store, only=None):
    crop_count, feat_width = features_ref.shape
    half_rows = block_rows // HALVES
    slabs = feat_width // LANES
    halves = range(HALVES) if only is None else (only,)
    match = labels_ref[...] if base is None else match_of(base, labels_ref, block_rows)

    def put(h, first, part):
        if came is not None:
            part = part + came(h, first, part.shape[0]).astype(jnp.float32)
        store(h, first, part.astype(jnp.bfloat16))

    for s in range(0, slabs, WIDE):
        rows = match if only is None else match[only * half_rows : (only + 1) * half_rows]
        part = jnp.dot(
            rows,
            features_ref[:, s * LANES : (s + WIDE) * LANES],
            preferred_element_type=jnp.float32,
        )
        for h in halves:
            at = (h - halves[0]) * half_rows
            for i in range(WIDE):
                put(
                    h,
                    (s + i) * half_rows,
                    part[at : at + half_rows, i * LANES : (i + 1) * LANES],
                )
    counts = lax.dot_general(
        jnp.ones((EXTRA, crop_count), jnp.bfloat16),
        match,
        (((1,), (1,)), ((), ())),
        preferred_element_type=jnp.float32,
    )
    high = jnp.floor(counts * (1.0 / BASE))
    digit = lax.broadcasted_iota(jnp.int32, counts.shape, 0)
    digits = jnp.where(digit == 0, counts - BASE * high, jnp.where(digit == 1, high, 0.0))
    for h in halves:
        put(h, slabs * half_rows, digits)


def layer_at(place, layers):
    layer = lax.axis_index("region") // CORES
    return jnp.where(layer < layers // 2, layers - 1 - place, place)


def base_at(place, layers, core, block_rows):
    return (layer_at(place, layers) * CORES + core) * block_rows


def block_of(ref, *at):
    def store(h, first, part):
        ref[(*at, h, pl.ds(first, part.shape[0]), slice(None))] = part

    return store


def came_at(ref, *at):
    return lambda h, first, rows: ref[(*at, h, pl.ds(first, rows), slice(None))]


def match_kernel(layers, block_rows, labels_ref, out_ref):
    core = 1 - lax.axis_index("region") % CORES
    out_ref[...] = match_of(base_at(0, layers, core, block_rows), labels_ref, block_rows)


def away_first_kernel(block_rows, match_ref, features_ref, out_ref):
    write_sums(None, match_ref, features_ref, block_rows, None, block_of(out_ref, 0))


def away_rest_kernel(layers, block_rows, labels_ref, features_ref, out_ref):
    core = 1 - lax.axis_index("region") % CORES

    def one(p, carry):
        base = base_at(p + 1, layers, core, block_rows)
        write_sums(base, labels_ref, features_ref, block_rows, None, block_of(out_ref, p))
        return carry

    lax.fori_loop(0, layers - 1, one, 0)


def chip_first_kernel(layers, block_rows, labels_ref, features_ref, came_ref, *outs):
    base = base_at(0, layers, lax.axis_index("region") % CORES, block_rows)

    def store(h, first, part):
        outs[h][pl.ds(first, part.shape[0]), :] = part

    def write():
        write_sums(base, labels_ref, features_ref, block_rows, came_at(came_ref, 0), store)

    if layers == 4:
        pl.when(jnp.logical_not(has_odd(layers)))(write)
    else:
        write()


def chip_rest_kernel(layers, block_rows, labels_ref, features_ref, came_ref, second_ref, out_ref):
    core = lax.axis_index("region") % CORES

    def one(p, carry):
        base = base_at(p + 1, layers, core, block_rows)
        write_sums(
            base, labels_ref, features_ref, block_rows, came_at(came_ref, p), block_of(out_ref, p)
        )
        return carry

    lax.fori_loop(0, layers - 1, one, 0)
    second_ref[0] = out_ref[0]


def has_odd(layers):
    layer = lax.axis_index("region") // CORES
    return (layer > 0) & (layer < layers - 1)


def join_half_kernel(mine_ref, came_ref, out_ref):
    out_ref[...] = (
        mine_ref[...].astype(jnp.float32) + came_ref[...].astype(jnp.float32)
    ).astype(jnp.bfloat16)


def join_first_kernel(layers, block_rows, h, labels_ref, features_ref, sibling_ref, came_ref, out_ref):
    base = base_at(0, layers, lax.axis_index("region") % CORES, block_rows)

    def came(_, first, rows):
        part = pl.ds(first, rows)
        return sibling_ref[0, h, part, :].astype(jnp.float32) + came_ref[part, :].astype(jnp.float32)

    def store(_, first, part):
        out_ref[pl.ds(first, part.shape[0]), :] = part

    @pl.when(has_odd(layers))
    def _():
        write_sums(base, labels_ref, features_ref, block_rows, came, store, only=h)


def join_second_kernel(h, mine_ref, came_ref, out_ref):
    out_ref[...] = (
        mine_ref[0, h].astype(jnp.float32) + came_ref[0, h].astype(jnp.float32)
    ).astype(jnp.bfloat16)


def join_kernel(layers, hop, odd, *refs):
    first_refs, rest_ref, came_refs, out_ref = (
        refs[:HALVES],
        refs[HALVES],
        refs[HALVES + 1 : -1],
        refs[-1],
    )
    layer = lax.axis_index("region") // CORES
    up = (layer % 2 == 1) if odd else (layer % 2 == 0)
    target = jnp.where(up, layers - 1 - hop + layer, hop - (layers - 1 - layer))
    target = jnp.clip(target, 0, layers - 1)
    place = jnp.where(layer < layers // 2, layers - 1 - target, target)

    def add(mine):
        for h in range(HALVES):
            came = came_refs[h][...] if len(came_refs) > 1 else came_refs[0][0, h]
            came = came.astype(jnp.float32)
            if not odd:
                came = jnp.where(has_odd(layers), came, 0.0)
            out_ref[0, h] = (mine(h).astype(jnp.float32) + came).astype(jnp.bfloat16)

    @pl.when(place == 0)
    def _():
        add(lambda h: first_refs[h][...])

    @pl.when(place > 0)
    def _():
        add(lambda h: rest_ref[jnp.maximum(place - 1, 0), h])


def update_kernel(layers, h, memory_ref, rest_ref, even_ref, odd_ref, *rest):
    out_hbm, mixed_ref, out_ref, sem = rest[-4:]
    layer = lax.axis_index("region") // CORES
    place = jnp.where(layer < layers // 2, layers - 1 - layer, layer) - 1
    linked = has_odd(layers)
    block_rows, feat_width = memory_ref.shape
    half_rows = block_rows // HALVES
    slabs = feat_width // LANES
    half = pl.ds(h * half_rows, half_rows)

    def total(first, rows):
        part = pl.ds(first, rows)
        mine = rest_ref[place, h, part, :].astype(jnp.float32)
        even = even_ref[0, h, part, :].astype(jnp.float32)
        odd = odd_ref[part, :] if len(odd_ref.shape) == 2 else odd_ref[0, h, part, :]
        return mine + even + jnp.where(linked, odd.astype(jnp.float32), 0.0)

    digits = total(slabs * half_rows, EXTRA)
    counts_row = digits[0:1, :] + BASE * digits[1:2, :]
    row = lax.broadcasted_iota(jnp.int32, (half_rows, LANES), 0) + h * half_rows
    lane = lax.broadcasted_iota(jnp.int32, (half_rows, LANES), 1)
    counts = jnp.sum(jnp.where(row == lane, counts_row, 0.0), axis=1, keepdims=True)
    seen = counts > 0
    share = jnp.where(seen, (1.0 - momentum_keep) / jnp.maximum(counts, 1.0), 0.0)
    share = jnp.broadcast_to(share, (half_rows, LANES))
    keep = jnp.broadcast_to(jnp.where(seen, momentum_keep, 1.0), (half_rows, LANES))
    squares = jnp.zeros((half_rows, LANES), jnp.float32)
    for s in range(slabs):
        old = memory_ref[half, pl.ds(s * LANES, LANES)].astype(jnp.float32)
        mixed = keep * old + share * total(s * half_rows, half_rows)
        mixed_ref[:, pl.ds(s * LANES, LANES)] = mixed
        squares = squares + mixed * mixed
    mean = jnp.sum(squares, axis=1, keepdims=True) * (1.0 / feat_width)
    scale = lax.rsqrt(mean + 1e-06) * D ** (-0.5)
    copies = []
    for i in range(half_rows // EXTRA):
        rows = pl.ds(i * EXTRA, EXTRA)
        rows_scale = jnp.broadcast_to(scale[i * EXTRA : (i + 1) * EXTRA], (EXTRA, LANES))
        for s in range(slabs):
            columns = pl.ds(s * LANES, LANES)
            out_ref[rows, columns] = (mixed_ref[rows, columns] * rows_scale).astype(jnp.bfloat16)
        copies.append(
            pltpu.make_async_copy(
                out_ref.at[rows, :],
                out_hbm.at[pl.ds(h * half_rows + i * EXTRA, EXTRA), :],
                sem.at[i],
            )
        )
        copies[i].start()
    for copy in copies:
        copy.wait()


def grad_kernel(requests_ref, owners_ref, features_ref, *rest):
    group = lax.axis_index("group")
    out_ref, candidates_ref, sems = rest[-3:]
    blocks = rest[:-3]
    block_rows = blocks[0].shape[0]
    cand_count = candidates_ref.shape[0]
    wanted_count = cand_count // block_rows

    def copy(j, k):
        return pltpu.make_async_copy(
            blocks[j], candidates_ref.at[pl.ds(k * block_rows, block_rows), :], sems.at[k]
        )

    for k in range(wanted_count):
        place = owners_ref[0, requests_ref[0, k]] ^ group
        for j in range(len(blocks)):
            @pl.when(place == j)
            def _():
                copy(j, k).start()
    for k in range(wanted_count):
        copy(0, k).wait()
    scores = (
        lax.dot_general(
            features_ref[...],
            candidates_ref[...],
            (((1,), (1,)), ((), ())),
            preferred_element_type=jnp.float32,
        )
        / exponent_sharpness
    )
    expo = jnp.exp(scores - jnp.max(scores, axis=1, keepdims=True))
    likelihoods = expo / jnp.sum(expo, axis=1, keepdims=True)
    column = lax.broadcasted_iota(jnp.int32, (1, cand_count), 1)
    target = jnp.where(column < block_rows, (1.0 - smoothing) / block_rows, 0.0) + (
        smoothing / cand_count
    )
    logit_grad = ((likelihoods - target) / exponent_sharpness).astype(jnp.bfloat16)
    wide = 512
    for n in range(0, out_ref.shape[1], wide):
        out_ref[:, n : n + wide] = jnp.dot(
            logit_grad, candidates_ref[:, n : n + wide], preferred_element_type=jnp.float32
        ).astype(jnp.bfloat16)


def on_device(features, memory, requests, owners, labels):
    group_count = lax.axis_size("group")
    region_count = lax.axis_size("region")
    layers = region_count // CORES
    crop_count, feat_width = features.shape
    block_rows = memory.shape[0]
    half_rows = block_rows // HALVES
    pay_rows = feat_width // LANES * half_rows + EXTRA
    bf16 = jnp.bfloat16
    after = lax.optimization_barrier

    def call(kernel, name, out_shape, operands, flops, scratch=(), smem=0, any_from=None, out_from_vmem=True, aliases={}):
        outs = out_shape if isinstance(out_shape, list) else [out_shape]
        flat, tree = jax.tree.flatten(operands)
        specs = [SMEM if i < smem else VMEM for i in range(len(flat))]
        if any_from is not None:
            specs[any_from:] = [pl.BlockSpec(memory_space=pl.ANY)] * (len(flat) - any_from)
        out_spec = VMEM if out_from_vmem else pl.BlockSpec(memory_space=pl.ANY)
        return pl.pallas_call(
            kernel,
            out_shape=out_shape,
            in_specs=specs,
            out_specs=[out_spec] * len(outs) if isinstance(out_shape, list) else out_spec,
            scratch_shapes=list(scratch),
            input_output_aliases=aliases,
            compiler_params=PARAMS,
            cost_estimate=pl.CostEstimate(
                flops=flops,
                bytes_accessed=sum(2 * x.size for x in [*flat, *outs]),
                transcendentals=0,
            ),
            name=name,
        )(*flat)

    swap = [(r, r ^ 1) for r in range(region_count)]
    block_flops = 2 * block_rows * crop_count * feat_width
    part = functools.partial

    def payloads(count):
        return jax.ShapeDtypeStruct((count, HALVES, pay_rows, LANES), bf16)

    match_first = call(
        part(match_kernel, layers, block_rows),
        "match_first",
        jax.ShapeDtypeStruct((block_rows, crop_count), bf16),
        (labels,),
        10**9,
    )
    away_first = call(
        part(away_first_kernel, block_rows),
        "away_first",
        payloads(1),
        (match_first, features),
        block_flops,
    )
    came_first = lax.ppermute(away_first, "region", swap)
    later_labels, away_first = after((labels, away_first))
    away_rest = call(
        part(away_rest_kernel, layers, block_rows),
        "away_rest",
        payloads(layers - 1),
        (later_labels, features),
        block_flops * (layers - 1),
    )
    came_first, away_rest = after((came_first, away_rest))
    first = call(
        part(chip_first_kernel, layers, block_rows),
        "chip_first",
        [jax.ShapeDtypeStruct((pay_rows, LANES), bf16)] * HALVES,
        (labels, features, came_first),
        block_flops,
    )
    first, sent_memory = after((first, memory))
    second, rest = call(
        part(chip_rest_kernel, layers, block_rows),
        "chip_rest",
        [payloads(1), payloads(layers - 1)],
        (labels, features, lax.ppermute(away_rest, "region", swap)),
        block_flops * (layers - 1),
    )

    blocks = {0: memory}

    def fetch(k, step, block):
        blocks[k] = lax.ppermute(block, "group", [(g, g ^ step) for g in range(group_count)])

    even = [(r, ((r // CORES) ^ 1) * CORES + r % CORES) for r in range(region_count)]
    odd = []
    for z in range(1, layers - 1):
        other = z + 1 if z % 2 else z - 1
        odd += [(z * CORES + c, other * CORES + c) for c in range(CORES)]
    for z in (0, layers - 1):
        odd += [(z * CORES + c, z * CORES + (c ^ 1)) for c in range(CORES)]

    def joined(hop, is_odd, came):
        return call(
            part(join_kernel, layers, hop, is_odd),
            "join_odd" if is_odd else "join_even",
            payloads(1),
            (*first, rest, *came),
            HALVES * pay_rows * LANES,
        )

    even_came = [lax.ppermute(x, "region", even) for x in first]
    for k in range(1, group_count):
        if k & (k - 1) == 0:
            fetch(k, k, sent_memory)
    odd_came = []
    for h in range(HALVES):
        if layers == 4:
            kernel = part(join_first_kernel, layers, block_rows, h)
            operands = (labels, features, came_first, even_came[h])
        else:
            kernel, operands = join_half_kernel, (first[h], even_came[h])
        leaves = call(
            kernel,
            "join_half",
            jax.ShapeDtypeStruct((pay_rows, LANES), bf16),
            operands,
            pay_rows * LANES,
        )
        odd_came.append(lax.ppermute(leaves, "region", odd))
    near, odd_came[0] = after((dict(blocks), odd_came[0]))
    blocks.update(near)
    for k in range(1, group_count):
        if k & (k - 1):
            bit = 1 << (k.bit_length() - 1)
            fetch(k, bit, blocks[k ^ bit])
    even_came = [lax.ppermute(second, "region", even)]
    for hop in range(2, layers - 1):
        even_next = joined(hop, False, odd_came)
        if hop == 2:
            odd_came = []
            for h in range(HALVES):
                leaves = call(
                    part(join_second_kernel, h),
                    "join_second",
                    jax.ShapeDtypeStruct((pay_rows, LANES), bf16),
                    (second, *even_came),
                    2 * 10**9,
                )
                odd_came.append(lax.ppermute(leaves, "region", odd))
        else:
            odd_came = [lax.ppermute(joined(hop, True, even_came), "region", odd)]
        even_came = [lax.ppermute(even_next, "region", even)]

    cand_count = requests.shape[1] * block_rows
    feat_grad = call(
        grad_kernel,
        "feat_grad",
        jax.ShapeDtypeStruct(features.shape, bf16),
        (requests, owners, features, *[blocks[k] for k in range(group_count)]),
        4 * crop_count * cand_count * feat_width,
        scratch=(
            pltpu.VMEM((cand_count, feat_width), bf16),
            pltpu.SemaphoreType.DMA((requests.shape[1],)),
        ),
        smem=2,
        any_from=3,
    )

    new_memory = None
    for h in range(HALVES):
        before = () if new_memory is None else (new_memory,)
        new_memory = call(
            part(update_kernel, layers, h),
            "update",
            jax.ShapeDtypeStruct(memory.shape, bf16),
            (memory, rest, even_came[0], odd_came[h if len(odd_came) > 1 else 0], *before),
            5 * block_rows * feat_width,
            scratch=(
                pltpu.VMEM((half_rows, feat_width), jnp.float32),
                pltpu.VMEM((half_rows, feat_width), bf16),
                pltpu.SemaphoreType.DMA((half_rows // EXTRA,)),
            ),
            any_from=4,
            out_from_vmem=False,
            aliases={4: 0} if before else {},
        )
    return (feat_grad, new_memory)


def solution(mesh):
    placed = (
        P(("region", "group"), None),
        P(("region", "group"), None),
        P(("region", "group"), None),
        P("region", None),
        P(("region", "group"), None),
    )
    return jax.shard_map(
        on_device,
        mesh=mesh,
        in_specs=placed,
        out_specs=(P(("region", "group"), None), P(("region", "group"), None)),
        check_vma=False,
    )
```
